32 devices in a mesh: groups: 2 (over y), seq: 4 (over z), head: 2 (over x), fsdp: 2 (over core).
Axes of the slice: x: 2, y: 2, z: 4, core: 2. Of those that a mesh axis runs over, the one named last changes fastest.
Arguments:
- residual_in: bfloat16 [16384, 2048], P(('groups', 'seq', 'fsdp'), 'head'), parts along dimension 0, may hold values from -6 to 6
- query_rows: bfloat16 [16384, 2048], P(('groups', 'seq', 'fsdp'), 'head'), parts along dimension 0, may hold values from -7 to 7
- key_rows: bfloat16 [16384, 2048], P(('groups', 'seq', 'fsdp'), 'head'), parts along dimension 0, may hold values from -7 to 7
- value_rows: bfloat16 [16384, 2048], P(('groups', 'seq', 'fsdp'), 'head'), parts along dimension 0, may hold values from -6 to 6
- bc_weight: bfloat16 [2048, 256], P(('head', 'fsdp')), may hold values from -0.125 to 0.125
- decay_rate: float32 [16384, 32], P(('groups', 'seq', 'fsdp'), 'head'), parts along dimension 0, may hold values from 0 to 0.8
- level_codes: int32 [16384, 18], P(('groups', 'seq', 'fsdp')), parts along dimension 0, may hold values from 0 to 255
- level_scale: float32 [18], replicated, may hold values from 0.05 to 1
- positions: int32 [16384], P(('groups', 'seq', 'fsdp')), parts along dimension 0, may hold values from 0 to 2047, as said below
- ssm_gain: float32 [2048], P('head'), may hold values from 0.25 to 1.75
Outputs:
- mixed_out: bfloat16 [16384, 2048], P(('groups', 'seq', 'fsdp'), 'head'), parts along dimension 0
The draws below stay inside these ranges and needn't reach their ends.
There are 2 independent parts, one for each index of `groups`. The reference program is written for one: setup_inputs(seed, part) draws one part's arguments, and reference() takes and returns one part's arrays. A program takes and returns all parts, laid end to end along the dimension named above; an argument that names none is the same for every part. Nothing has to cross between parts.
Inputs may be any that keep to these rules, and one draw needn't show every extreme that they name: positions[t] is 0 where a document begins (always at t = 0) and positions[t - 1] + 1 elsewhere.
All inputs are finite; a program needn't handle non-finite values.
Results may differ from the reference program's by a relative error of at most 0.008.
Values may be sent and summed in bfloat16 or wider, within the bound.
No kernel may reach another device: no remote copies, remote signals or barrier semaphores. Data moves between devices by JAX's collectives and lax.ppermute only.
A program may use at most 64 MiB of HBM per device.

```python
import math
import jax
import jax.numpy as jnp
from jax import lax

D = 2048
ATT_HEADS = 16
SSM_HEADS = 32
HEAD_VALUES = 64
STATES = 128
WINDOW = 128
LEVELS = 18
TOK_DEV = 1024
TOKEN_TOTAL = 8192


def attention_pair(key):
    base_key = jax.random.fold_in(key, 501)
    key_collection = jax.random.split(base_key, 2)
    query_vals = jnp.clip(jax.random.normal(key_collection[0], (TOKEN_TOTAL, D), jnp.float32), -4.0, 4.0)
    key_vals = jnp.clip(jax.random.normal(key_collection[1], (TOKEN_TOTAL, D), jnp.float32), -4.0, 4.0)
    return (query_vals, key_vals)


def draw_query_rows(key, part):
    return attention_pair(key)[0].astype(jnp.bfloat16)


def draw_key_rows(key, part):
    return attention_pair(key)[1].astype(jnp.bfloat16)


def draw_decay_rate(key, part):
    base_key = jax.random.fold_in(key, 733)
    key_collection = jax.random.split(base_key, 9)
    fast_share = 0.5
    fast_heads = jax.random.uniform(key_collection[0], (SSM_HEADS,), jnp.float32) < fast_share
    fast_rate = jnp.exp(jax.random.uniform(key_collection[1], (SSM_HEADS,), jnp.float32, math.log(1.0 / 50.0), math.log(1.0 / 30.0)))
    slow_rate = jnp.exp(jax.random.uniform(key_collection[2], (SSM_HEADS,), jnp.float32, math.log(0.4), math.log(1.2))) / TOKEN_TOTAL
    head_decay_speed = jnp.where(fast_heads, fast_rate, slow_rate)
    block_total = TOKEN_TOTAL // TOK_DEV
    narrow_factor = jnp.exp(jax.random.uniform(key_collection[3], (block_total, SSM_HEADS), jnp.float32, math.log(0.5), math.log(2.0)))
    wide_factor = jnp.exp(jax.random.uniform(key_collection[7], (block_total, SSM_HEADS), jnp.float32, math.log(0.25), math.log(4.0)))
    block_multiplier = jnp.where(fast_heads[None, :], narrow_factor, wide_factor)
    block_multiplier = jnp.repeat(block_multiplier, TOK_DEV, axis=0)
    jaggedness = jax.random.uniform(key_collection[4], (TOKEN_TOTAL, SSM_HEADS), jnp.float32, 0.5, 1.5)
    leading_spike = jax.random.randint(key_collection[5], (1,), 0, TOKEN_TOTAL)
    trailing_spike = (leading_spike + 1 + jax.random.randint(key_collection[8], (1,), 0, TOKEN_TOTAL - 1)) % TOKEN_TOTAL
    spike_position = jnp.concatenate([leading_spike, trailing_spike])
    spike_length = jnp.concatenate([jnp.full((1,), math.log(2.0), jnp.float32), jax.random.uniform(key_collection[6], (1,), jnp.float32, 0.22, 0.69)])
    token_index = jnp.arange(TOKEN_TOTAL, dtype=jnp.int32)
    spike_events = jnp.sum(jnp.where(token_index[:, None] == spike_position[None, :], spike_length[None, :], 0.0), axis=1)
    return head_decay_speed[None, :] * block_multiplier * jaggedness + spike_events[:, None]


def draw_positions(key, part):
    base_key = jax.random.fold_in(key, 919)
    token_index = jnp.arange(TOKEN_TOTAL, dtype=jnp.int32)
    offset = TOK_DEV // 2
    random_marks = (jax.random.randint(base_key, (TOKEN_TOTAL,), 0, 2 * TOK_DEV) == 0) & (token_index >= offset + 2 * TOK_DEV)
    start_marks = random_marks | (token_index % (2 * TOK_DEV) == offset) | (token_index == 0)
    starts = jnp.where(start_marks, token_index, 0)
    return token_index - lax.cummax(starts, axis=0)


def touch_ends(entries, key, smallest, top_value):
    dims = entries.shape
    place = [jax.random.randint(jax.random.fold_in(key, axis), (), 0, dims[axis]) for axis in range(len(dims))]
    entries = entries.at[tuple(place)].set(smallest)
    longest = dims.index(max(dims))
    place[longest] = (place[longest] + 1) % dims[longest]
    return entries.at[tuple(place)].set(top_value)


def shard_levels(stream_key, shape, cuts, least, top_value):
    level = 1.0
    for dim, blocks in cuts:
        draws = jax.random.uniform(jax.random.fold_in(jax.random.fold_in(stream_key, 6), dim), (blocks,), jnp.float32, least / len(cuts), top_value / len(cuts))
        level = level * jnp.repeat(jnp.exp(draws), shape[dim] // blocks).reshape((-1,) + (1,) * (len(shape) - 1 - dim))
    return level


def normal_values(stream_key, dims, scale, most, cuts=(), kind=jnp.bfloat16):
    values = scale * jax.random.normal(stream_key, dims, jnp.float32)
    if cuts:
        values = values * shard_levels(stream_key, dims, cuts, -0.22, 0.18)
    return jnp.clip(values, -most, most).astype(kind)


def setup_inputs(seed: int = 0, part: int = 0) -> dict:
    keys = jax.random.split(jax.random.key(seed), 11)
    part_keys = jax.random.split(jax.random.fold_in(keys[10], part), 11)
    residual_in = normal_values(part_keys[0], (TOKEN_TOTAL, D), 1.0, 6.0, ((0, 8), (1, 2)))
    query_rows = draw_query_rows(jax.random.fold_in(jax.random.fold_in(keys[10], part), 71), part)
    key_rows = draw_key_rows(jax.random.fold_in(jax.random.fold_in(keys[10], part), 71), part)
    value_rows = normal_values(part_keys[3], (TOKEN_TOTAL, D), 1.0, 6.0, ((0, 8), (1, 2)))
    bc_weight = normal_values(keys[4], (D, 2 * STATES), D ** -0.5, 0.125, ((0, 4),))
    decay_rate = draw_decay_rate(jax.random.fold_in(jax.random.fold_in(keys[10], part), 71), part)
    level_codes = touch_ends(jax.random.randint(part_keys[6], (TOKEN_TOTAL, LEVELS), 0, 256), jax.random.fold_in(part_keys[6], 1), 0, 255).astype(jnp.int32)
    level_scale = jnp.clip(jnp.exp(jax.random.uniform(keys[7], (LEVELS,), jnp.float32, math.log(0.05), math.log(1.0))), 0.05, 1.0)
    positions = draw_positions(jax.random.fold_in(jax.random.fold_in(keys[10], part), 71), part)
    ssm_gain = jnp.clip(1.0 + 0.15 * jax.random.normal(keys[9], (D,), jnp.float32), 0.25, 1.75)
    return dict(residual_in=residual_in, query_rows=query_rows, key_rows=key_rows, value_rows=value_rows, bc_weight=bc_weight, decay_rate=decay_rate, level_codes=level_codes, level_scale=level_scale, positions=positions, ssm_gain=ssm_gain)


def attend_block(queries, keys_part, values_part, doc_pos, head_count):
    query_len = queries.shape[0]
    key_len = keys_part.shape[0]
    window_len = key_len - query_len
    shaped_q = queries.reshape(query_len, head_count, -1).astype(jnp.float32)
    shaped_k = keys_part.reshape(key_len, head_count, -1).astype(jnp.float32)
    shaped_v = values_part.reshape(key_len, head_count, -1).astype(jnp.float32)
    scores = jnp.einsum('qhd,khd->hqk', shaped_q, shaped_k) / math.sqrt(shaped_q.shape[2])
    query_idx = jnp.arange(query_len, dtype=jnp.int32)[:, None]
    key_idx = jnp.arange(key_len, dtype=jnp.int32)[None, :]
    distance = query_idx + window_len - key_idx
    visible = (distance >= 0) & (distance < window_len) & (distance <= doc_pos[:, None])
    masked = jnp.where(visible[None], scores, -jnp.inf)
    top_score = lax.optimization_barrier(jnp.max(masked, axis=2, keepdims=True))
    weights = jnp.exp(masked - top_score)
    probabilities = (weights / lax.optimization_barrier(jnp.sum(weights, axis=2, keepdims=True))).astype(jnp.bfloat16)
    return jnp.einsum('hqk,khd->qhd', probabilities.astype(jnp.float32), shaped_v).reshape(query_len, -1)

def reference(residual_in, query_rows, key_rows, value_rows, bc_weight, decay_rate, level_codes, level_scale, positions, ssm_gain):
    tokens, feature_count = residual_in.shape
    padding = jnp.zeros((WINDOW, feature_count), jnp.bfloat16)
    keys_all = jnp.concatenate([padding, key_rows], axis=0)
    values_all = jnp.concatenate([padding, value_rows], axis=0)

    def attend_at(index):
        start_row = index * WINDOW
        return attend_block(lax.dynamic_slice_in_dim(query_rows, start_row, WINDOW, 0), lax.dynamic_slice_in_dim(keys_all, start_row, 2 * WINDOW, 0), lax.dynamic_slice_in_dim(values_all, start_row, 2 * WINDOW, 0), lax.dynamic_slice_in_dim(positions, start_row, WINDOW, 0), ATT_HEADS)
    attended = lax.map(attend_at, jnp.arange(tokens // WINDOW, dtype=jnp.int32)).reshape(tokens, feature_count)
    hidden = (residual_in.astype(jnp.float32) + attended).astype(jnp.bfloat16)
    bc_full = jnp.dot(hidden, bc_weight, preferred_element_type=jnp.float32).astype(jnp.bfloat16)
    block_count = tokens // TOK_DEV
    b_blocks = bc_full[:, :STATES].reshape(block_count, TOK_DEV, STATES)
    c_blocks = bc_full[:, STATES:].reshape(block_count, TOK_DEV, STATES)
    values_h = hidden.reshape(block_count, TOK_DEV, SSM_HEADS, HEAD_VALUES)
    log_cum = -jnp.cumsum(decay_rate.reshape(block_count, TOK_DEV, SSM_HEADS), axis=1)
    log_end = log_cum[:, TOK_DEV - 1]
    scaled = (jnp.exp(log_end[:, None, :] - log_cum)[..., None] * values_h.astype(jnp.float32)).astype(jnp.bfloat16)
    states = jnp.einsum('jrn,jrhp->jnhp', b_blocks.astype(jnp.float32), scaled.astype(jnp.float32))
    prefix = jnp.cumsum(log_end, axis=0) - log_end
    span_log = prefix[:, None, :] - prefix[None, :, :] - log_end[None, :, :]
    block_idx = jnp.arange(block_count, dtype=jnp.int32)
    differ = jnp.bitwise_xor(block_idx[:, None], block_idx[None, :])
    cross_count = block_count.bit_length() - 1
    carried_list = []
    for bit_pos in range(cross_count):
        chosen = (block_idx[None, :] < block_idx[:, None]) & (differ >= 1 << bit_pos) & (differ < 2 << bit_pos)
        level_w = jnp.exp(jnp.where(chosen[:, :, None], span_log, -jnp.inf))
        carried_list.append(jnp.einsum('jih,inhp->jnhp', level_w, states, precision=lax.Precision.HIGHEST))
    carried = jnp.stack(carried_list, axis=1).astype(jnp.bfloat16)
    lambdas = (level_codes.astype(jnp.float32) * level_scale[None, :]).reshape(block_count, TOK_DEV, LEVELS)
    local_bits = TOK_DEV.bit_length() - 1
    token_index = jnp.arange(TOK_DEV, dtype=jnp.int32)
    xor_idx = jnp.bitwise_xor(token_index[:, None], token_index[None, :])
    causal = token_index[None, :] <= token_index[:, None]
    level_index = jnp.zeros((TOK_DEV, TOK_DEV), jnp.int32)
    for bit_pos in range(local_bits):
        level_index = level_index + (xor_idx >= 1 << bit_pos).astype(jnp.int32)

    def finish(operands):
        lam_blk, b_blk, c_blk, cum_blk, values_blk, carried_blk, hidden_blk = operands
        level_weight = jnp.take_along_axis(lam_blk, level_index, axis=1)
        gram_mat = jnp.dot(c_blk, b_blk.T, preferred_element_type=jnp.float32)
        shared = jnp.where(causal, gram_mat * level_weight, 0.0)
        cum_heads = cum_blk.T
        decay_mat = jnp.exp(jnp.where(causal[None], cum_heads[:, :, None] - cum_heads[:, None, :], -jnp.inf))
        mixing = (shared[None] * decay_mat).astype(jnp.bfloat16)
        intra_term = jnp.einsum('hts,shp->thp', mixing.astype(jnp.float32), values_blk.astype(jnp.float32))
        level_reads = jnp.einsum('rn,lnhp->rlhp', c_blk.astype(jnp.float32), carried_blk.astype(jnp.float32))
        lam_cross = lam_blk[:, local_bits + 1:local_bits + 1 + cross_count]
        cross_term = jnp.einsum('rl,rlhp->rhp', lam_cross, level_reads) * jnp.exp(cum_blk)[:, :, None]
        ssm_out = intra_term + cross_term
        inv_rms = lax.rsqrt(lax.optimization_barrier(jnp.mean(ssm_out * ssm_out, axis=2, keepdims=True)) + 1e-05)
        result = hidden_blk.astype(jnp.float32) + (ssm_out * inv_rms).reshape(TOK_DEV, -1) * ssm_gain[None, :]
        return result.astype(jnp.bfloat16)
    outputs = lax.map(finish, (lambdas, b_blocks, c_blocks, log_cum, values_h, carried, hidden.reshape(block_count, TOK_DEV, feature_count)))
    return outputs.reshape(tokens, feature_count)
```

```python
import functools
import math

import jax
import jax.numpy as jnp
import numpy as np
from jax import lax
from jax.experimental import pallas as pl
from jax.experimental.pallas import tpu as pltpu
from jax.sharding import PartitionSpec as P

HEAD_DIM = 128
HEAD_VALUES = 64
STATES = 128
WINDOW = 128
CHUNK = 128
NORM_TILE = 256
VMEM_LIMIT = 48 * 1024 * 1024
HIDDEN = -1e30

F32 = jnp.float32
BF16 = jnp.bfloat16


def params():
    return pltpu.CompilerParams(vmem_limit_bytes=VMEM_LIMIT)


def cost(flops, moved, transcendentals=0):
    return pl.CostEstimate(flops=flops, bytes_accessed=moved, transcendentals=transcendentals)


def fixed(shape):
    return pl.BlockSpec(shape, lambda i: (0,) * len(shape))


def dot(left, right):
    return jnp.dot(left, right, preferred_element_type=F32)


def widen_rows(rows, spread):
    high = rows.astype(BF16)
    low = (rows - high.astype(F32)).astype(BF16)
    return dot(high, spread) + dot(low, spread)


def decay_kernel(rate_ref, lower_ref, spread_ref, rise_ref, fall_ref, carry_ref, rows_ref, end_ref, prefix):
    @pl.when(pl.program_id(0) == 0)
    def _():
        prefix[...] = jnp.zeros_like(prefix)

    rate = rate_ref[...]
    first = rate.astype(BF16)
    rest = rate - first.astype(F32)
    second = rest.astype(BF16)
    third = (rest - second.astype(F32)).astype(BF16)
    total = dot(lower_ref[...], jnp.concatenate([first, second, third], axis=0))
    middle = total[CHUNK // 2 - 1 : CHUNK // 2]
    last = total[CHUNK - 1 :]
    before = prefix[0:1]
    rise_ref[...] = jnp.exp(total - middle)
    fall_ref[...] = jnp.exp(middle - total)
    carry_ref[...] = jnp.exp(-(total + before))
    after = before + last
    row_idx = lax.broadcasted_iota(jnp.int32, prefix.shape, 0)
    logs = jnp.where(
        row_idx == 0,
        middle - last,
        jnp.where(row_idx == 1, -last, jnp.where(row_idx == 2, -middle, 0.0)),
    )
    rows_ref[...] = widen_rows(jnp.exp(logs), spread_ref[...])
    prefix[...] = jnp.broadcast_to(after, prefix.shape)
    end_ref[...] = jnp.broadcast_to(-after, end_ref.shape)


def decay_factors(decay_rate, spread):
    row_count, heads = decay_rate.shape
    width = spread.shape[1]
    chunks = row_count // CHUNK
    lower = np.tril(np.ones((CHUNK, CHUNK), np.float32))
    lower = jnp.asarray(np.concatenate([lower] * 3, axis=1), BF16)
    rows = pl.BlockSpec((CHUNK, heads), lambda i: (i, 0))
    return pl.pallas_call(
        decay_kernel,
        grid=(chunks,),
        in_specs=[rows, fixed(lower.shape), fixed(spread.shape)],
        out_specs=[rows, rows, rows, pl.BlockSpec((8, width), lambda i: (i, 0)), fixed((8, heads))],
        out_shape=[jax.ShapeDtypeStruct((row_count, heads), F32)] * 3
        + [jax.ShapeDtypeStruct((chunks * 8, width), F32), jax.ShapeDtypeStruct((8, heads), F32)],
        scratch_shapes=[pltpu.VMEM((8, heads), F32)],
        compiler_params=params(),
        cost_estimate=cost(10**8, 5 * 10**6),
        name="decay_factors",
    )(decay_rate, lower, spread)


def attend_kernel(
    first_chunk,
    alias_count,
    half_ref,
    pos_ref,
    query_ref,
    key_before_ref,
    key_ref,
    value_before_ref,
    value_ref,
    residual_ref,
    own_weight_ref,
    other_weight_ref,
    rise_ref,
    spread_ref,
    *refs,
):
    hidden_ref, scaled_ref, b_ref, c_ref = refs[alias_count:]
    width = query_ref.shape[1]
    chunk = pl.program_id(0) + first_chunk
    key_row = lax.broadcasted_iota(jnp.int32, (WINDOW, WINDOW), 0)
    query_lane = lax.broadcasted_iota(jnp.int32, (WINDOW, WINDOW), 1)
    away = query_lane - key_row
    away = jnp.where(away < 0, away + WINDOW, away)
    doc_pos = pos_ref[pl.ds(chunk, 1), :]
    bias = jnp.where(away <= doc_pos, 0.0, HIDDEN).astype(F32).T
    current = query_lane <= key_row
    current_share = current.astype(F32).astype(BF16)
    before_share = (1.0 - current.astype(F32)).astype(BF16)
    ones = jnp.ones((2 * WINDOW, HEAD_DIM), BF16)
    factor = math.log2(math.e) / math.sqrt(HEAD_DIM)
    pieces = []
    for head in range(width // HEAD_DIM):
        lanes = slice(head * HEAD_DIM, (head + 1) * HEAD_DIM)
        keys = jnp.concatenate([key_before_ref[:, lanes], key_ref[:, lanes]], axis=0)
        values = jnp.concatenate([value_before_ref[:, lanes], value_ref[:, lanes]], axis=0)
        scores = lax.dot_general(
            query_ref[:, lanes], keys, (((1,), (1,)), ((), ())), preferred_element_type=F32
        )
        merged = jnp.where(current, scores[:, WINDOW:], scores[:, :WINDOW]) + bias
        top = jnp.max(merged, axis=1, keepdims=True)
        weights = jnp.exp2((merged - top) * factor).astype(BF16)
        weights = jnp.concatenate([weights * before_share, weights * current_share], axis=1)
        summed = dot(weights, jnp.concatenate([values, ones], axis=1))
        attended = summed[:, :HEAD_DIM] / summed[:, HEAD_DIM:]
        pieces.append((residual_ref[:, lanes].astype(F32) + attended).astype(BF16))
    hidden = jnp.concatenate(pieces, axis=1)
    hidden_ref[...] = hidden
    rise = widen_rows(rise_ref[...], spread_ref[...])
    scaled_ref[...] = (rise * hidden.astype(F32)).astype(BF16)
    low, high = hidden[:, : width // 2], hidden[:, width // 2 :]
    is_low = half_ref[0] == 0
    own = jnp.where(is_low, low, high)
    other = jnp.where(is_low, high, low)
    shared = dot(own, own_weight_ref[...]) + dot(other, other_weight_ref[...])
    b_ref[...] = shared[:, :STATES].astype(BF16)
    c_ref[...] = shared[:, STATES:].astype(BF16)


def attend(first, count, half, positions, query, key, value, edges, residual, weights, rise, spread, held):
    row_count, width = query.shape
    heads = rise.shape[1]

    def rows(columns, shift=0):
        return pl.BlockSpec((CHUNK, columns), lambda i: (i + first + shift, 0))

    if edges is None:
        key_before, value_before = key, value
        before = rows(width, -1)
    else:
        key_before, value_before = edges
        before = pl.BlockSpec((CHUNK, width), lambda i: (i, 0))
    aliased = [] if held is None else list(held)
    in_specs = [
        pl.BlockSpec(memory_space=pltpu.SMEM),
        fixed(positions.shape),
        rows(width),
        before,
        rows(width),
        before,
        rows(width),
        rows(width),
        fixed(weights[0].shape),
        fixed(weights[1].shape),
        rows(heads),
        fixed(spread.shape),
    ]
    arg_count = len(in_specs)
    in_specs += [pl.BlockSpec(memory_space=pl.ANY)] * len(aliased)
    part = pl.BlockSpec((CHUNK, STATES), lambda i: (i, 0))
    return pl.pallas_call(
        functools.partial(attend_kernel, first, len(aliased)),
        grid=(count,),
        in_specs=in_specs,
        out_specs=[rows(width), rows(width), part, part],
        out_shape=[jax.ShapeDtypeStruct((row_count, width), BF16)] * 2
        + [jax.ShapeDtypeStruct((count * CHUNK, STATES), BF16)] * 2,
        input_output_aliases={arg_count + i: i for i in range(len(aliased))},
        compiler_params=params(),
        cost_estimate=cost(count * 3 * 10**8, count * 2 * 10**6),
        name="window_attention",
    )(half, positions, query, key_before, key, value_before, value, residual, *weights, rise, spread, *aliased)


def state_kernel(own_ref, other_ref, scaled_ref, rows_ref, state_ref, turned):
    chunks = scaled_ref.shape[0] // CHUNK

    @pl.when(pl.program_id(0) == 0)
    def _():
        b_mat = own_ref[...].astype(F32) + other_ref[...].astype(F32)
        for chunk in range(chunks):
            span = slice(chunk * CHUNK, (chunk + 1) * CHUNK)
            turned[:, span] = b_mat[span].T.astype(BF16)

    total = None
    for chunk in range(chunks):
        span = slice(chunk * CHUNK, (chunk + 1) * CHUNK)
        added = dot(turned[:, span], scaled_ref[span, :]) * rows_ref[chunk * 8 : chunk * 8 + 1]
        total = added if total is None else total * rows_ref[chunk * 8 + 1 : chunk * 8 + 2] + added
    state_ref[...] = total.astype(BF16)


def block_state(b_own, b_other, scaled, factor_rows):
    row_count, width = scaled.shape
    tile = min(width, 256)
    return pl.pallas_call(
        state_kernel,
        grid=(width // tile,),
        in_specs=[
            fixed(b_own.shape),
            fixed(b_own.shape),
            pl.BlockSpec((row_count, tile), lambda i: (0, i)),
            pl.BlockSpec((factor_rows.shape[0], tile), lambda i: (0, i)),
        ],
        out_specs=pl.BlockSpec((STATES, tile), lambda i: (0, i)),
        out_shape=jax.ShapeDtypeStruct((STATES, width), BF16),
        scratch_shapes=[pltpu.VMEM((STATES, row_count), BF16)],
        compiler_params=params(),
        cost_estimate=cost(3 * 10**8, 4 * 10**6),
        name="block_state",
    )(b_own, b_other, scaled, factor_rows)


def local_kernel(
    local_levels,
    cross_levels,
    b_own_ref,
    b_other_ref,
    c_own_ref,
    c_other_ref,
    codes_ref,
    scale_ref,
    scaled_ref,
    fall_ref,
    rows_ref,
    spread_ref,
    local_ref,
    reads_ref,
    held,
):
    chunk = pl.program_id(0)

    @pl.when(chunk == 0)
    def _():
        held[...] = jnp.zeros_like(held)

    b_mat = b_own_ref[...].astype(F32) + b_other_ref[...].astype(F32)
    c_mat = (c_own_ref[...].astype(F32) + c_other_ref[...].astype(F32)).astype(BF16)
    lam = codes_ref[...].astype(F32) * scale_ref[...]
    gram = lax.dot_general(
        c_mat, b_mat.astype(BF16), (((1,), (1,)), ((), ())), preferred_element_type=F32
    )
    query_row = lax.broadcasted_iota(jnp.int32, (CHUNK, CHUNK), 0)
    key_lane = lax.broadcasted_iota(jnp.int32, (CHUNK, CHUNK), 1)
    differ = jnp.bitwise_xor(query_row, key_lane)
    inner_levels = CHUNK.bit_length() - 1

    def column(level):
        return jnp.broadcast_to(lam[:, level : level + 1], (CHUNK, CHUNK))

    weight = column(0)
    for level in range(1, inner_levels + 1):
        weight = jnp.where(differ >= 1 << (level - 1), column(level), weight)
    mixing = jnp.where(key_lane <= query_row, gram * weight, 0.0).astype(BF16)
    c_wide = c_mat.astype(F32)
    left = [mixing]
    right = [scaled_ref[...]]
    for level in range(local_levels):
        left.append((c_wide * column(inner_levels + 1 + level)).astype(BF16))
        right.append((held[level] * rows_ref[2:3]).astype(BF16))
    summed = dot(jnp.concatenate(left, axis=1), jnp.concatenate(right, axis=0))
    local_ref[...] = (summed * widen_rows(fall_ref[...], spread_ref[...])).astype(local_ref.dtype)
    for level in range(cross_levels):
        at = inner_levels + 1 + local_levels + level
        reads_ref[:, level * STATES : (level + 1) * STATES] = (c_wide * column(at)).astype(BF16)

    state = dot(b_mat.T.astype(BF16), scaled_ref[...]) * rows_ref[0:1]
    fade = rows_ref[1:2]

    def place(level, joined):
        if level == local_levels:
            return
        taken = jnp.bitwise_and(jnp.right_shift(chunk, level), 1) == 1

        @pl.when(jnp.logical_not(taken))
        def _():
            held[level] = joined
            for later in range(level + 1, local_levels):
                held[later] = held[later] * fade

        @pl.when(taken)
        def _():
            both = joined + held[level] * fade
            held[level] = jnp.zeros_like(joined)
            place(level + 1, both)

    place(0, state)


def local_terms(b_own, b_other, c_own, c_other, codes, scale, scaled, fall, factor_rows, spread, cross_levels):
    row_count, width = scaled.shape
    heads = fall.shape[1]
    levels = codes.shape[1]
    chunks = row_count // CHUNK
    local_levels = chunks.bit_length() - 1

    def rows(columns):
        return pl.BlockSpec((CHUNK, columns), lambda i: (i, 0))

    return pl.pallas_call(
        functools.partial(local_kernel, local_levels, cross_levels),
        grid=(chunks,),
        in_specs=[rows(STATES)] * 4
        + [
            rows(levels),
            fixed((1, levels)),
            rows(width),
            rows(heads),
            pl.BlockSpec((8, width), lambda i: (i, 0)),
            fixed(spread.shape),
        ],
        out_specs=[rows(width), rows(cross_levels * STATES)],
        out_shape=[
            jax.ShapeDtypeStruct((row_count, width), BF16),
            jax.ShapeDtypeStruct((row_count, cross_levels * STATES), BF16),
        ],
        scratch_shapes=[pltpu.VMEM((local_levels, STATES, width), F32)],
        compiler_params=params(),
        cost_estimate=cost(2 * 10**9, 8 * 10**6),
        name="local_terms",
    )(b_own, b_other, c_own, c_other, codes, scale, scaled, fall, factor_rows, spread)


def finish_kernel(
    cross_levels,
    half_ref,
    near_ref,
    own_ref,
    other_ref,
    before_ref,
    reads_ref,
    local_ref,
    hidden_ref,
    carry_ref,
    spread_ref,
    mean_ref,
    gain_ref,
    out_ref,
    carried,
):
    width = hidden_ref.shape[1]
    half_width = width // 2

    @pl.when(pl.program_id(0) == 0)
    def _():
        carried[0:STATES] = (near_ref[...].astype(F32) * before_ref[0:1]).astype(BF16)
        is_low = half_ref[0] == 0
        for level in range(1, cross_levels):
            span = slice((level - 1) * STATES, level * STATES)
            own, other = own_ref[span, :], other_ref[span, :]
            low = jnp.where(is_low, own, other).astype(F32)
            high = jnp.where(is_low, other, own).astype(F32)
            row = before_ref[level : level + 1]
            target = slice(level * STATES, (level + 1) * STATES)
            carried[target, :half_width] = (low * row[:, :half_width]).astype(BF16)
            carried[target, half_width:] = (high * row[:, half_width:]).astype(BF16)

    cross = dot(reads_ref[...], carried[...])
    mixed = local_ref[...].astype(F32) + cross * widen_rows(carry_ref[...], spread_ref[...])
    squares = (mixed * mixed).astype(BF16)
    tile = mean_ref.shape[0]
    for at in range(0, width, tile):
        lanes = slice(at, at + tile)
        mean = dot(squares[:, lanes], mean_ref[...])
        normed = mixed[:, lanes] * lax.rsqrt(mean + 1e-05) * gain_ref[:, lanes]
        out_ref[:, lanes] = (hidden_ref[:, lanes].astype(F32) + normed).astype(BF16)


def finish(half, near, own, other, before, reads, local, hidden, carry, spread, gain):
    row_count, width = hidden.shape
    heads = carry.shape[1]
    cross_levels = before.shape[0]
    tile = min(width, NORM_TILE)
    place = np.arange(tile) // HEAD_VALUES
    mean = jnp.asarray((place[:, None] == place[None, :]) / HEAD_VALUES, BF16)
    step = 2 * CHUNK

    def rows(columns):
        return pl.BlockSpec((step, columns), lambda i: (i, 0))

    return pl.pallas_call(
        functools.partial(finish_kernel, cross_levels),
        grid=(row_count // step,),
        in_specs=[
            pl.BlockSpec(memory_space=pltpu.SMEM),
            fixed(near.shape),
            fixed(own.shape),
            fixed(other.shape),
            fixed(before.shape),
            rows(cross_levels * STATES),
            rows(width),
            rows(width),
            rows(heads),
            fixed(spread.shape),
            fixed(mean.shape),
            fixed(gain.shape),
        ],
        out_specs=rows(width),
        out_shape=jax.ShapeDtypeStruct((row_count, width), BF16),
        scratch_shapes=[pltpu.VMEM((cross_levels * STATES, width), BF16)],
        compiler_params=params(),
        cost_estimate=cost(2 * 10**9, 8 * 10**6),
        name="carried_and_norm",
    )(half, near, own, other, before, reads, local, hidden, carry, spread, mean, gain)


def from_behind(x, axis, by):
    length = lax.axis_size(axis)
    return lax.ppermute(x, axis, [(i, i + by) for i in range(length - by)])


def partner(x, axis, distance):
    return lax.ppermute(x, axis, [(i, i ^ 1 << distance) for i in range(lax.axis_size(axis))])


def summed_over_heads(share):
    rounds = lax.axis_size("head").bit_length() - 1
    if rounds == 0:
        return share, jnp.zeros_like(share)
    total = share
    for distance in range(rounds - 1):
        total = (total.astype(F32) + partner(total, "head", distance).astype(F32)).astype(BF16)
    return total, partner(total, "head", rounds - 1)


def body(
    residual_in,
    query_rows,
    key_rows,
    value_rows,
    bc_weight,
    decay_rate,
    level_codes,
    level_scale,
    positions,
    ssm_gain,
):
    row_count, width = residual_in.shape
    heads = decay_rate.shape[1]
    chunks = row_count // CHUNK
    half_width = width // 2
    spread = jnp.asarray(np.arange(width)[None, :] // HEAD_VALUES == np.arange(heads)[:, None], BF16)
    half_index = lax.axis_index("fsdp")
    half = half_index.reshape(1).astype(jnp.int32)

    edges = from_behind(
        (key_rows[row_count - WINDOW :], value_rows[row_count - WINDOW :]), ("seq", "fsdp"), 1
    )
    weights = (bc_weight, partner(bc_weight, "fsdp", 0))
    rise, fall, carry, factor_rows, end_rows = decay_factors(decay_rate, spread)
    pos_rows = positions.reshape(chunks, CHUNK)

    held = None
    b_parts, c_parts = [], []
    split = chunks // 2
    for first, count in ((split, chunks - split), (1, split - 1), (0, 1)):
        hidden, scaled, b_part, c_part = attend(
            first,
            count,
            half,
            pos_rows,
            query_rows,
            key_rows,
            value_rows,
            edges if first == 0 else None,
            residual_in,
            weights,
            rise,
            spread,
            held,
        )
        held = (hidden, scaled)
        b_parts.insert(0, summed_over_heads(b_part))
        c_parts.insert(0, c_part)
    c_part = jnp.concatenate(c_parts, axis=0)
    c_own, c_other = summed_over_heads(c_part)
    b_own = jnp.concatenate([part[0] for part in b_parts], axis=0)
    b_other = jnp.concatenate([part[1] for part in b_parts], axis=0)
    state = block_state(b_own, b_other, scaled, factor_rows)

    shard_axes = ("seq", "fsdp")
    shard_total = lax.axis_size(shard_axes)
    shard = lax.axis_index(shard_axes)
    cross_levels = shard_total.bit_length() - 1
    ends = lax.all_gather(end_rows[0], shard_axes)
    shard_idx = jnp.arange(shard_total)
    before_rows, upper_fades, lower_fades = [], [], []
    for level in range(cross_levels):
        is_upper = jnp.bitwise_and(jnp.right_shift(shard, level), 1) == 1
        run = jnp.right_shift(shard, level) << level
        sibling = jnp.bitwise_xor(run, 1 << level)

        def run_end(start, stop):
            inside = (shard_idx >= start) & (shard_idx < stop)
            return jnp.sum(jnp.where(inside[:, None], ends, 0.0), axis=0)

        between = run_end(run, shard)
        own_end = run_end(run, run + (1 << level))
        other_end = run_end(sibling, sibling + (1 << level))
        before_rows.append(jnp.where(is_upper, jnp.exp(between), 0.0))
        upper_fades.append(jnp.where(is_upper, 1.0, jnp.exp(other_end)))
        lower_fades.append(jnp.where(is_upper, jnp.exp(own_end), 1.0))
    stacked = jnp.repeat(jnp.stack(before_rows + upper_fades + lower_fades), HEAD_VALUES, axis=-1)
    before = stacked[:cross_levels]
    own_fades = stacked[cross_levels : 2 * cross_levels]
    other_fades = stacked[2 * cross_levels :]

    def own_half(x):
        return jnp.where(half_index == 0, x[..., :half_width], x[..., half_width:])

    own_fades = own_half(own_fades)
    other_fades = own_half(other_fades)

    near = partner(state, "fsdp", 0)
    joined = (
        own_half(state).astype(F32) * own_fades[0] + own_half(near).astype(F32) * other_fades[0]
    ).astype(BF16)
    received = []
    for level in range(1, cross_levels):
        other = partner(joined, "seq", level - 1)
        received.append(other)
        joined = (joined.astype(F32) * own_fades[level] + other.astype(F32) * other_fades[level]).astype(BF16)
    own_received = jnp.concatenate(received, axis=0)
    other_received = jnp.concatenate([partner(x, "fsdp", 0) for x in received], axis=0)

    local, reads = local_terms(
        b_own,
        b_other,
        c_own,
        c_other,
        level_codes,
        level_scale[None, :],
        scaled,
        fall,
        factor_rows,
        spread,
        cross_levels,
    )
    return finish(
        half, near, own_received, other_received, before, reads, local, hidden, carry, spread, ssm_gain[None, :]
    )


def solution(mesh):
    in_specs = (
        P(("groups", "seq", "fsdp"), "head"),
        P(("groups", "seq", "fsdp"), "head"),
        P(("groups", "seq", "fsdp"), "head"),
        P(("groups", "seq", "fsdp"), "head"),
        P(("head", "fsdp"), None),
        P(("groups", "seq", "fsdp"), "head"),
        P(("groups", "seq", "fsdp"), None),
        P(),
        P(("groups", "seq", "fsdp")),
        P("head"),
    )
    out_specs = P(("groups", "seq", "fsdp"), "head")
    return jax.shard_map(body, mesh=mesh, in_specs=in_specs, out_specs=out_specs, check_vma=False)
```

```python
import functools
import math

import jax
import jax.numpy as jnp
from jax import lax
from jax.experimental import pallas as pl
from jax.experimental.pallas import tpu as pltpu
from jax.sharding import PartitionSpec as P

HEAD_DIM = 128
HEAD_VALUES = 64
STATES = 128
WINDOW = 128
CHUNK = 128
EXTRA = 16
VMEM_LIMIT = 24 * 1024 * 1024
HIDDEN = -1e30

F32 = jnp.float32
BF16 = jnp.bfloat16
VMEM = pl.BlockSpec(memory_space=pltpu.VMEM)
SMEM = pl.BlockSpec(memory_space=pltpu.SMEM)
HBM = pl.BlockSpec(memory_space=pltpu.HBM)


def params():
    return pltpu.CompilerParams(vmem_limit_bytes=VMEM_LIMIT)


def cost(flops, moved, transcendentals=0):
    return pl.CostEstimate(flops=flops, bytes_accessed=moved, transcendentals=transcendentals)


def shaped(shape, dtype):
    return pltpu.VMEM(shape, dtype)


def far_shaped(shape, dtype):
    return pltpu.HBM(shape, dtype)


def near_by(*arrays):
    return [pltpu.with_memory_space_constraint(x, pltpu.VMEM) for x in arrays]


def far_off(*arrays):
    return [pltpu.with_memory_space_constraint(x, pltpu.HBM) for x in arrays]


def dot(left, right):
    return jnp.dot(left, right, preferred_element_type=F32)


def dot_turned(left, right):
    return lax.dot_general(left, right, (((1,), (1,)), ((), ())), preferred_element_type=F32)


def chunk_rows(index, count=1):
    return pl.ds(pl.multiple_of(index * CHUNK, CHUNK), count * CHUNK)


def spread_matrix(heads, width):
    lane = lax.broadcasted_iota(jnp.int32, (heads, width), 1)
    start = lax.broadcasted_iota(jnp.int32, (heads, width), 0) * HEAD_VALUES
    return ((lane >= start) & (lane < start + HEAD_VALUES)).astype(F32).astype(BF16)


def lane_tiles(width):
    tile = min(width, 256)
    return [slice(at, at + tile) for at in range(0, width, tile)]


def split_rows(rows):
    high = rows.astype(BF16)
    return high, (rows - high.astype(F32)).astype(BF16)


def edge_kernel(key_ref, value_ref, edge_ref, sems):
    row_count = key_ref.shape[0]
    copies = [
        pltpu.make_async_copy(
            ref.at[pl.ds(row_count - WINDOW, WINDOW)], edge_ref.at[pl.ds(at * WINDOW, WINDOW)], sems.at[at]
        )
        for at, ref in enumerate((key_ref, value_ref))
    ]
    for copy in copies:
        copy.start()
    for copy in copies:
        copy.wait()


def edge_rows(key_rows, value_rows):
    width = key_rows.shape[1]
    return pl.pallas_call(
        edge_kernel,
        in_specs=[HBM, HBM],
        out_specs=VMEM,
        out_shape=shaped((2 * WINDOW, width), BF16),
        scratch_shapes=[pltpu.SemaphoreType.DMA((2,))],
        compiler_params=params(),
        cost_estimate=cost(0, 2**20),
        name="edge_rows",
    )(*far_off(key_rows, value_rows))


def chunk_masks(doc_pos):
    key_row = lax.broadcasted_iota(jnp.int32, (WINDOW, WINDOW), 0)
    query_lane = lax.broadcasted_iota(jnp.int32, (WINDOW, WINDOW), 1)
    away = query_lane - key_row
    away = jnp.where(away < 0, away + WINDOW, away)
    bias = jnp.where(away <= doc_pos, 0.0, HIDDEN).astype(F32).T
    return bias


def attend_chunk(bias, query, key_before, key, value_before, value, residual):
    query_row = lax.broadcasted_iota(jnp.int32, (WINDOW, WINDOW), 0)
    key_lane = lax.broadcasted_iota(jnp.int32, (WINDOW, WINDOW), 1)
    current = key_lane <= query_row
    current_share = current.astype(F32).astype(BF16)
    before_share = (1.0 - current.astype(F32)).astype(BF16)
    ones = jnp.ones((2 * WINDOW, HEAD_DIM), BF16)
    factor = math.log2(math.e) / math.sqrt(HEAD_DIM)
    scores = dot_turned(query, jnp.concatenate([key_before, key], axis=0))
    merged = jnp.where(current, scores[:, WINDOW:], scores[:, :WINDOW]) + bias
    top = jnp.max(merged, axis=1, keepdims=True)
    weights = jnp.exp2((merged - top) * factor).astype(BF16)
    weights = jnp.concatenate([weights * before_share, weights * current_share], axis=1)
    values = jnp.concatenate([value_before, value], axis=0)
    summed = dot(weights, jnp.concatenate([values, ones], axis=1))
    attended = summed[:, :HEAD_DIM] / summed[:, HEAD_DIM:]
    return (residual.astype(F32) + attended).astype(BF16)


def attend_heads(bias, width, query, key_before, key, value_before, value, residual, hidden):
    def lanes_of(at, ref, rows):
        return ref[rows, at : at + HEAD_DIM]

    for at in range(0, width, HEAD_DIM):
        hidden[0][hidden[1], at : at + HEAD_DIM] = attend_chunk(
            bias,
            lanes_of(at, *query),
            lanes_of(at, *key_before),
            lanes_of(at, *key),
            lanes_of(at, *value_before),
            lanes_of(at, *value),
            lanes_of(at, *residual),
        )


def most_kernel(
    place_ref,
    pos_ref,
    query_ref,
    key_ref,
    value_ref,
    residual_ref,
    own_weight_ref,
    other_weight_ref,
    hidden_ref,
    hidden_far_ref,
    b_ref,
    c_ref,
    weight_ref,
    first_query_ref,
    first_key_ref,
    first_value_ref,
    first_residual_ref,
    query_buf,
    key_buf,
    value_buf,
    residual_buf,
    sems,
    out_sems,
):
    row_count, width = query_ref.shape
    chunks = row_count // CHUNK
    half_width = width // 2
    arrays = (
        (key_ref, key_buf, first_key_ref),
        (value_ref, value_buf, first_value_ref),
        (query_ref, query_buf, first_query_ref),
        (residual_ref, residual_buf, first_residual_ref),
    )

    def copy(which, chunk):
        source, buffer, _ = arrays[which]
        rows = chunk_rows(chunk)
        return pltpu.make_async_copy(source.at[rows], buffer.at[rows], sems.at[which, chunk])

    def copy_out(chunk):
        rows = chunk_rows(chunk)
        return pltpu.make_async_copy(hidden_ref.at[rows], hidden_far_ref.at[rows], out_sems.at[chunk])

    for which in range(2):
        copy(which, 0).start()
    for chunk in range(1, chunks):
        for which in range(4):
            copy(which, chunk).start()
    for which in range(2, 4):
        copy(which, 0).start()
    is_low = place_ref[0] == 0
    own_weight, other_weight = own_weight_ref[...], other_weight_ref[...]
    weight_ref[:half_width, :] = jnp.where(is_low, own_weight, other_weight)
    weight_ref[half_width:, :] = jnp.where(is_low, other_weight, own_weight)
    for which in range(2):
        copy(which, 0).wait()

    def step(chunk, carry):
        for which in range(4):
            copy(which, chunk).wait()
        rows, before = chunk_rows(chunk), chunk_rows(chunk - 1)
        bias = chunk_masks(pos_ref[pl.ds(chunk, 1), :])
        attend_heads(
            bias,
            width,
            (query_buf, rows),
            (key_buf, before),
            (key_buf, rows),
            (value_buf, before),
            (value_buf, rows),
            (residual_buf, rows),
            (hidden_ref, rows),
        )
        copy_out(chunk).start()
        shared = dot(hidden_ref[rows, :], weight_ref[...])
        b_ref[chunk_rows(chunk - 1), :] = shared[:, :STATES].astype(BF16)
        c_ref[rows, :] = shared[:, STATES:].astype(BF16)
        return carry

    lax.fori_loop(1, chunks, step, 0)
    for which in range(2, 4):
        copy(which, 0).wait()
    for _, buffer, first in arrays:
        first[...] = buffer[:CHUNK]
    for chunk in range(1, chunks):
        copy_out(chunk).wait()


def attend_most(place, positions, query, key, value, residual, weights):
    row_count, width = query.shape
    chunks = row_count // CHUNK
    return pl.pallas_call(
        most_kernel,
        in_specs=[SMEM, VMEM] + [HBM] * 4 + [VMEM] * 2,
        out_specs=[VMEM, HBM] + [VMEM] * 7,
        out_shape=[
            shaped((row_count, width), BF16),
            far_shaped((row_count, width), BF16),
            shaped((row_count - CHUNK, STATES), BF16),
            shaped((row_count, STATES), BF16),
            shaped((width, 2 * STATES), BF16),
        ]
        + [shaped((CHUNK, width), BF16)] * 4,
        scratch_shapes=[pltpu.VMEM((row_count, width), BF16)] * 4
        + [pltpu.SemaphoreType.DMA((4, chunks)), pltpu.SemaphoreType.DMA((chunks,))],
        compiler_params=params(),
        cost_estimate=cost(3 * 10**9, 10**7),
        name="attention_most",
    )(place, *near_by(positions), *far_off(query, key, value, residual), *near_by(*weights))


def first_kernel(
    pos_ref,
    edge_ref,
    query_ref,
    key_ref,
    value_ref,
    residual_ref,
    weight_ref,
    hidden_in_ref,
    hidden_far_in_ref,
    c_in_ref,
    hidden_ref,
    hidden_far_ref,
    c_ref,
    b_ref,
    c_far_ref,
    sems,
):
    width = query_ref.shape[1]
    rows = slice(0, CHUNK)
    attend_heads(
        chunk_masks(pos_ref[0:1, :]),
        width,
        (query_ref, rows),
        (edge_ref, slice(0, WINDOW)),
        (key_ref, rows),
        (edge_ref, slice(WINDOW, 2 * WINDOW)),
        (value_ref, rows),
        (residual_ref, rows),
        (hidden_ref, rows),
    )
    span = pl.ds(0, CHUNK)
    hidden_copy = pltpu.make_async_copy(hidden_ref.at[span], hidden_far_ref.at[span], sems.at[0])
    hidden_copy.start()
    shared = dot(hidden_ref[rows, :], weight_ref[...])
    b_ref[...] = shared[:, :STATES].astype(BF16)
    c_ref[rows, :] = shared[:, STATES:].astype(BF16)
    c_copy = pltpu.make_async_copy(c_ref, c_far_ref, sems.at[1])
    c_copy.start()
    hidden_copy.wait()
    c_copy.wait()


def attend_first(positions, edges, firsts, weight, hidden, hidden_far, c_mat):
    width = hidden.shape[1]
    return pl.pallas_call(
        first_kernel,
        in_specs=[VMEM] * 8 + [HBM, VMEM],
        out_specs=[VMEM, HBM, VMEM, VMEM, HBM],
        out_shape=[
            shaped(hidden.shape, BF16),
            far_shaped(hidden.shape, BF16),
            shaped(c_mat.shape, BF16),
            shaped((CHUNK, STATES), BF16),
            far_shaped(c_mat.shape, BF16),
        ],
        input_output_aliases={7: 0, 8: 1, 9: 2},
        scratch_shapes=[pltpu.SemaphoreType.DMA((2,))],
        compiler_params=params(),
        cost_estimate=cost(4 * 10**8, 2 * 10**6),
        name="attention_first",
    )(*near_by(positions, edges, *firsts, weight, hidden), *far_off(hidden_far), *near_by(c_mat))


def lower_ones():
    row = lax.broadcasted_iota(jnp.int32, (CHUNK, CHUNK), 0)
    lane = lax.broadcasted_iota(jnp.int32, (CHUNK, CHUNK), 1)
    lower = (lane <= row).astype(F32).astype(BF16)
    return jnp.concatenate([lower] * 3, axis=1)


def chunk_sums(lower, rate):
    first = rate.astype(BF16)
    second, third = split_rows(rate - first.astype(F32))
    return dot_turned(lower, jnp.concatenate([first, second, third], axis=1))


def scale_kernel(rate_ref, hidden_ref, scaled_ref, rows_ref):
    heads, row_count = rate_ref.shape
    width = hidden_ref.shape[1]
    spread = spread_matrix(heads, width)
    lower = lower_ones()
    row_idx = lax.broadcasted_iota(jnp.int32, (8, heads), 0)

    def step(chunk, token):
        rows = chunk_rows(chunk)
        total = chunk_sums(lower, rate_ref[:, rows])
        middle = total[CHUNK // 2 - 1 : CHUNK // 2]
        last = total[CHUNK - 1 :]
        rise = jnp.exp(total - middle).astype(BF16)
        logs = jnp.where(
            row_idx == 0,
            middle - last,
            jnp.where(row_idx == 1, -last, jnp.where(row_idx == 2, -middle, 0.0)),
        )
        high, low = split_rows(jnp.exp(logs))
        factors = pl.ds(pl.multiple_of(chunk * 8, 8), 8)
        for lanes in lane_tiles(width):
            wide = dot(rise, spread[:, lanes])
            scaled_ref[rows, lanes] = (wide * hidden_ref[rows, lanes].astype(F32)).astype(BF16)
            rows_ref[factors, lanes] = dot(high, spread[:, lanes]) + dot(low, spread[:, lanes])
        return token

    lax.fori_loop(0, row_count // CHUNK, step, 0)


def scale_hidden(rate_turned, hidden):
    row_count, width = hidden.shape
    return pl.pallas_call(
        scale_kernel,
        in_specs=[VMEM] * 2,
        out_specs=[VMEM] * 2,
        out_shape=[shaped((row_count, width), BF16), shaped((row_count // CHUNK * 8, width), F32)],
        compiler_params=params(),
        cost_estimate=cost(10**9, 4 * 10**6),
        name="scale_hidden",
    )(*near_by(rate_turned, hidden))


def state_kernel(
    own_first_ref,
    own_most_ref,
    other_first_ref,
    other_most_ref,
    scaled_ref,
    rows_ref,
    state_ref,
    b_far_ref,
    b_buf,
    turned,
    sems,
):
    row_count, width = scaled_ref.shape
    chunks = row_count // CHUNK
    b_buf[:CHUNK, :] = (own_first_ref[...].astype(F32) + other_first_ref[...].astype(F32)).astype(BF16)
    b_buf[CHUNK:, :] = (own_most_ref[...].astype(F32) + other_most_ref[...].astype(F32)).astype(BF16)
    b_copy = pltpu.make_async_copy(b_buf, b_far_ref, sems.at[0])
    b_copy.start()
    for chunk in range(chunks):
        span = slice(chunk * CHUNK, (chunk + 1) * CHUNK)
        turned[:, span] = b_buf[span, :].astype(F32).T.astype(BF16)
    tile = min(width, 256)

    def step(at, carry):
        lanes = pl.ds(pl.multiple_of(at * tile, tile), tile)
        total = fade = None
        for chunk in range(chunks):
            span = slice(chunk * CHUNK, (chunk + 1) * CHUNK)
            added = dot(turned[:, span], scaled_ref[span, lanes]) * rows_ref[chunk * 8 : chunk * 8 + 1, lanes]
            fades = rows_ref[chunk * 8 + 1 : chunk * 8 + 2, lanes]
            total = added if total is None else total * fades + added
            fade = fades if fade is None else fade * fades
        state_ref[:STATES, lanes] = total.astype(BF16)
        state_ref[STATES:, lanes] = fade_rows(fade)
        return carry

    lax.fori_loop(0, width // tile, step, 0)
    b_copy.wait()


def fade_rows(fade):
    high, low = split_rows(fade)
    row = lax.broadcasted_iota(jnp.int32, (EXTRA, fade.shape[1]), 0)
    return jnp.where(row == 0, high.astype(F32), jnp.where(row == 1, low.astype(F32), 0.0)).astype(BF16)


def fade_of(message):
    return message[STATES : STATES + 1].astype(F32) + message[STATES + 1 : STATES + 2].astype(F32)


def block_state(own_first, own_most, other_first, other_most, scaled, factor_rows):
    row_count, width = scaled.shape
    return pl.pallas_call(
        state_kernel,
        in_specs=[VMEM] * 6,
        out_specs=[VMEM, HBM],
        out_shape=[shaped((STATES + EXTRA, width), BF16), far_shaped((row_count, STATES), BF16)],
        scratch_shapes=[
            pltpu.VMEM((row_count, STATES), BF16),
            pltpu.VMEM((STATES, row_count), BF16),
            pltpu.SemaphoreType.DMA((1,)),
        ],
        compiler_params=params(),
        cost_estimate=cost(3 * 10**8, 4 * 10**6),
        name="block_state",
    )(*near_by(own_first, own_most, other_first, other_most, scaled, factor_rows))


def join_kernel(level, place_ref, own_ref, other_ref, joined_ref):
    half_width = joined_ref.shape[1]
    own, other = own_ref[...], other_ref[...]
    if own.shape[1] != half_width:
        is_low = place_ref[0] == 0
        own = jnp.where(is_low, own[:, :half_width], own[:, half_width:])
        other = jnp.where(is_low, other[:, :half_width], other[:, half_width:])
    upper = place_ref[1 + level] == 1
    own_fade, other_fade = fade_of(own), fade_of(other)
    lower, higher = jnp.where(upper, other, own), jnp.where(upper, own, other)
    fade = jnp.where(upper, own_fade, other_fade)
    joined_ref[:STATES, :] = (lower[:STATES].astype(F32) * fade + higher[:STATES].astype(F32)).astype(BF16)
    joined_ref[STATES:, :] = fade_rows(own_fade * other_fade)


def join(level, place, own, other, half_width):
    return pl.pallas_call(
        functools.partial(join_kernel, level),
        in_specs=[SMEM, VMEM, VMEM],
        out_specs=VMEM,
        out_shape=shaped((own.shape[0], half_width), BF16),
        compiler_params=params(),
        cost_estimate=cost(10**6, 10**5),
        name="join_runs",
    )(place, *near_by(own, other))


def local_kernel(
    local_levels,
    cross_levels,
    b_far_ref,
    c_far_ref,
    c_other_ref,
    codes_ref,
    scale_ref,
    rate_ref,
    scaled_ref,
    rows_ref,
    local_ref,
    reads_ref,
    carry_wide_ref,
    b_buf,
    c_buf,
    held,
    fresh,
    sems,
):
    row_count, width = scaled_ref.shape
    heads = rate_ref.shape[0]
    copies = [
        pltpu.make_async_copy(b_far_ref, b_buf, sems.at[0]),
        pltpu.make_async_copy(c_far_ref, c_buf, sems.at[1]),
    ]
    for copy in copies:
        copy.start()
    spread = spread_matrix(heads, width)
    lower = lower_ones()
    held[...] = jnp.zeros_like(held)
    query_row = lax.broadcasted_iota(jnp.int32, (CHUNK, CHUNK), 0)
    key_lane = lax.broadcasted_iota(jnp.int32, (CHUNK, CHUNK), 1)
    differ = jnp.bitwise_xor(query_row, key_lane)
    inner_levels = CHUNK.bit_length() - 1
    for copy in copies:
        copy.wait()

    def step(chunk, prefix):
        rows = chunk_rows(chunk)
        factors = pl.ds(pl.multiple_of(chunk * 8, 8), 8)
        total = chunk_sums(lower, rate_ref[:, rows])
        fall = jnp.exp(total[CHUNK // 2 - 1 : CHUNK // 2] - total).astype(BF16)
        carry = jnp.exp(-(total + prefix)).astype(BF16)
        b_mat = b_buf[rows, :]
        c_wide = (c_buf[rows, :].astype(F32) + c_other_ref[rows, :].astype(F32)).astype(BF16).astype(F32)
        lam = codes_ref[:, rows].astype(F32).T * scale_ref[...]
        gram = dot_turned(c_wide.astype(BF16), b_mat)

        def column(level):
            return jnp.broadcast_to(lam[:, level : level + 1], (CHUNK, CHUNK))

        weight = column(0)
        for level in range(1, inner_levels + 1):
            weight = jnp.where(differ >= 1 << (level - 1), column(level), weight)
        left = [jnp.where(key_lane <= query_row, gram * weight, 0.0).astype(BF16)]
        for level in range(local_levels):
            left.append((c_wide * column(inner_levels + 1 + level)).astype(BF16))
        left = jnp.concatenate(left, axis=1)
        for level in range(cross_levels):
            at = inner_levels + 1 + local_levels + level
            reads_ref[rows, level * STATES : (level + 1) * STATES] = (c_wide * column(at)).astype(BF16)
        b_turned = b_mat.astype(F32).T.astype(BF16)
        for lanes in lane_tiles(width):
            factor = rows_ref[factors, lanes]
            scaled = scaled_ref[rows, lanes]
            right = [scaled]
            for level in range(local_levels):
                right.append((held[level, :, lanes] * factor[2:3]).astype(BF16))
            summed = dot(left, jnp.concatenate(right, axis=0))
            local_ref[rows, lanes] = (summed * dot(fall, spread[:, lanes])).astype(BF16)
            carry_wide_ref[rows, lanes] = dot(carry, spread[:, lanes]).astype(BF16)
            fresh[:, lanes] = dot(b_turned, scaled) * factor[0:1]

        fade = rows_ref[factors, :][1:2]

        def put(level):
            if level == local_levels:
                return
            taken = jnp.bitwise_and(jnp.right_shift(chunk, level), 1) == 1

            @pl.when(jnp.logical_not(taken))
            def _():
                held[level] = fresh[...]
                for later in range(level + 1, local_levels):
                    held[later] = held[later] * fade

            @pl.when(taken)
            def _():
                fresh[...] = fresh[...] + held[level] * fade
                held[level] = jnp.zeros((STATES, width), F32)
                put(level + 1)

        put(0)
        return prefix + total[CHUNK - 1 :]

    lax.fori_loop(0, row_count // CHUNK, step, jnp.zeros((1, heads), F32))


def local_terms(b_far, c_far, c_other, codes_turned, scale, rate_turned, scaled, factor_rows, cross_levels):
    row_count, width = scaled.shape
    local_levels = (row_count // CHUNK).bit_length() - 1
    return pl.pallas_call(
        functools.partial(local_kernel, local_levels, cross_levels),
        in_specs=[HBM] * 2 + [VMEM] * 6,
        out_specs=[VMEM] * 3,
        out_shape=[
            shaped((row_count, width), BF16),
            shaped((row_count, cross_levels * STATES), BF16),
            shaped((row_count, width), BF16),
        ],
        scratch_shapes=[
            pltpu.VMEM((row_count, STATES), BF16),
            pltpu.VMEM((row_count, STATES), BF16),
            pltpu.VMEM((local_levels, STATES, width), F32),
            pltpu.VMEM((STATES, width), F32),
            pltpu.SemaphoreType.DMA((2,)),
        ],
        compiler_params=params(),
        cost_estimate=cost(3 * 10**9, 10**7),
        name="local_terms",
    )(
        *far_off(b_far, c_far),
        *near_by(c_other, codes_turned, scale, rate_turned, scaled, factor_rows),
    )


def finish_kernel(cross_levels, place_ref, hidden_far_ref, reads_ref, local_ref, carry_wide_ref, gain_ref, near_ref, *refs):
    received = refs[: cross_levels - 1]
    swapped = refs[cross_levels - 1 : 2 * (cross_levels - 1)]
    out_ref, carried, hidden_buf, result, in_sems, out_sems = refs[2 * (cross_levels - 1) :]
    row_count, width = local_ref.shape
    chunks = row_count // CHUNK
    step_chunks = 2 if chunks % 2 == 0 else 1
    steps = chunks // step_chunks

    def copy_in(at):
        rows = chunk_rows(at * step_chunks, step_chunks)
        return pltpu.make_async_copy(hidden_far_ref.at[rows], hidden_buf.at[rows], in_sems.at[at])

    def copy_out(at):
        rows = chunk_rows(at * step_chunks, step_chunks)
        return pltpu.make_async_copy(result.at[rows], out_ref.at[rows], out_sems.at[at])

    for at in range(steps):
        copy_in(at).start()
    is_low = place_ref[0] == 0
    before = jnp.ones((1, width), F32)
    for level in range(cross_levels):
        upper = place_ref[1 + level]
        if level == 0:
            message = near_ref[...]
        else:
            own, other = received[level - 1][...], swapped[level - 1][...]
            message = jnp.concatenate(
                [jnp.where(is_low, own, other), jnp.where(is_low, other, own)], axis=1
            )
        carried[level * STATES : (level + 1) * STATES, :] = (
            message[:STATES].astype(F32) * (before * upper.astype(F32))
        ).astype(BF16)
        before = jnp.where(upper == 1, before * fade_of(message), before)

    tiles = lane_tiles(width)
    tile = tiles[0].stop
    row = lax.broadcasted_iota(jnp.int32, (tile, tile), 0) // HEAD_VALUES
    lane = lax.broadcasted_iota(jnp.int32, (tile, tile), 1) // HEAD_VALUES
    mean_mat = jnp.where(row == lane, 1.0 / HEAD_VALUES, 0.0).astype(BF16)

    def step(at, token):
        rows = chunk_rows(at * step_chunks, step_chunks)
        copy_in(at).wait()
        reads = reads_ref[rows, :]
        for lanes in tiles:
            cross = dot(reads, carried[:, lanes])
            mixed = local_ref[rows, lanes].astype(F32) + cross * carry_wide_ref[rows, lanes].astype(F32)
            mean = dot((mixed * mixed).astype(BF16), mean_mat)
            normed = mixed * lax.rsqrt(mean + 1e-05) * gain_ref[:, lanes]
            result[rows, lanes] = (hidden_buf[rows, lanes].astype(F32) + normed).astype(BF16)
        copy_out(at).start()
        return token

    lax.fori_loop(0, steps, step, 0)
    for at in range(steps):
        copy_out(at).wait()


def finish(place, hidden_far, reads, local, carry_wide, gain, near, received, swapped):
    row_count, width = local.shape
    cross_levels = 1 + len(received)
    chunks = row_count // CHUNK
    return pl.pallas_call(
        functools.partial(finish_kernel, cross_levels),
        in_specs=[SMEM, HBM] + [VMEM] * (5 + 2 * len(received)),
        out_specs=HBM,
        out_shape=jax.ShapeDtypeStruct((row_count, width), BF16),
        scratch_shapes=[
            pltpu.VMEM((cross_levels * STATES, width), BF16),
            pltpu.VMEM((row_count, width), BF16),
            pltpu.VMEM((row_count, width), BF16),
            pltpu.SemaphoreType.DMA((chunks,)),
            pltpu.SemaphoreType.DMA((chunks,)),
        ],
        compiler_params=params(),
        cost_estimate=cost(2 * 10**9, 8 * 10**6),
        name="carried_and_norm",
    )(place, *far_off(hidden_far), *near_by(reads, local, carry_wide, gain, near, *received, *swapped))


def from_behind(x, axis, by):
    length = lax.axis_size(axis)
    return lax.ppermute(x, axis, [(i, i + by) for i in range(length - by)])


def partner(x, axis, distance):
    return lax.ppermute(x, axis, [(i, i ^ 1 << distance) for i in range(lax.axis_size(axis))])


def summed_over_heads(share):
    rounds = lax.axis_size("head").bit_length() - 1
    if rounds == 0:
        return share, jnp.zeros_like(share)
    total = share
    for distance in range(rounds - 1):
        total = (total.astype(F32) + partner(total, "head", distance).astype(F32)).astype(BF16)
    return total, partner(total, "head", rounds - 1)


def body(
    residual_in,
    query_rows,
    key_rows,
    value_rows,
    bc_weight,
    decay_rate,
    level_codes,
    level_scale,
    positions,
    ssm_gain,
):
    row_count, width = residual_in.shape
    half_width = width // 2
    shard_axes = ("seq", "fsdp")
    cross_levels = lax.axis_size(shard_axes).bit_length() - 1
    shard = lax.axis_index(shard_axes)
    half_index = lax.axis_index("fsdp")
    place = jnp.stack(
        [half_index] + [jnp.bitwise_and(jnp.right_shift(shard, level), 1) for level in range(cross_levels)]
    ).astype(jnp.int32)

    weights = (bc_weight, partner(bc_weight, "fsdp", 0))
    edges = from_behind(edge_rows(key_rows, value_rows), shard_axes, 1)
    pos_rows = positions.reshape(row_count // CHUNK, CHUNK)
    hidden, hidden_far, b_most, c_mat, weight, *firsts = attend_most(
        place, pos_rows, query_rows, key_rows, value_rows, residual_in, weights
    )
    b_most, b_most_other = summed_over_heads(b_most)
    hidden, hidden_far, c_mat, b_first, c_far = attend_first(
        pos_rows, edges, firsts, weight, hidden, hidden_far, c_mat
    )
    b_first, b_first_other = summed_over_heads(b_first)
    c_sent, c_other = summed_over_heads(c_mat)
    if lax.axis_size("head") > 2:
        c_far = c_sent
    rate_turned = decay_rate.T
    scaled, factor_rows = scale_hidden(rate_turned, hidden)
    state, b_far = block_state(b_first, b_most, b_first_other, b_most_other, scaled, factor_rows)

    near = partner(state, "fsdp", 0)
    joined = join(0, place, state, near, half_width)
    received = []
    for level in range(1, cross_levels):
        if level == cross_levels - 1:
            joined, c_other = lax.optimization_barrier((joined, c_other))
        received.append(partner(joined, "seq", level - 1))
        if level < cross_levels - 1:
            joined = join(level, place, joined, received[-1], half_width)
    local, reads, carry_wide = local_terms(
        b_far, c_far, c_other, level_codes.T, level_scale[None, :], rate_turned, scaled, factor_rows, cross_levels
    )
    received[-1], local = lax.optimization_barrier((received[-1], local))
    swapped = [partner(x, "fsdp", 0) for x in received]
    return finish(
        place, hidden_far, reads, local, carry_wide, ssm_gain[None, :], near, received, swapped
    )


def solution(mesh):
    in_specs = (
        P(("groups", "seq", "fsdp"), "head"),
        P(("groups", "seq", "fsdp"), "head"),
        P(("groups", "seq", "fsdp"), "head"),
        P(("groups", "seq", "fsdp"), "head"),
        P(("head", "fsdp"), None),
        P(("groups", "seq", "fsdp"), "head"),
        P(("groups", "seq", "fsdp"), None),
        P(),
        P(("groups", "seq", "fsdp")),
        P("head"),
    )
    out_specs = P(("groups", "seq", "fsdp"), "head")
    return jax.shard_map(body, mesh=mesh, in_specs=in_specs, out_specs=out_specs, check_vma=False)
```

```python
import functools
import math

import jax
import jax.numpy as jnp
from jax import lax
from jax.experimental import pallas as pl
from jax.experimental.pallas import tpu as pltpu
from jax.sharding import PartitionSpec as P

HEAD_DIM = 128
HEAD_VALUES = 64
STATES = 128
WINDOW = 128
CHUNK = 128
EXTRA = 16
OUT_PIECES = 4
VMEM_LIMIT = 24 * 1024 * 1024
HIDDEN = -1e30

F32 = jnp.float32
BF16 = jnp.bfloat16
VMEM = pl.BlockSpec(memory_space=pltpu.VMEM)
SMEM = pl.BlockSpec(memory_space=pltpu.SMEM)
HBM = pl.BlockSpec(memory_space=pltpu.HBM)


def params():
    return pltpu.CompilerParams(vmem_limit_bytes=VMEM_LIMIT)


def cost(flops, moved, transcendentals=0):
    return pl.CostEstimate(flops=flops, bytes_accessed=moved, transcendentals=transcendentals)


def shaped(shape, dtype):
    return pltpu.VMEM(shape, dtype)


def far_shaped(shape, dtype):
    return pltpu.HBM(shape, dtype)


def near_by(*arrays):
    return [pltpu.with_memory_space_constraint(x, pltpu.VMEM) for x in arrays]


def far_off(*arrays):
    return [pltpu.with_memory_space_constraint(x, pltpu.HBM) for x in arrays]


def dot(left, right):
    return jnp.dot(left, right, preferred_element_type=F32)


def dot_turned(left, right):
    return lax.dot_general(left, right, (((1,), (1,)), ((), ())), preferred_element_type=F32)


def chunk_rows(index, count=1):
    return pl.ds(pl.multiple_of(index * CHUNK, CHUNK), count * CHUNK)


def spread_matrix(heads, width):
    lane = lax.broadcasted_iota(jnp.int32, (heads, width), 1)
    start = lax.broadcasted_iota(jnp.int32, (heads, width), 0) * HEAD_VALUES
    return ((lane >= start) & (lane < start + HEAD_VALUES)).astype(F32).astype(BF16)


def lane_tiles(width):
    tile = min(width, 256)
    return [slice(at, at + tile) for at in range(0, width, tile)]


def split_rows(rows):
    high = rows.astype(BF16)
    return high, (rows - high.astype(F32)).astype(BF16)


def edge_kernel(key_ref, value_ref, edge_ref, sems):
    row_count = key_ref.shape[0]
    part = WINDOW // 4
    copies = [
        pltpu.make_async_copy(
            ref.at[pl.ds(row_count - WINDOW + piece * part, part)],
            edge_ref.at[pl.ds(at * WINDOW + piece * part, part)],
            sems.at[at, piece],
        )
        for at, ref in enumerate((key_ref, value_ref))
        for piece in range(4)
    ]
    for copy in copies:
        copy.start()
    for copy in copies:
        copy.wait()


def edge_rows(key_rows, value_rows):
    width = key_rows.shape[1]
    return pl.pallas_call(
        edge_kernel,
        in_specs=[HBM, HBM],
        out_specs=VMEM,
        out_shape=shaped((2 * WINDOW, width), BF16),
        scratch_shapes=[pltpu.SemaphoreType.DMA((2, 4))],
        compiler_params=params(),
        cost_estimate=cost(0, 2**20),
        name="edge_rows",
    )(*far_off(key_rows, value_rows))


def chunk_masks(doc_pos):
    key_row = lax.broadcasted_iota(jnp.int32, (WINDOW, WINDOW), 0)
    query_lane = lax.broadcasted_iota(jnp.int32, (WINDOW, WINDOW), 1)
    away = query_lane - key_row
    away = jnp.where(away < 0, away + WINDOW, away)
    bias = jnp.where(away <= doc_pos, 0.0, HIDDEN).astype(F32).T
    return bias


def attend_chunk(bias, query, key_before, key, value_before, value, residual):
    query_row = lax.broadcasted_iota(jnp.int32, (WINDOW, WINDOW), 0)
    key_lane = lax.broadcasted_iota(jnp.int32, (WINDOW, WINDOW), 1)
    current = key_lane <= query_row
    current_share = current.astype(F32).astype(BF16)
    before_share = (1.0 - current.astype(F32)).astype(BF16)
    ones = jnp.ones((2 * WINDOW, HEAD_DIM), BF16)
    factor = math.log2(math.e) / math.sqrt(HEAD_DIM)
    scores = dot_turned(query, jnp.concatenate([key_before, key], axis=0))
    merged = jnp.where(current, scores[:, WINDOW:], scores[:, :WINDOW]) + bias
    top = jnp.max(merged, axis=1, keepdims=True)
    weights = jnp.exp2((merged - top) * factor).astype(BF16)
    weights = jnp.concatenate([weights * before_share, weights * current_share], axis=1)
    values = jnp.concatenate([value_before, value], axis=0)
    summed = dot(weights, jnp.concatenate([values, ones], axis=1))
    attended = summed[:, :HEAD_DIM] / summed[:, HEAD_DIM:]
    return (residual.astype(F32) + attended).astype(BF16)


def attend_heads(bias, width, query, key_before, key, value_before, value, residual, hidden):
    def lanes_of(at, ref, rows):
        return ref[rows, at : at + HEAD_DIM]

    for at in range(0, width, HEAD_DIM):
        hidden[0][hidden[1], at : at + HEAD_DIM] = attend_chunk(
            bias,
            lanes_of(at, *query),
            lanes_of(at, *key_before),
            lanes_of(at, *key),
            lanes_of(at, *value_before),
            lanes_of(at, *value),
            lanes_of(at, *residual),
        )


def late_kernel(
    split,
    place_ref,
    pos_ref,
    query_ref,
    key_ref,
    value_ref,
    residual_ref,
    own_weight_ref,
    other_weight_ref,
    hidden_ref,
    c_ref,
    weight_ref,
    b_ref,
    key_early_ref,
    query_early_ref,
    value_early_ref,
    residual_early_ref,
    query_buf,
    value_buf,
    residual_buf,
    sems,
):
    row_count, width = query_ref.shape
    chunks = row_count // CHUNK
    half_width = width // 2
    arrays = (
        (value_ref, value_buf, value_early_ref),
        (query_ref, query_buf, query_early_ref),
        (residual_ref, residual_buf, residual_early_ref),
    )

    def copy(which, chunk):
        source, buffer, _ = arrays[which]
        return pltpu.make_async_copy(
            source.at[chunk_rows(chunk)], buffer.at[chunk_rows(chunk - split)], sems.at[which, chunk - split]
        )

    def copy_early(which, chunk):
        source, _, early = arrays[which]
        rows = chunk_rows(chunk)
        return pltpu.make_async_copy(source.at[rows], early.at[rows], sems.at[which, chunk + chunks - split])

    copy_early(0, split - 1).start()
    for chunk in range(split, chunks):
        for which in range(3):
            copy(which, chunk).start()
    for which in range(1, 3):
        copy_early(which, split - 1).start()
    for chunk in range(split - 1):
        for which in range(3):
            copy_early(which, chunk).start()
    is_low = place_ref[0] == 0
    own_weight, other_weight = own_weight_ref[...], other_weight_ref[...]
    weight_ref[:half_width, :] = jnp.where(is_low, own_weight, other_weight)
    weight_ref[half_width:, :] = jnp.where(is_low, other_weight, own_weight)
    key_early_ref[...] = key_ref[: split * CHUNK, :]

    def attend_one(chunk, value_before):
        for which in range(3):
            copy(which, chunk).wait()
        rows = chunk_rows(chunk - split)
        attend_heads(
            chunk_masks(pos_ref[pl.ds(chunk, 1), :]),
            width,
            (query_buf, rows),
            (key_ref, chunk_rows(chunk - 1)),
            (key_ref, chunk_rows(chunk)),
            value_before,
            (value_buf, rows),
            (residual_buf, rows),
            (hidden_ref, chunk_rows(chunk)),
        )

    copy_early(0, split - 1).wait()
    attend_one(split, (value_early_ref, chunk_rows(split - 1)))

    def step(chunk, token):
        attend_one(chunk, (value_buf, chunk_rows(chunk - split - 1)))
        return token

    lax.fori_loop(split + 1, chunks, step, 0)
    shared = dot(hidden_ref[split * CHUNK :, :], weight_ref[...])
    b_ref[...] = shared[:, :STATES].astype(BF16)
    c_ref[split * CHUNK :, :] = shared[:, STATES:].astype(BF16)
    for which in range(1, 3):
        copy_early(which, split - 1).wait()
    for chunk in range(split - 1):
        for which in range(3):
            copy_early(which, chunk).wait()


def attend_late(split, place, positions, query, key, value, residual, weights):
    row_count, width = query.shape
    chunks = row_count // CHUNK
    late = row_count - split * CHUNK
    return pl.pallas_call(
        functools.partial(late_kernel, split),
        in_specs=[SMEM, VMEM, HBM, VMEM, HBM, HBM, VMEM, VMEM],
        out_specs=[VMEM] * 8,
        out_shape=[
            shaped((row_count, width), BF16),
            shaped((row_count, STATES), BF16),
            shaped((width, 2 * STATES), BF16),
            shaped((late, STATES), BF16),
        ]
        + [shaped((split * CHUNK, width), BF16)] * 4,
        scratch_shapes=[pltpu.VMEM((late, width), BF16)] * 3 + [pltpu.SemaphoreType.DMA((3, chunks))],
        compiler_params=params(),
        cost_estimate=cost(6 * 10**9, 10**7),
        name="attention_late",
    )(
        place,
        *near_by(positions),
        *far_off(query),
        *near_by(key),
        *far_off(value, residual),
        *near_by(*weights),
    )


def early_kernel(
    split,
    pos_ref,
    edge_ref,
    key_ref,
    query_ref,
    value_ref,
    residual_ref,
    weight_ref,
    hidden_in_ref,
    c_in_ref,
    hidden_ref,
    c_ref,
    b_ref,
):
    width = query_ref.shape[1]
    early = split * CHUNK

    def attend_one(chunk, key_before, value_before):
        rows = chunk_rows(chunk)
        attend_heads(
            chunk_masks(pos_ref[pl.ds(chunk, 1), :]),
            width,
            (query_ref, rows),
            key_before,
            (key_ref, rows),
            value_before,
            (value_ref, rows),
            (residual_ref, rows),
            (hidden_ref, rows),
        )

    def step(chunk, token):
        rows = chunk_rows(chunk - 1)
        attend_one(chunk, (key_ref, rows), (value_ref, rows))
        return token

    lax.fori_loop(1, split, step, 0)
    attend_one(0, (edge_ref, slice(0, WINDOW)), (edge_ref, slice(WINDOW, 2 * WINDOW)))
    shared = dot(hidden_ref[:early, :], weight_ref[...])
    b_ref[...] = shared[:, :STATES].astype(BF16)
    c_ref[:early, :] = shared[:, STATES:].astype(BF16)


def attend_early(split, positions, edges, parts, weight, hidden, c_mat):
    return pl.pallas_call(
        functools.partial(early_kernel, split),
        in_specs=[VMEM] * 9,
        out_specs=[VMEM] * 3,
        out_shape=[
            shaped(hidden.shape, BF16),
            shaped(c_mat.shape, BF16),
            shaped((split * CHUNK, STATES), BF16),
        ],
        input_output_aliases={7: 0, 8: 1},
        compiler_params=params(),
        cost_estimate=cost(2 * 10**9, 2 * 10**6),
        name="attention_early",
    )(*near_by(positions, edges, *parts, weight, hidden, c_mat))


def lower_ones():
    row = lax.broadcasted_iota(jnp.int32, (CHUNK, CHUNK), 0)
    lane = lax.broadcasted_iota(jnp.int32, (CHUNK, CHUNK), 1)
    lower = (lane <= row).astype(F32).astype(BF16)
    return jnp.concatenate([lower] * 3, axis=1)


def chunk_sums(lower, rate):
    first = rate.astype(BF16)
    second, third = split_rows(rate - first.astype(F32))
    return dot_turned(lower, jnp.concatenate([first, second, third], axis=1))


def scale_kernel(
    rate_ref,
    hidden_ref,
    c_ref,
    scaled_ref,
    rows_ref,
    fall_ref,
    carry_ref,
    hidden_far_ref,
    c_far_ref,
    rise,
    fall,
    carry,
    logs,
    sems,
):
    heads, row_count = rate_ref.shape
    width = hidden_ref.shape[1]
    chunks = row_count // CHUNK
    copies = [pltpu.make_async_copy(c_ref, c_far_ref, sems.at[chunks])]
    for chunk in range(chunks):
        rows = pl.ds(chunk * CHUNK, CHUNK)
        copies.append(pltpu.make_async_copy(hidden_ref.at[rows], hidden_far_ref.at[rows], sems.at[chunk]))
    for copy in copies:
        copy.start()
    spread = spread_matrix(heads, width)
    lower = lower_ones()
    row_idx = lax.broadcasted_iota(jnp.int32, (8, heads), 0)
    prefix = jnp.zeros((1, heads), F32)
    for chunk in range(chunks):
        rows = slice(chunk * CHUNK, (chunk + 1) * CHUNK)
        total = chunk_sums(lower, rate_ref[:, rows])
        middle = total[CHUNK // 2 - 1 : CHUNK // 2]
        last = total[CHUNK - 1 :]
        rise[rows, :] = jnp.exp(total - middle).astype(BF16)
        fall[rows, :] = jnp.exp(middle - total).astype(BF16)
        carry[rows, :] = jnp.exp(-(total + prefix)).astype(BF16)
        logs[chunk * 8 : (chunk + 1) * 8, :] = jnp.where(
            row_idx == 0,
            middle - last,
            jnp.where(row_idx == 1, -last, jnp.where(row_idx == 2, -middle, 0.0)),
        )
        prefix = prefix + last
    high, low = split_rows(jnp.exp(logs[...]))
    for lanes in lane_tiles(width):
        wide = dot(rise[...], spread[:, lanes])
        scaled_ref[:, lanes] = (wide * hidden_ref[:, lanes].astype(F32)).astype(BF16)
        rows_ref[:, lanes] = dot(high, spread[:, lanes]) + dot(low, spread[:, lanes])
        fall_ref[:, lanes] = dot(fall[...], spread[:, lanes]).astype(BF16)
        carry_ref[:, lanes] = dot(carry[...], spread[:, lanes]).astype(BF16)
    for copy in copies:
        copy.wait()


def scale_hidden(rate_turned, hidden, c_mat):
    row_count, width = hidden.shape
    heads = rate_turned.shape[0]
    chunks = row_count // CHUNK
    return pl.pallas_call(
        scale_kernel,
        in_specs=[VMEM] * 3,
        out_specs=[VMEM] * 4 + [HBM] * 2,
        out_shape=[
            shaped((row_count, width), BF16),
            shaped((chunks * 8, width), F32),
            shaped((row_count, width), BF16),
            shaped((row_count, width), BF16),
            far_shaped(hidden.shape, BF16),
            far_shaped(c_mat.shape, BF16),
        ],
        scratch_shapes=[pltpu.VMEM((row_count, heads), BF16)] * 3
        + [pltpu.VMEM((chunks * 8, heads), F32), pltpu.SemaphoreType.DMA((chunks + 1,))],
        compiler_params=params(),
        cost_estimate=cost(10**9, 4 * 10**6),
        name="scale_hidden",
    )(*near_by(rate_turned, hidden, c_mat))


def state_kernel(
    local_levels,
    early_own_ref,
    early_other_ref,
    late_own_ref,
    late_other_ref,
    scaled_ref,
    rows_ref,
    state_ref,
    runs_ref,
    turned_far_ref,
    turned,
    sems,
):
    row_count, width = scaled_ref.shape
    chunks = row_count // CHUNK
    early = early_own_ref.shape[0]
    for chunk in range(chunks):
        at = chunk * CHUNK
        if at < early:
            span = slice(at, at + CHUNK)
            own, other = early_own_ref[span, :], early_other_ref[span, :]
        else:
            span = slice(at - early, at - early + CHUNK)
            own, other = late_own_ref[span, :], late_other_ref[span, :]
        turned[:, at : at + CHUNK] = (own.astype(F32) + other.astype(F32)).T.astype(BF16)
    turned_copy = pltpu.make_async_copy(turned, turned_far_ref, sems.at[0])
    turned_copy.start()
    tile = min(width, 256)

    def step(at, carry):
        lanes = pl.ds(pl.multiple_of(at * tile, tile), tile)
        held = {}
        fade = None
        for chunk in range(chunks):
            factor = rows_ref[chunk * 8 : (chunk + 1) * 8, lanes]
            fades = factor[1:2]
            for level in range(local_levels):
                start = (chunk * local_levels + level) * STATES
                if level in held:
                    run = (held[level] * factor[2:3]).astype(BF16)
                else:
                    run = jnp.zeros((STATES, tile), BF16)
                runs_ref[start : start + STATES, lanes] = run
            span = slice(chunk * CHUNK, (chunk + 1) * CHUNK)
            joined = dot(turned[:, span], scaled_ref[span, lanes]) * factor[0:1]
            held = {level: state * fades for level, state in held.items()}
            level = 0
            while level in held:
                joined = joined + held.pop(level)
                level += 1
            held[level] = joined
            fade = fades if fade is None else fade * fades
        state_ref[:STATES, lanes] = held[local_levels].astype(BF16)
        state_ref[STATES:, lanes] = fade_rows(fade)
        return carry

    lax.fori_loop(0, width // tile, step, 0)
    turned_copy.wait()


def fade_rows(fade):
    high, low = split_rows(fade)
    row = lax.broadcasted_iota(jnp.int32, (EXTRA, fade.shape[1]), 0)
    return jnp.where(row == 0, high.astype(F32), jnp.where(row == 1, low.astype(F32), 0.0)).astype(BF16)


def fade_of(message):
    return message[STATES : STATES + 1].astype(F32) + message[STATES + 1 : STATES + 2].astype(F32)


def block_state(early_own, early_other, late_own, late_other, scaled, factor_rows):
    row_count, width = scaled.shape
    chunks = row_count // CHUNK
    local_levels = chunks.bit_length() - 1
    return pl.pallas_call(
        functools.partial(state_kernel, local_levels),
        in_specs=[VMEM] * 6,
        out_specs=[VMEM, VMEM, HBM],
        out_shape=[
            shaped((STATES + EXTRA, width), BF16),
            shaped((chunks * local_levels * STATES, width), BF16),
            far_shaped((STATES, row_count), BF16),
        ],
        scratch_shapes=[pltpu.VMEM((STATES, row_count), BF16), pltpu.SemaphoreType.DMA((1,))],
        compiler_params=params(),
        cost_estimate=cost(3 * 10**8, 4 * 10**6),
        name="block_state",
    )(*near_by(early_own, early_other, late_own, late_other, scaled, factor_rows))


def join_kernel(level, place_ref, own_ref, other_ref, joined_ref):
    half_width = joined_ref.shape[1]
    own, other = own_ref[...], other_ref[...]
    if own.shape[1] != half_width:
        is_low = place_ref[0] == 0
        own = jnp.where(is_low, own[:, :half_width], own[:, half_width:])
        other = jnp.where(is_low, other[:, :half_width], other[:, half_width:])
    upper = place_ref[1 + level] == 1
    own_fade, other_fade = fade_of(own), fade_of(other)
    lower, higher = jnp.where(upper, other, own), jnp.where(upper, own, other)
    fade = jnp.where(upper, own_fade, other_fade)
    joined_ref[:STATES, :] = (lower[:STATES].astype(F32) * fade + higher[:STATES].astype(F32)).astype(BF16)
    joined_ref[STATES:, :] = fade_rows(own_fade * other_fade)


def join(level, place, own, other, half_width):
    return pl.pallas_call(
        functools.partial(join_kernel, level),
        in_specs=[SMEM, VMEM, VMEM],
        out_specs=VMEM,
        out_shape=shaped((own.shape[0], half_width), BF16),
        compiler_params=params(),
        cost_estimate=cost(10**6, 10**5),
        name="join_runs",
    )(place, *near_by(own, other))


def codes_kernel(codes_ref, wide_ref):
    codes = codes_ref[...].astype(F32).T.astype(BF16)
    levels = codes.shape[1]
    pair = 2 * CHUNK
    level_of = lax.broadcasted_iota(jnp.int32, (levels, pair), 0)
    lane = lax.broadcasted_iota(jnp.int32, (levels, pair), 1)
    for at in range(0, wide_ref.shape[1], pair):
        start = (level_of * CHUNK) - at
        pick = ((lane >= start) & (lane < start + CHUNK)).astype(F32).astype(BF16)
        wide_ref[:, at : at + pair] = dot(codes, pick).astype(BF16)


def widen_codes(codes_turned):
    levels, row_count = codes_turned.shape
    levels += levels % 2
    return pl.pallas_call(
        codes_kernel,
        in_specs=[VMEM],
        out_specs=VMEM,
        out_shape=shaped((row_count, levels * CHUNK), BF16),
        compiler_params=params(),
        cost_estimate=cost(10**9, 10**6),
        name="widen_codes",
    )(*near_by(codes_turned))


def weights_kernel(
    local_levels,
    cross_levels,
    scale_ref,
    turned_far_ref,
    c_far_ref,
    c_other_ref,
    codes_ref,
    left_ref,
    early_reads_ref,
    last_reads_ref,
    turned,
    c_buf,
    sems,
):
    row_count = c_other_ref.shape[0]
    copies = [
        pltpu.make_async_copy(turned_far_ref, turned, sems.at[0]),
        pltpu.make_async_copy(c_far_ref, c_buf, sems.at[1]),
    ]
    for copy in copies:
        copy.start()
    for copy in copies:
        copy.wait()

    query_row = lax.broadcasted_iota(jnp.int32, (CHUNK, CHUNK), 0)
    key_lane = lax.broadcasted_iota(jnp.int32, (CHUNK, CHUNK), 1)
    differ = jnp.bitwise_xor(query_row, key_lane)
    inner_levels = CHUNK.bit_length() - 1

    def step(chunk, token):
        rows = chunk_rows(chunk)

        def lam_of(level):
            return codes_ref[rows, level * CHUNK : (level + 1) * CHUNK].astype(F32) * scale_ref[level]

        c_wide = (c_buf[rows, :].astype(F32) + c_other_ref[rows, :].astype(F32)).astype(BF16).astype(F32)
        gram = dot(c_wide.astype(BF16), turned[:, rows])
        weight = lam_of(0)
        for level in range(1, inner_levels + 1):
            weight = jnp.where(differ >= 1 << (level - 1), lam_of(level), weight)
        left_ref[rows, :CHUNK] = jnp.where(key_lane <= query_row, gram * weight, 0.0).astype(BF16)
        for level in range(local_levels + cross_levels):
            read = (c_wide * lam_of(inner_levels + 1 + level)).astype(BF16)
            if level < local_levels:
                left_ref[rows, (level + 1) * CHUNK : (level + 2) * CHUNK] = read
            elif level < local_levels + cross_levels - 1:
                at = (level - local_levels) * STATES
                early_reads_ref[rows, at : at + STATES] = read
            else:
                last_reads_ref[rows, :] = read
        return token

    lax.fori_loop(0, row_count // CHUNK, step, 0)


def level_products(scale, turned_far, c_far, c_other, codes_wide, cross_levels):
    row_count = c_other.shape[0]
    local_levels = (row_count // CHUNK).bit_length() - 1
    return pl.pallas_call(
        functools.partial(weights_kernel, local_levels, cross_levels),
        in_specs=[SMEM] + [HBM] * 2 + [VMEM] * 2,
        out_specs=[VMEM] * 3,
        out_shape=[
            shaped((row_count, (1 + local_levels) * STATES), BF16),
            shaped((row_count, (cross_levels - 1) * STATES), BF16),
            shaped((row_count, STATES), BF16),
        ],
        scratch_shapes=[
            pltpu.VMEM((STATES, row_count), BF16),
            pltpu.VMEM((row_count, STATES), BF16),
            pltpu.SemaphoreType.DMA((2,)),
        ],
        compiler_params=params(),
        cost_estimate=cost(10**9, 10**7),
        name="level_products",
    )(scale, *far_off(turned_far, c_far), *near_by(c_other, codes_wide))


def carried_state(message, before, upper):
    return (message[:STATES].astype(F32) * (before * upper.astype(F32))).astype(BF16)


def local_kernel(
    local_levels,
    cross_levels,
    place_ref,
    hidden_far_ref,
    left_ref,
    early_reads_ref,
    scaled_ref,
    fall_ref,
    carry_ref,
    runs_ref,
    near_ref,
    *refs,
):
    received = refs[: cross_levels - 2]
    swapped = refs[cross_levels - 2 : 2 * (cross_levels - 2)]
    local_ref, hidden_ref, before_ref, carried, crossed, sems = refs[2 * (cross_levels - 2) :]
    row_count, width = scaled_ref.shape
    chunks = row_count // CHUNK
    copies = [
        pltpu.make_async_copy(
            hidden_far_ref.at[chunk_rows(chunk)], hidden_ref.at[chunk_rows(chunk)], sems.at[chunk]
        )
        for chunk in range(chunks)
    ]
    for copy in copies:
        copy.start()

    is_low = place_ref[0] == 0
    before = jnp.ones((1, width), F32)
    for level in range(cross_levels - 1):
        upper = place_ref[1 + level]
        if level == 0:
            message = near_ref[...]
        else:
            own, other = received[level - 1][...], swapped[level - 1][...]
            message = jnp.concatenate(
                [jnp.where(is_low, own, other), jnp.where(is_low, other, own)], axis=1
            )
        carried[level * STATES : (level + 1) * STATES, :] = carried_state(message, before, upper)
        before = jnp.where(upper == 1, before * fade_of(message), before)
    before_ref[...] = jnp.broadcast_to(before, before_ref.shape)
    tiles = lane_tiles(width)
    for lanes in tiles:
        crossed[:, lanes] = dot(early_reads_ref[...], carried[:, lanes]) * carry_ref[:, lanes].astype(F32)

    def step(chunk, token):
        rows = chunk_rows(chunk)
        left = left_ref[rows, :]
        run_rows = local_levels * STATES
        runs = pl.ds(pl.multiple_of(chunk * run_rows, run_rows), run_rows)
        for lanes in tiles:
            summed = dot(left, jnp.concatenate([scaled_ref[rows, lanes], runs_ref[runs, lanes]], axis=0))
            local_ref[rows, lanes] = (
                summed * fall_ref[rows, lanes].astype(F32) + crossed[rows, lanes]
            ).astype(BF16)
        return token

    lax.fori_loop(0, chunks, step, 0)
    for copy in copies:
        copy.wait()


def local_terms(place, hidden_far, left, early_reads, scaled, fall, carry, runs, near, received, swapped):
    row_count, width = scaled.shape
    local_levels = (row_count // CHUNK).bit_length() - 1
    cross_levels = 2 + len(received)
    return pl.pallas_call(
        functools.partial(local_kernel, local_levels, cross_levels),
        in_specs=[SMEM, HBM] + [VMEM] * (7 + 2 * len(received)),
        out_specs=[VMEM] * 3,
        out_shape=[shaped((row_count, width), BF16)] * 2 + [shaped((8, width), F32)],
        scratch_shapes=[
            pltpu.VMEM(((cross_levels - 1) * STATES, width), BF16),
            pltpu.VMEM((row_count, width), F32),
            pltpu.SemaphoreType.DMA((row_count // CHUNK,)),
        ],
        compiler_params=params(),
        cost_estimate=cost(3 * 10**9, 10**7),
        name="local_terms",
    )(
        place,
        *far_off(hidden_far),
        *near_by(left, early_reads, scaled, fall, carry, runs, near, *received, *swapped),
    )


def finish_kernel(
    swap, place_ref, message_ref, before_ref, hidden_ref, reads_ref, local_ref, carry_ref, gain_ref, *refs
):
    row_count, width = local_ref.shape
    half_width = width // 2
    own_start = place_ref[0] * half_width
    start = half_width - own_start if swap else own_start
    upper = place_ref[place_ref.shape[0] - 1]
    tile = min(half_width, 256)
    row = lax.broadcasted_iota(jnp.int32, (tile, tile), 0) // HEAD_VALUES
    lane = lax.broadcasted_iota(jnp.int32, (tile, tile), 1) // HEAD_VALUES
    mean_mat = jnp.where(row == lane, 1.0 / HEAD_VALUES, 0.0).astype(BF16)
    copies = []
    if swap:
        held_ref, out_ref, result, sems = refs
    else:
        (result,) = refs

    def copy_out(source, here, lanes, at):
        for piece in range(OUT_PIECES):
            rows = pl.ds(piece * (row_count // OUT_PIECES), row_count // OUT_PIECES)
            copies.append(
                pltpu.make_async_copy(source.at[rows, here], out_ref.at[rows, lanes], sems.at[at, piece])
            )
            copies[-1].start()

    if swap:
        lanes = pl.ds(pl.multiple_of(own_start, half_width), half_width)
        copy_out(held_ref, pl.ds(0, half_width), lanes, 0)
    for at in range(half_width // tile):
        lanes = pl.ds(pl.multiple_of(start + at * tile, tile), tile)
        here = slice(at * tile, (at + 1) * tile)
        carried = carried_state(message_ref[:, here], before_ref[0:1, lanes], upper)
        cross = dot(reads_ref[...], carried)
        mixed = local_ref[:, lanes].astype(F32) + cross * carry_ref[:, lanes].astype(F32)
        mean = dot((mixed * mixed).astype(BF16), mean_mat)
        normed = mixed * lax.rsqrt(mean + 1e-05) * gain_ref[:, lanes]
        result[:, here] = (hidden_ref[:, lanes].astype(F32) + normed).astype(BF16)
        if swap:
            copy_out(result, here, lanes, 1 + at)
    for copy in copies:
        copy.wait()


def finish(place, message, before, hidden, reads, local, carry, gain, held):
    row_count, width = local.shape
    half_width = width // 2
    swap = held is not None
    half_shape = (row_count, half_width)
    return pl.pallas_call(
        functools.partial(finish_kernel, swap),
        in_specs=[SMEM] + [VMEM] * (8 if swap else 7),
        out_specs=HBM if swap else VMEM,
        out_shape=far_shaped((row_count, width), BF16) if swap else shaped(half_shape, BF16),
        scratch_shapes=[
            pltpu.VMEM(half_shape, BF16),
            pltpu.SemaphoreType.DMA((1 + max(1, half_width // 256), OUT_PIECES)),
        ]
        if swap
        else [],
        compiler_params=params(),
        cost_estimate=cost(2 * 10**9, 8 * 10**6),
        name="carried_and_norm",
    )(place, *near_by(message, before, hidden, reads, local, carry, gain, *([held] if swap else [])))


def from_behind(x, axis, by):
    length = lax.axis_size(axis)
    return lax.ppermute(x, axis, [(i, i + by) for i in range(length - by)])


def partner(x, axis, distance):
    return lax.ppermute(x, axis, [(i, i ^ 1 << distance) for i in range(lax.axis_size(axis))])


def summed_over_heads(share):
    rounds = lax.axis_size("head").bit_length() - 1
    if rounds == 0:
        return share, jnp.zeros_like(share)
    total = share
    for distance in range(rounds - 1):
        total = (total.astype(F32) + partner(total, "head", distance).astype(F32)).astype(BF16)
    return total, partner(total, "head", rounds - 1)


def body(
    residual_in,
    query_rows,
    key_rows,
    value_rows,
    bc_weight,
    decay_rate,
    level_codes,
    level_scale,
    positions,
    ssm_gain,
):
    row_count, width = residual_in.shape
    half_width = width // 2
    shard_axes = ("seq", "fsdp")
    cross_levels = lax.axis_size(shard_axes).bit_length() - 1
    shard = lax.axis_index(shard_axes)
    half_index = lax.axis_index("fsdp")
    place = jnp.stack(
        [half_index] + [jnp.bitwise_and(jnp.right_shift(shard, level), 1) for level in range(cross_levels)]
    ).astype(jnp.int32)

    weights = (bc_weight, partner(bc_weight, "fsdp", 0))
    edges = from_behind(edge_rows(key_rows, value_rows), shard_axes, 1)
    pos_rows = positions.reshape(row_count // CHUNK, CHUNK)
    split = max(1, row_count // CHUNK // 4)
    hidden, c_mat, weight, b_late, *parts = attend_late(
        split, place, pos_rows, query_rows, key_rows, value_rows, residual_in, weights
    )
    late_own, late_other = summed_over_heads(b_late)
    hidden, c_mat, b_early = attend_early(split, pos_rows, edges, parts, weight, hidden, c_mat)
    early_own, early_other = summed_over_heads(b_early)
    scaled, factor_rows, fall, carry, hidden_far, c_far = scale_hidden(decay_rate.T, hidden, c_mat)
    c_mat, scaled = lax.optimization_barrier((c_mat, scaled))
    c_sent, c_other = summed_over_heads(c_mat)
    if lax.axis_size("head") > 2:
        c_far = c_sent
    state, runs, turned_far = block_state(
        early_own, early_other, late_own, late_other, scaled, factor_rows
    )
    near = partner(state, "fsdp", 0)
    joined = join(0, place, state, near, half_width)
    received, swapped = [], []
    for level in range(1, cross_levels):
        other = partner(joined, "seq", level - 1)
        if level == 1:
            codes_wide = widen_codes(level_codes.T)
            other, codes_wide = lax.optimization_barrier((other, codes_wide))
        received.append(other)
        if level < cross_levels - 1:
            joined = join(level, place, joined, other, half_width)
            swapped.append(partner(other, "fsdp", 0))
    left, early_reads, last_reads = level_products(
        level_scale, turned_far, c_far, c_other, codes_wide, cross_levels
    )
    local, hidden, before = local_terms(
        place, hidden_far, left, early_reads, scaled, fall, carry, runs, near, received[:-1], swapped
    )
    last, local = lax.optimization_barrier((received[-1], local))
    last_swapped = partner(last, "fsdp", 0)
    gain = ssm_gain[None, :]
    half = finish(place, last, before, hidden, last_reads, local, carry, gain, None)
    return finish(place, last_swapped, before, hidden, last_reads, local, carry, gain, half)


def solution(mesh):
    in_specs = (
        P(("groups", "seq", "fsdp"), "head"),
        P(("groups", "seq", "fsdp"), "head"),
        P(("groups", "seq", "fsdp"), "head"),
        P(("groups", "seq", "fsdp"), "head"),
        P(("head", "fsdp"), None),
        P(("groups", "seq", "fsdp"), "head"),
        P(("groups", "seq", "fsdp"), None),
        P(),
        P(("groups", "seq", "fsdp")),
        P("head"),
    )
    out_specs = P(("groups", "seq", "fsdp"), "head")
    return jax.shard_map(body, mesh=mesh, in_specs=in_specs, out_specs=out_specs, check_vma=False)
```

```python
import functools
import math

import jax
import jax.numpy as jnp
from jax import lax
from jax.experimental import pallas as pl
from jax.experimental.pallas import tpu as pltpu
from jax.sharding import PartitionSpec as P

HEAD_DIM = 128
HEAD_VALUES = 64
STATES = 128
WINDOW = 128
CHUNK = 128
EXTRA = 16
OUT_PIECES = 4
VMEM_LIMIT = 24 * 1024 * 1024
HIDDEN = -1e30

F32 = jnp.float32
BF16 = jnp.bfloat16
VMEM = pl.BlockSpec(memory_space=pltpu.VMEM)
SMEM = pl.BlockSpec(memory_space=pltpu.SMEM)
HBM = pl.BlockSpec(memory_space=pltpu.HBM)


def params():
    return pltpu.CompilerParams(vmem_limit_bytes=VMEM_LIMIT)


def cost(flops, moved, transcendentals=0):
    return pl.CostEstimate(flops=flops, bytes_accessed=moved, transcendentals=transcendentals)


def shaped(shape, dtype):
    return pltpu.VMEM(shape, dtype)


def far_shaped(shape, dtype):
    return pltpu.HBM(shape, dtype)


def near_by(*arrays):
    return [pltpu.with_memory_space_constraint(x, pltpu.VMEM) for x in arrays]


def far_off(*arrays):
    return [pltpu.with_memory_space_constraint(x, pltpu.HBM) for x in arrays]


def dot(left, right):
    return jnp.dot(left, right, preferred_element_type=F32)


def dot_turned(left, right):
    return lax.dot_general(left, right, (((1,), (1,)), ((), ())), preferred_element_type=F32)


def chunk_rows(index, count=1):
    return pl.ds(pl.multiple_of(index * CHUNK, CHUNK), count * CHUNK)


def spread_matrix(heads, width):
    lane = lax.broadcasted_iota(jnp.int32, (heads, width), 1)
    start = lax.broadcasted_iota(jnp.int32, (heads, width), 0) * HEAD_VALUES
    return ((lane >= start) & (lane < start + HEAD_VALUES)).astype(F32).astype(BF16)


def lane_tiles(width):
    tile = min(width, 256)
    return [slice(at, at + tile) for at in range(0, width, tile)]


def split_rows(rows):
    high = rows.astype(BF16)
    return high, (rows - high.astype(F32)).astype(BF16)


def half_index():
    return lax.axis_index("fsdp")


def shard_bit(level):
    shard = lax.axis_index("seq") * lax.axis_size("fsdp") + lax.axis_index("fsdp")
    return jnp.bitwise_and(jnp.right_shift(shard, level), 1)


def edge_kernel(key_ref, value_ref, edge_ref, sems):
    row_count = key_ref.shape[0]
    part = WINDOW // 4
    copies = [
        pltpu.make_async_copy(
            ref.at[pl.ds(row_count - WINDOW + piece * part, part)],
            edge_ref.at[pl.ds(at * WINDOW + piece * part, part)],
            sems.at[at, piece],
        )
        for at, ref in enumerate((key_ref, value_ref))
        for piece in range(4)
    ]
    for copy in copies:
        copy.start()
    for copy in copies:
        copy.wait()


def edge_rows(key_rows, value_rows):
    width = key_rows.shape[1]
    return pl.pallas_call(
        edge_kernel,
        in_specs=[HBM, HBM],
        out_specs=VMEM,
        out_shape=shaped((2 * WINDOW, width), BF16),
        scratch_shapes=[pltpu.SemaphoreType.DMA((2, 4))],
        compiler_params=params(),
        cost_estimate=cost(0, 2**20),
        name="edge_rows",
    )(*far_off(key_rows, value_rows))


def lower_ones():
    row = lax.broadcasted_iota(jnp.int32, (CHUNK, CHUNK), 0)
    lane = lax.broadcasted_iota(jnp.int32, (CHUNK, CHUNK), 1)
    lower = (lane <= row).astype(F32).astype(BF16)
    return jnp.concatenate([lower] * 3, axis=1)


def chunk_sums(lower, rate):
    first = rate.astype(BF16)
    second, third = split_rows(rate - first.astype(F32))
    return dot_turned(lower, jnp.concatenate([first, second, third], axis=1))


def fade_wide(rate_ref, fall, carry, fall_ref, carry_ref):
    heads, row_count = rate_ref.shape
    width = fall_ref.shape[1]
    lower = lower_ones()
    spread = spread_matrix(heads, width)
    prefix = jnp.zeros((1, heads), F32)
    for at in range(0, row_count, CHUNK):
        rows = slice(at, at + CHUNK)
        total = chunk_sums(lower, rate_ref[:, rows])
        fall[rows, :] = jnp.exp(total[CHUNK // 2 - 1 : CHUNK // 2] - total).astype(BF16)
        carry[rows, :] = jnp.exp(-(total + prefix)).astype(BF16)
        prefix = prefix + total[CHUNK - 1 :]
    for lanes in lane_tiles(width):
        fall_ref[:, lanes] = dot(fall[...], spread[:, lanes]).astype(BF16)
        carry_ref[:, lanes] = dot(carry[...], spread[:, lanes]).astype(BF16)


def chunk_masks(doc_pos):
    key_row = lax.broadcasted_iota(jnp.int32, (WINDOW, WINDOW), 0)
    query_lane = lax.broadcasted_iota(jnp.int32, (WINDOW, WINDOW), 1)
    away = query_lane - key_row
    away = jnp.where(away < 0, away + WINDOW, away)
    bias = jnp.where(away <= doc_pos, 0.0, HIDDEN).astype(F32).T
    return bias


def attend_chunk(bias, query, key_before, key, value_before, value, residual):
    query_row = lax.broadcasted_iota(jnp.int32, (WINDOW, WINDOW), 0)
    key_lane = lax.broadcasted_iota(jnp.int32, (WINDOW, WINDOW), 1)
    current = key_lane <= query_row
    current_share = current.astype(F32).astype(BF16)
    before_share = (1.0 - current.astype(F32)).astype(BF16)
    ones = jnp.ones((2 * WINDOW, HEAD_DIM), BF16)
    factor = math.log2(math.e) / math.sqrt(HEAD_DIM)
    scores = dot_turned(query, jnp.concatenate([key_before, key], axis=0))
    merged = jnp.where(current, scores[:, WINDOW:], scores[:, :WINDOW]) + bias
    top = jnp.max(merged, axis=1, keepdims=True)
    weights = jnp.exp2((merged - top) * factor).astype(BF16)
    weights = jnp.concatenate([weights * before_share, weights * current_share], axis=1)
    values = jnp.concatenate([value_before, value], axis=0)
    summed = dot(weights, jnp.concatenate([values, ones], axis=1))
    attended = summed[:, :HEAD_DIM] / summed[:, HEAD_DIM:]
    return (residual.astype(F32) + attended).astype(BF16)


def attend_heads(bias, width, query, key_before, key, value_before, value, residual, hidden):
    def lanes_of(at, ref, rows):
        return ref[rows, at : at + HEAD_DIM]

    for at in range(0, width, HEAD_DIM):
        hidden[0][hidden[1], at : at + HEAD_DIM] = attend_chunk(
            bias,
            lanes_of(at, *query),
            lanes_of(at, *key_before),
            lanes_of(at, *key),
            lanes_of(at, *value_before),
            lanes_of(at, *value),
            lanes_of(at, *residual),
        )


def late_kernel(
    split,
    pos_ref,
    rate_ref,
    query_ref,
    key_ref,
    value_ref,
    residual_ref,
    own_weight_ref,
    other_weight_ref,
    fall_ref,
    carry_ref,
    hidden_ref,
    c_ref,
    weight_ref,
    b_ref,
    key_early_ref,
    query_early_ref,
    value_early_ref,
    residual_early_ref,
    query_buf,
    value_buf,
    residual_buf,
    fall,
    carry,
    sems,
):
    row_count, width = query_ref.shape
    chunks = row_count // CHUNK
    half_width = width // 2
    arrays = (
        (value_ref, value_buf, value_early_ref),
        (query_ref, query_buf, query_early_ref),
        (residual_ref, residual_buf, residual_early_ref),
    )

    def copy(which, chunk):
        source, buffer, _ = arrays[which]
        return pltpu.make_async_copy(
            source.at[chunk_rows(chunk)], buffer.at[chunk_rows(chunk - split)], sems.at[which, chunk - split]
        )

    def copy_early(which, chunk):
        source, _, early = arrays[which]
        rows = chunk_rows(chunk)
        return pltpu.make_async_copy(source.at[rows], early.at[rows], sems.at[which, chunk + chunks - split])

    copy_early(0, split - 1).start()
    for chunk in range(split, chunks):
        for which in range(3):
            copy(which, chunk).start()
    for which in range(1, 3):
        copy_early(which, split - 1).start()
    for chunk in range(split - 1):
        for which in range(3):
            copy_early(which, chunk).start()
    is_low = half_index() == 0
    own_weight, other_weight = own_weight_ref[...], other_weight_ref[...]
    weight_ref[:half_width, :] = jnp.where(is_low, own_weight, other_weight)
    weight_ref[half_width:, :] = jnp.where(is_low, other_weight, own_weight)
    key_early_ref[...] = key_ref[: split * CHUNK, :]
    fade_wide(rate_ref, fall, carry, fall_ref, carry_ref)

    def attend_one(chunk, value_before):
        for which in range(3):
            copy(which, chunk).wait()
        rows = chunk_rows(chunk - split)
        attend_heads(
            chunk_masks(pos_ref[pl.ds(chunk, 1), :]),
            width,
            (query_buf, rows),
            (key_ref, chunk_rows(chunk - 1)),
            (key_ref, chunk_rows(chunk)),
            value_before,
            (value_buf, rows),
            (residual_buf, rows),
            (hidden_ref, chunk_rows(chunk)),
        )

    copy_early(0, split - 1).wait()
    attend_one(split, (value_early_ref, chunk_rows(split - 1)))

    def step(chunk, token):
        attend_one(chunk, (value_buf, chunk_rows(chunk - split - 1)))
        return token

    lax.fori_loop(split + 1, chunks, step, 0)
    shared = dot(hidden_ref[split * CHUNK :, :], weight_ref[...])
    b_ref[...] = shared[:, :STATES].astype(BF16)
    c_ref[split * CHUNK :, :] = shared[:, STATES:].astype(BF16)
    for which in range(1, 3):
        copy_early(which, split - 1).wait()
    for chunk in range(split - 1):
        for which in range(3):
            copy_early(which, chunk).wait()


def attend_late(split, positions, rate_turned, query, key, value, residual, weights):
    row_count, width = query.shape
    chunks = row_count // CHUNK
    late = row_count - split * CHUNK
    return pl.pallas_call(
        functools.partial(late_kernel, split),
        in_specs=[VMEM, VMEM, HBM, VMEM, HBM, HBM, VMEM, VMEM],
        out_specs=[VMEM] * 10,
        out_shape=[
            shaped((row_count, width), BF16),
            shaped((row_count, width), BF16),
            shaped((row_count, width), BF16),
            shaped((row_count, STATES), BF16),
            shaped((width, 2 * STATES), BF16),
            shaped((late, STATES), BF16),
        ]
        + [shaped((split * CHUNK, width), BF16)] * 4,
        scratch_shapes=[pltpu.VMEM((late, width), BF16)] * 3
        + [pltpu.VMEM((row_count, rate_turned.shape[0]), BF16)] * 2
        + [pltpu.SemaphoreType.DMA((3, chunks))],
        compiler_params=params(),
        cost_estimate=cost(6 * 10**9, 10**7),
        name="attention_late",
    )(
        *near_by(positions, rate_turned),
        *far_off(query),
        *near_by(key),
        *far_off(value, residual),
        *near_by(*weights),
    )


def early_kernel(
    split,
    pos_ref,
    edge_ref,
    key_ref,
    query_ref,
    value_ref,
    residual_ref,
    weight_ref,
    hidden_in_ref,
    c_in_ref,
    hidden_ref,
    c_ref,
    b_ref,
):
    width = query_ref.shape[1]
    early = split * CHUNK

    def attend_one(chunk, key_before, value_before):
        rows = chunk_rows(chunk)
        attend_heads(
            chunk_masks(pos_ref[pl.ds(chunk, 1), :]),
            width,
            (query_ref, rows),
            key_before,
            (key_ref, rows),
            value_before,
            (value_ref, rows),
            (residual_ref, rows),
            (hidden_ref, rows),
        )

    def step(chunk, token):
        rows = chunk_rows(chunk - 1)
        attend_one(chunk, (key_ref, rows), (value_ref, rows))
        return token

    lax.fori_loop(1, split, step, 0)
    attend_one(0, (edge_ref, slice(0, WINDOW)), (edge_ref, slice(WINDOW, 2 * WINDOW)))
    shared = dot(hidden_ref[:early, :], weight_ref[...])
    b_ref[...] = shared[:, :STATES].astype(BF16)
    c_ref[:early, :] = shared[:, STATES:].astype(BF16)


def attend_early(split, positions, edges, parts, weight, hidden, c_mat):
    return pl.pallas_call(
        functools.partial(early_kernel, split),
        in_specs=[VMEM] * 9,
        out_specs=[VMEM] * 3,
        out_shape=[
            shaped(hidden.shape, BF16),
            shaped(c_mat.shape, BF16),
            shaped((split * CHUNK, STATES), BF16),
        ],
        input_output_aliases={7: 0, 8: 1},
        compiler_params=params(),
        cost_estimate=cost(2 * 10**9, 2 * 10**6),
        name="attention_early",
    )(*near_by(positions, edges, *parts, weight, hidden, c_mat))


def scale_kernel(
    rate_ref,
    hidden_ref,
    c_ref,
    scaled_ref,
    rows_ref,
    hidden_far_ref,
    c_far_ref,
    rise,
    logs,
    sems,
):
    heads, row_count = rate_ref.shape
    width = hidden_ref.shape[1]
    chunks = row_count // CHUNK
    copies = [pltpu.make_async_copy(c_ref, c_far_ref, sems.at[chunks])]
    for chunk in range(chunks):
        rows = pl.ds(chunk * CHUNK, CHUNK)
        copies.append(pltpu.make_async_copy(hidden_ref.at[rows], hidden_far_ref.at[rows], sems.at[chunk]))
    for copy in copies:
        copy.start()
    spread = spread_matrix(heads, width)
    lower = lower_ones()
    row_idx = lax.broadcasted_iota(jnp.int32, (8, heads), 0)
    for chunk in range(chunks):
        rows = slice(chunk * CHUNK, (chunk + 1) * CHUNK)
        total = chunk_sums(lower, rate_ref[:, rows])
        middle = total[CHUNK // 2 - 1 : CHUNK // 2]
        last = total[CHUNK - 1 :]
        rise[rows, :] = jnp.exp(total - middle).astype(BF16)
        logs[chunk * 8 : (chunk + 1) * 8, :] = jnp.where(
            row_idx == 0,
            middle - last,
            jnp.where(row_idx == 1, -last, jnp.where(row_idx == 2, -middle, 0.0)),
        )
    high, low = split_rows(jnp.exp(logs[...]))
    for lanes in lane_tiles(width):
        wide = dot(rise[...], spread[:, lanes])
        scaled_ref[:, lanes] = (wide * hidden_ref[:, lanes].astype(F32)).astype(BF16)
        rows_ref[:, lanes] = dot(high, spread[:, lanes]) + dot(low, spread[:, lanes])
    for copy in copies:
        copy.wait()


def scale_hidden(rate_turned, hidden, c_mat):
    row_count, width = hidden.shape
    heads = rate_turned.shape[0]
    chunks = row_count // CHUNK
    return pl.pallas_call(
        scale_kernel,
        in_specs=[VMEM] * 3,
        out_specs=[VMEM] * 2 + [HBM] * 2,
        out_shape=[
            shaped((row_count, width), BF16),
            shaped((chunks * 8, width), F32),
            far_shaped(hidden.shape, BF16),
            far_shaped(c_mat.shape, BF16),
        ],
        scratch_shapes=[pltpu.VMEM((row_count, heads), BF16)]
        + [pltpu.VMEM((chunks * 8, heads), F32), pltpu.SemaphoreType.DMA((chunks + 1,))],
        compiler_params=params(),
        cost_estimate=cost(10**9, 4 * 10**6),
        name="scale_hidden",
    )(*near_by(rate_turned, hidden, c_mat))


def state_kernel(
    early_own_ref,
    early_other_ref,
    late_own_ref,
    late_other_ref,
    scaled_ref,
    rows_ref,
    state_ref,
    turned_far_ref,
    turned,
    sems,
):
    row_count, width = scaled_ref.shape
    chunks = row_count // CHUNK
    early = early_own_ref.shape[0]
    for chunk in range(chunks):
        at = chunk * CHUNK
        if at < early:
            span = slice(at, at + CHUNK)
            own, other = early_own_ref[span, :], early_other_ref[span, :]
        else:
            span = slice(at - early, at - early + CHUNK)
            own, other = late_own_ref[span, :], late_other_ref[span, :]
        turned[:, at : at + CHUNK] = (own.astype(F32) + other.astype(F32)).T.astype(BF16)
    turned_copy = pltpu.make_async_copy(turned, turned_far_ref, sems.at[0])
    turned_copy.start()
    tile = min(width, 256)

    def step(at, carry):
        lanes = pl.ds(pl.multiple_of(at * tile, tile), tile)
        total = fade = None
        for chunk in range(chunks):
            span = slice(chunk * CHUNK, (chunk + 1) * CHUNK)
            factor = rows_ref[chunk * 8 : (chunk + 1) * 8, lanes]
            added = dot(turned[:, span], scaled_ref[span, lanes]) * factor[0:1]
            total = added if total is None else total * factor[1:2] + added
            fade = factor[1:2] if fade is None else fade * factor[1:2]
        state_ref[:STATES, lanes] = total.astype(BF16)
        state_ref[STATES:, lanes] = fade_rows(fade)
        return carry

    lax.fori_loop(0, width // tile, step, 0)
    turned_copy.wait()


def fade_rows(fade):
    high, low = split_rows(fade)
    row = lax.broadcasted_iota(jnp.int32, (EXTRA, fade.shape[1]), 0)
    return jnp.where(row == 0, high.astype(F32), jnp.where(row == 1, low.astype(F32), 0.0)).astype(BF16)


def fade_of(message):
    return message[STATES : STATES + 1].astype(F32) + message[STATES + 1 : STATES + 2].astype(F32)


def block_state(early_own, early_other, late_own, late_other, scaled, factor_rows):
    row_count, width = scaled.shape
    return pl.pallas_call(
        state_kernel,
        in_specs=[VMEM] * 6,
        out_specs=[VMEM, HBM],
        out_shape=[shaped((STATES + EXTRA, width), BF16), far_shaped((STATES, row_count), BF16)],
        scratch_shapes=[pltpu.VMEM((STATES, row_count), BF16), pltpu.SemaphoreType.DMA((1,))],
        compiler_params=params(),
        cost_estimate=cost(3 * 10**8, 4 * 10**6),
        name="block_state",
    )(*near_by(early_own, early_other, late_own, late_other, scaled, factor_rows))


def join_kernel(level, own_ref, other_ref, joined_ref):
    half_width = joined_ref.shape[1]
    own, other = own_ref[...], other_ref[...]
    if own.shape[1] != half_width:
        is_low = half_index() == 0
        own = jnp.where(is_low, own[:, :half_width], own[:, half_width:])
        other = jnp.where(is_low, other[:, :half_width], other[:, half_width:])
    upper = shard_bit(level) == 1
    own_fade, other_fade = fade_of(own), fade_of(other)
    lower, higher = jnp.where(upper, other, own), jnp.where(upper, own, other)
    fade = jnp.where(upper, own_fade, other_fade)
    joined_ref[:STATES, :] = (lower[:STATES].astype(F32) * fade + higher[:STATES].astype(F32)).astype(BF16)
    if joined_ref.shape[0] > STATES:
        joined_ref[STATES:, :] = fade_rows(own_fade * other_fade)


def join(level, own, other, half_width, last):
    return pl.pallas_call(
        functools.partial(join_kernel, level),
        in_specs=[VMEM, VMEM],
        out_specs=VMEM,
        out_shape=shaped((STATES if last else STATES + EXTRA, half_width), BF16),
        compiler_params=params(),
        cost_estimate=cost(10**6, 10**5),
        name="join_runs",
    )(*near_by(own, other))


def runs_kernel(local_levels, turned_far_ref, codes_ref, scaled_ref, rows_ref, wide_ref, runs_ref, turned, sems):
    row_count, width = scaled_ref.shape
    chunks = row_count // CHUNK
    turned_copy = pltpu.make_async_copy(turned_far_ref, turned, sems.at[0])
    turned_copy.start()
    codes = codes_ref[...].astype(F32).T.astype(BF16)
    levels = codes.shape[1]
    pair = 2 * CHUNK
    level_of = lax.broadcasted_iota(jnp.int32, (levels, pair), 0)
    lane = lax.broadcasted_iota(jnp.int32, (levels, pair), 1)
    for at in range(0, wide_ref.shape[1], pair):
        start = (level_of * CHUNK) - at
        pick = ((lane >= start) & (lane < start + CHUNK)).astype(F32).astype(BF16)
        wide_ref[:, at : at + pair] = dot(codes, pick).astype(BF16)
    turned_copy.wait()
    tile = min(width, 256)

    def step(at, token):
        lanes = pl.ds(pl.multiple_of(at * tile, tile), tile)
        held = {}
        for chunk in range(chunks):
            factor = rows_ref[chunk * 8 : (chunk + 1) * 8, lanes]
            for level in range(local_levels):
                start = (chunk * local_levels + level) * STATES
                if level in held:
                    run = (held[level] * factor[2:3]).astype(BF16)
                else:
                    run = jnp.zeros((STATES, tile), BF16)
                runs_ref[start : start + STATES, lanes] = run
            if chunk == chunks - 1:
                break
            span = slice(chunk * CHUNK, (chunk + 1) * CHUNK)
            joined = dot(turned[:, span], scaled_ref[span, lanes]) * factor[0:1]
            held = {level: state * factor[1:2] for level, state in held.items()}
            level = 0
            while level in held:
                joined = joined + held.pop(level)
                level += 1
            held[level] = joined
        return token

    lax.fori_loop(0, width // tile, step, 0)


def codes_and_runs(turned_far, codes_turned, scaled, factor_rows):
    row_count, width = scaled.shape
    levels = codes_turned.shape[0]
    levels += levels % 2
    chunks = row_count // CHUNK
    local_levels = chunks.bit_length() - 1
    return pl.pallas_call(
        functools.partial(runs_kernel, local_levels),
        in_specs=[HBM] + [VMEM] * 3,
        out_specs=[VMEM] * 2,
        out_shape=[
            shaped((row_count, levels * CHUNK), BF16),
            shaped((chunks * local_levels * STATES, width), BF16),
        ],
        scratch_shapes=[pltpu.VMEM((STATES, row_count), BF16), pltpu.SemaphoreType.DMA((1,))],
        compiler_params=params(),
        cost_estimate=cost(10**9, 10**7),
        name="codes_and_runs",
    )(*far_off(turned_far), *near_by(codes_turned, scaled, factor_rows))


def weights_kernel(
    local_levels,
    cross_levels,
    scale_ref,
    turned_far_ref,
    c_far_ref,
    c_other_ref,
    codes_ref,
    left_ref,
    early_reads_ref,
    last_reads_ref,
    turned,
    c_buf,
    sems,
):
    row_count = c_other_ref.shape[0]
    copies = [
        pltpu.make_async_copy(turned_far_ref, turned, sems.at[0]),
        pltpu.make_async_copy(c_far_ref, c_buf, sems.at[1]),
    ]
    for copy in copies:
        copy.start()
    for copy in copies:
        copy.wait()

    query_row = lax.broadcasted_iota(jnp.int32, (CHUNK, CHUNK), 0)
    key_lane = lax.broadcasted_iota(jnp.int32, (CHUNK, CHUNK), 1)
    differ = jnp.bitwise_xor(query_row, key_lane)
    inner_levels = CHUNK.bit_length() - 1

    def step(chunk, token):
        rows = chunk_rows(chunk)

        def lam_of(level):
            return codes_ref[rows, level * CHUNK : (level + 1) * CHUNK].astype(F32) * scale_ref[level]

        c_wide = (c_buf[rows, :].astype(F32) + c_other_ref[rows, :].astype(F32)).astype(BF16).astype(F32)
        gram = dot(c_wide.astype(BF16), turned[:, rows])
        weight = lam_of(0)
        for level in range(1, inner_levels + 1):
            weight = jnp.where(differ >= 1 << (level - 1), lam_of(level), weight)
        left_ref[rows, :CHUNK] = jnp.where(key_lane <= query_row, gram * weight, 0.0).astype(BF16)
        for level in range(local_levels + cross_levels):
            read = (c_wide * lam_of(inner_levels + 1 + level)).astype(BF16)
            if level < local_levels:
                left_ref[rows, (level + 1) * CHUNK : (level + 2) * CHUNK] = read
            elif level < local_levels + cross_levels - 1:
                at = (level - local_levels) * STATES
                early_reads_ref[rows, at : at + STATES] = read
            else:
                last_reads_ref[rows, :] = read
        return token

    lax.fori_loop(0, row_count // CHUNK, step, 0)


def level_products(scale, turned_far, c_far, c_other, codes_wide, cross_levels):
    row_count = c_other.shape[0]
    local_levels = (row_count // CHUNK).bit_length() - 1
    return pl.pallas_call(
        functools.partial(weights_kernel, local_levels, cross_levels),
        in_specs=[SMEM] + [HBM] * 2 + [VMEM] * 2,
        out_specs=[VMEM] * 3,
        out_shape=[
            shaped((row_count, (1 + local_levels) * STATES), BF16),
            shaped((row_count, (cross_levels - 1) * STATES), BF16),
            shaped((row_count, STATES), BF16),
        ],
        scratch_shapes=[
            pltpu.VMEM((STATES, row_count), BF16),
            pltpu.VMEM((row_count, STATES), BF16),
            pltpu.SemaphoreType.DMA((2,)),
        ],
        compiler_params=params(),
        cost_estimate=cost(10**9, 10**7),
        name="level_products",
    )(scale, *far_off(turned_far, c_far), *near_by(c_other, codes_wide))


def carried_state(message, before, upper):
    return (message[:STATES].astype(F32) * (before * upper.astype(F32))).astype(BF16)


def local_kernel(
    local_levels,
    cross_levels,
    hidden_far_ref,
    left_ref,
    early_reads_ref,
    scaled_ref,
    fall_ref,
    carry_ref,
    runs_ref,
    near_ref,
    *refs,
):
    received = refs[: cross_levels - 2]
    swapped = refs[cross_levels - 2 : 2 * (cross_levels - 2)]
    local_ref, hidden_ref, before_ref, carried, crossed, sems = refs[2 * (cross_levels - 2) :]
    row_count, width = scaled_ref.shape
    chunks = row_count // CHUNK
    copies = [
        pltpu.make_async_copy(
            hidden_far_ref.at[chunk_rows(chunk)], hidden_ref.at[chunk_rows(chunk)], sems.at[chunk]
        )
        for chunk in range(chunks)
    ]
    for copy in copies:
        copy.start()

    is_low = half_index() == 0
    before = jnp.ones((1, width), F32)
    for level in range(cross_levels - 1):
        upper = shard_bit(level)
        if level == 0:
            message = near_ref[...]
        else:
            own, other = received[level - 1][...], swapped[level - 1][...]
            message = jnp.concatenate(
                [jnp.where(is_low, own, other), jnp.where(is_low, other, own)], axis=1
            )
        carried[level * STATES : (level + 1) * STATES, :] = carried_state(message, before, upper)
        before = jnp.where(upper == 1, before * fade_of(message), before)
    before_ref[...] = jnp.broadcast_to(before, before_ref.shape)
    tiles = lane_tiles(width)
    for lanes in tiles:
        crossed[:, lanes] = dot(early_reads_ref[...], carried[:, lanes]) * carry_ref[:, lanes].astype(F32)

    def step(chunk, token):
        rows = chunk_rows(chunk)
        left = left_ref[rows, :]
        run_rows = local_levels * STATES
        runs = pl.ds(pl.multiple_of(chunk * run_rows, run_rows), run_rows)
        for lanes in tiles:
            summed = dot(left, jnp.concatenate([scaled_ref[rows, lanes], runs_ref[runs, lanes]], axis=0))
            local_ref[rows, lanes] = (
                summed * fall_ref[rows, lanes].astype(F32) + crossed[rows, lanes]
            ).astype(BF16)
        return token

    lax.fori_loop(0, chunks, step, 0)
    for copy in copies:
        copy.wait()


def local_terms(hidden_far, left, early_reads, scaled, fall, carry, runs, near, received, swapped):
    row_count, width = scaled.shape
    local_levels = (row_count // CHUNK).bit_length() - 1
    cross_levels = 2 + len(received)
    return pl.pallas_call(
        functools.partial(local_kernel, local_levels, cross_levels),
        in_specs=[HBM] + [VMEM] * (7 + 2 * len(received)),
        out_specs=[VMEM] * 3,
        out_shape=[shaped((row_count, width), BF16)] * 2 + [shaped((8, width), F32)],
        scratch_shapes=[
            pltpu.VMEM(((cross_levels - 1) * STATES, width), BF16),
            pltpu.VMEM((row_count, width), F32),
            pltpu.SemaphoreType.DMA((row_count // CHUNK,)),
        ],
        compiler_params=params(),
        cost_estimate=cost(3 * 10**9, 10**7),
        name="local_terms",
    )(
        *far_off(hidden_far),
        *near_by(left, early_reads, scaled, fall, carry, runs, near, *received, *swapped),
    )


def finish_kernel(
    swap, cross_levels, message_ref, before_ref, hidden_ref, reads_ref, local_ref, carry_ref, gain_ref, *refs
):
    row_count, width = local_ref.shape
    half_width = width // 2
    own_start = half_index() * half_width
    start = half_width - own_start if swap else own_start
    upper = shard_bit(cross_levels - 1)
    tile = min(half_width, 256)
    row = lax.broadcasted_iota(jnp.int32, (tile, tile), 0) // HEAD_VALUES
    lane = lax.broadcasted_iota(jnp.int32, (tile, tile), 1) // HEAD_VALUES
    mean_mat = jnp.where(row == lane, 1.0 / HEAD_VALUES, 0.0).astype(BF16)
    copies = []
    if swap:
        held_ref, out_ref, result, sems = refs
    else:
        (result,) = refs

    def copy_out(source, here, lanes, at):
        for piece in range(OUT_PIECES):
            rows = pl.ds(piece * (row_count // OUT_PIECES), row_count // OUT_PIECES)
            copies.append(
                pltpu.make_async_copy(source.at[rows, here], out_ref.at[rows, lanes], sems.at[at, piece])
            )
            copies[-1].start()

    if swap:
        lanes = pl.ds(pl.multiple_of(own_start, half_width), half_width)
        copy_out(held_ref, pl.ds(0, half_width), lanes, 0)
    for at in range(half_width // tile):
        lanes = pl.ds(pl.multiple_of(start + at * tile, tile), tile)
        here = slice(at * tile, (at + 1) * tile)
        carried = carried_state(message_ref[:, here], before_ref[0:1, lanes], upper)
        cross = dot(reads_ref[...], carried).astype(BF16)
        mixed = local_ref[:, lanes] + cross * carry_ref[:, lanes]
        mean = dot(mixed * mixed, mean_mat)
        normed = mixed * lax.rsqrt(mean + 1e-05).astype(BF16) * gain_ref[:, lanes].astype(BF16)
        result[:, here] = hidden_ref[:, lanes] + normed
        if swap:
            copy_out(result, here, lanes, 1 + at)
    for copy in copies:
        copy.wait()


def finish(cross_levels, message, before, hidden, reads, local, carry, gain, held):
    row_count, width = local.shape
    half_width = width // 2
    swap = held is not None
    half_shape = (row_count, half_width)
    return pl.pallas_call(
        functools.partial(finish_kernel, swap, cross_levels),
        in_specs=[VMEM] * (8 if swap else 7),
        out_specs=HBM if swap else VMEM,
        out_shape=far_shaped((row_count, width), BF16) if swap else shaped(half_shape, BF16),
        scratch_shapes=[
            pltpu.VMEM(half_shape, BF16),
            pltpu.SemaphoreType.DMA((1 + max(1, half_width // 256), OUT_PIECES)),
        ]
        if swap
        else [],
        compiler_params=params(),
        cost_estimate=cost(2 * 10**9, 8 * 10**6),
        name="carried_and_norm",
    )(*near_by(message, before, hidden, reads, local, carry, gain, *([held] if swap else [])))


def from_behind(x, axis, by):
    length = lax.axis_size(axis)
    return lax.ppermute(x, axis, [(i, i + by) for i in range(length - by)])


def partner(x, axis, distance):
    return lax.ppermute(x, axis, [(i, i ^ 1 << distance) for i in range(lax.axis_size(axis))])


def summed_over_heads(share):
    rounds = lax.axis_size("head").bit_length() - 1
    if rounds == 0:
        return share, jnp.zeros_like(share)
    total = share
    for distance in range(rounds - 1):
        total = (total.astype(F32) + partner(total, "head", distance).astype(F32)).astype(BF16)
    return total, partner(total, "head", rounds - 1)


def body(
    residual_in,
    query_rows,
    key_rows,
    value_rows,
    bc_weight,
    decay_rate,
    level_codes,
    level_scale,
    positions,
    ssm_gain,
):
    row_count, width = residual_in.shape
    half_width = width // 2
    shard_axes = ("seq", "fsdp")
    cross_levels = lax.axis_size(shard_axes).bit_length() - 1

    weights = (bc_weight, partner(bc_weight, "fsdp", 0))
    edges = from_behind(edge_rows(key_rows, value_rows), shard_axes, 1)
    pos_rows = positions.reshape(row_count // CHUNK, CHUNK)
    split = max(1, row_count // CHUNK // 4)
    rate_turned = decay_rate.T
    fall, carry, hidden, c_mat, weight, b_late, *parts = attend_late(
        split, pos_rows, rate_turned, query_rows, key_rows, value_rows, residual_in, weights
    )
    late_own, late_other = summed_over_heads(b_late)
    hidden, c_mat, b_early = attend_early(split, pos_rows, edges, parts, weight, hidden, c_mat)
    early_own, early_other = summed_over_heads(b_early)
    scaled, factor_rows, hidden_far, c_far = scale_hidden(rate_turned, hidden, c_mat)
    c_mat, scaled = lax.optimization_barrier((c_mat, scaled))
    c_sent, c_other = summed_over_heads(c_mat)
    if lax.axis_size("head") > 2:
        c_far = c_sent
    state, turned_far = block_state(
        early_own, early_other, late_own, late_other, scaled, factor_rows
    )
    near = partner(state, "fsdp", 0)
    joined = join(0, state, near, half_width, cross_levels == 2)
    received, swapped = [], []
    for level in range(1, cross_levels):
        other = partner(joined, "seq", level - 1)
        if level == 1:
            codes_wide, runs = codes_and_runs(turned_far, level_codes.T, scaled, factor_rows)
            other, codes_wide = lax.optimization_barrier((other, codes_wide))
        received.append(other)
        if level < cross_levels - 1:
            joined = join(level, joined, other, half_width, level == cross_levels - 2)
            swapped.append(partner(other, "fsdp", 0))
    left, early_reads, last_reads = level_products(
        level_scale, turned_far, c_far, c_other, codes_wide, cross_levels
    )
    local, hidden, before = local_terms(
        hidden_far, left, early_reads, scaled, fall, carry, runs, near, received[:-1], swapped
    )
    last, local = lax.optimization_barrier((received[-1], local))
    last_swapped = partner(last, "fsdp", 0)
    gain = ssm_gain[None, :]
    half = finish(cross_levels, last, before, hidden, last_reads, local, carry, gain, None)
    return finish(cross_levels, last_swapped, before, hidden, last_reads, local, carry, gain, half)


def solution(mesh):
    in_specs = (
        P(("groups", "seq", "fsdp"), "head"),
        P(("groups", "seq", "fsdp"), "head"),
        P(("groups", "seq", "fsdp"), "head"),
        P(("groups", "seq", "fsdp"), "head"),
        P(("head", "fsdp"), None),
        P(("groups", "seq", "fsdp"), "head"),
        P(("groups", "seq", "fsdp"), None),
        P(),
        P(("groups", "seq", "fsdp")),
        P("head"),
    )
    out_specs = P(("groups", "seq", "fsdp"), "head")
    return jax.shard_map(body, mesh=mesh, in_specs=in_specs, out_specs=out_specs, check_vma=False)
```

```python
import functools
import math

import jax
import jax.numpy as jnp
from jax import lax
from jax.experimental import pallas as pl
from jax.experimental.pallas import tpu as pltpu
from jax.sharding import PartitionSpec as P

HEAD_DIM = 128
HEAD_VALUES = 64
STATES = 128
WINDOW = 128
CHUNK = 128
EXTRA = 16
OUT_PIECES = 4
VMEM_LIMIT = 24 * 1024 * 1024
HIDDEN = -1e30

F32 = jnp.float32
BF16 = jnp.bfloat16
VMEM = pl.BlockSpec(memory_space=pltpu.VMEM)
SMEM = pl.BlockSpec(memory_space=pltpu.SMEM)
HBM = pl.BlockSpec(memory_space=pltpu.HBM)


def params():
    return pltpu.CompilerParams(vmem_limit_bytes=VMEM_LIMIT)


def cost(flops, moved, transcendentals=0):
    return pl.CostEstimate(flops=flops, bytes_accessed=moved, transcendentals=transcendentals)


def shaped(shape, dtype):
    return pltpu.VMEM(shape, dtype)


def far_shaped(shape, dtype):
    return pltpu.HBM(shape, dtype)


def near_by(*arrays):
    return [pltpu.with_memory_space_constraint(x, pltpu.VMEM) for x in arrays]


def far_off(*arrays):
    return [pltpu.with_memory_space_constraint(x, pltpu.HBM) for x in arrays]


def dot(left, right):
    return jnp.dot(left, right, preferred_element_type=F32)


def dot_turned(left, right):
    return lax.dot_general(left, right, (((1,), (1,)), ((), ())), preferred_element_type=F32)


def chunk_rows(index, count=1):
    return pl.ds(pl.multiple_of(index * CHUNK, CHUNK), count * CHUNK)


def spread_matrix(heads, width):
    lane = lax.broadcasted_iota(jnp.int32, (heads, width), 1)
    start = lax.broadcasted_iota(jnp.int32, (heads, width), 0) * HEAD_VALUES
    return ((lane >= start) & (lane < start + HEAD_VALUES)).astype(F32).astype(BF16)


def lane_tiles(width):
    tile = min(width, 256)
    return [slice(at, at + tile) for at in range(0, width, tile)]


def split_rows(rows):
    high = rows.astype(BF16)
    return high, (rows - high.astype(F32)).astype(BF16)


def half_index():
    return lax.axis_index("fsdp")


def shard_bit(level):
    shard = lax.axis_index("seq") * lax.axis_size("fsdp") + lax.axis_index("fsdp")
    return jnp.bitwise_and(jnp.right_shift(shard, level), 1)


def edge_kernel(
    split,
    key_ref,
    value_ref,
    query_ref,
    residual_ref,
    edge_ref,
    key_first_ref,
    value_first_ref,
    query_first_ref,
    residual_first_ref,
    sems,
):
    row_count = key_ref.shape[0]
    part = WINDOW // 4
    moves = []
    for at, ref in enumerate((key_ref, value_ref)):
        moves += [
            (ref, row_count - WINDOW + piece * part, edge_ref, at * WINDOW + piece * part, part) for piece in range(4)
        ]
    for ref, first_ref in ((key_ref, key_first_ref), (value_ref, value_first_ref)):
        moves += [(ref, (split - 1 + at) * CHUNK, first_ref, at * CHUNK, CHUNK) for at in range(2)]
    moves += [(query_ref, split * CHUNK, query_first_ref, 0, CHUNK)]
    moves += [(residual_ref, split * CHUNK, residual_first_ref, 0, CHUNK)]
    copies = [
        pltpu.make_async_copy(ref.at[pl.ds(start, rows)], to.at[pl.ds(to_start, rows)], sems.at[at])
        for at, (ref, start, to, to_start, rows) in enumerate(moves)
    ]
    for copy in copies:
        copy.start()
    for copy in copies:
        copy.wait()


def edge_rows(split, key_rows, value_rows, query_rows, residual):
    width = key_rows.shape[1]
    return pl.pallas_call(
        functools.partial(edge_kernel, split),
        in_specs=[HBM] * 4,
        out_specs=[VMEM] * 5,
        out_shape=[shaped((2 * WINDOW, width), BF16)]
        + [shaped((2 * CHUNK, width), BF16)] * 2
        + [shaped((CHUNK, width), BF16)] * 2,
        scratch_shapes=[pltpu.SemaphoreType.DMA((14,))],
        compiler_params=params(),
        cost_estimate=cost(0, 2**20),
        name="edge_rows",
    )(*far_off(key_rows, value_rows, query_rows, residual))


def lower_ones():
    row = lax.broadcasted_iota(jnp.int32, (CHUNK, CHUNK), 0)
    lane = lax.broadcasted_iota(jnp.int32, (CHUNK, CHUNK), 1)
    lower = (lane <= row).astype(F32).astype(BF16)
    return jnp.concatenate([lower] * 3, axis=1)


def chunk_sums(lower, rate):
    first = rate.astype(BF16)
    second, third = split_rows(rate - first.astype(F32))
    return dot_turned(lower, jnp.concatenate([first, second, third], axis=1))


def fade_wide(rate_ref, fall, carry, fall_ref, carry_ref):
    heads, row_count = rate_ref.shape
    width = fall_ref.shape[1]
    lower = lower_ones()
    spread = spread_matrix(heads, width)
    prefix = jnp.zeros((1, heads), F32)
    for at in range(0, row_count, CHUNK):
        rows = slice(at, at + CHUNK)
        total = chunk_sums(lower, rate_ref[:, rows])
        fall[rows, :] = jnp.exp(total[CHUNK // 2 - 1 : CHUNK // 2] - total).astype(BF16)
        carry[rows, :] = jnp.exp(-(total + prefix)).astype(BF16)
        prefix = prefix + total[CHUNK - 1 :]
    for lanes in lane_tiles(width):
        fall_ref[:, lanes] = dot(fall[...], spread[:, lanes]).astype(BF16)
        carry_ref[:, lanes] = dot(carry[...], spread[:, lanes]).astype(BF16)


def chunk_masks(doc_pos):
    key_row = lax.broadcasted_iota(jnp.int32, (WINDOW, WINDOW), 0)
    query_lane = lax.broadcasted_iota(jnp.int32, (WINDOW, WINDOW), 1)
    away = query_lane - key_row
    away = jnp.where(away < 0, away + WINDOW, away)
    bias = jnp.where(away <= doc_pos, 0.0, HIDDEN).astype(F32).T
    return bias


def attend_chunk(bias, query, key_before, key, value_before, value, residual):
    query_row = lax.broadcasted_iota(jnp.int32, (WINDOW, WINDOW), 0)
    key_lane = lax.broadcasted_iota(jnp.int32, (WINDOW, WINDOW), 1)
    current = key_lane <= query_row
    current_share = current.astype(F32).astype(BF16)
    before_share = (1.0 - current.astype(F32)).astype(BF16)
    ones = jnp.ones((2 * WINDOW, HEAD_DIM), BF16)
    factor = math.log2(math.e) / math.sqrt(HEAD_DIM)
    scores = dot_turned(query, jnp.concatenate([key_before, key], axis=0))
    merged = jnp.where(current, scores[:, WINDOW:], scores[:, :WINDOW]) + bias
    top = jnp.max(merged, axis=1, keepdims=True)
    weights = jnp.exp2((merged - top) * factor).astype(BF16)
    weights = jnp.concatenate([weights * before_share, weights * current_share], axis=1)
    values = jnp.concatenate([value_before, value], axis=0)
    summed = dot(weights, jnp.concatenate([values, ones], axis=1))
    attended = summed[:, :HEAD_DIM] / summed[:, HEAD_DIM:]
    return (residual.astype(F32) + attended).astype(BF16)


def attend_heads(bias, width, query, key_before, key, value_before, value, residual, hidden):
    def lanes_of(at, ref, rows):
        return ref[rows, at : at + HEAD_DIM]

    for at in range(0, width, HEAD_DIM):
        hidden[0][hidden[1], at : at + HEAD_DIM] = attend_chunk(
            bias,
            lanes_of(at, *query),
            lanes_of(at, *key_before),
            lanes_of(at, *key),
            lanes_of(at, *value_before),
            lanes_of(at, *value),
            lanes_of(at, *residual),
        )


def late_kernel(
    split,
    pos_ref,
    query_ref,
    key_ref,
    value_ref,
    residual_ref,
    key_first_ref,
    value_first_ref,
    query_first_ref,
    residual_first_ref,
    own_weight_ref,
    other_weight_ref,
    hidden_ref,
    c_ref,
    weight_ref,
    b_ref,
    key_early_ref,
    query_early_ref,
    value_early_ref,
    residual_early_ref,
    key_buf,
    value_buf,
    query_buf,
    residual_buf,
    sems,
):
    row_count, width = query_ref.shape
    chunks = row_count // CHUNK
    half_width = width // 2
    arrays = (
        (key_ref, key_buf, key_early_ref),
        (value_ref, value_buf, value_early_ref),
        (query_ref, query_buf, query_early_ref),
        (residual_ref, residual_buf, residual_early_ref),
    )

    def copy(which, chunk):
        source, buffer, _ = arrays[which]
        return pltpu.make_async_copy(
            source.at[chunk_rows(chunk)], buffer.at[chunk_rows(chunk - split)], sems.at[which, chunk - split]
        )

    def copy_early(which, chunk):
        source, _, early = arrays[which]
        rows = chunk_rows(chunk)
        return pltpu.make_async_copy(source.at[rows], early.at[rows], sems.at[which, chunk + chunks - split])

    for chunk in range(split + 1, chunks):
        for which in range(4):
            copy(which, chunk).start()
    for chunk in range(split):
        for which in range(4):
            copy_early(which, chunk).start()

    def attend_one(chunk, query, key_before, key, value_before, value, residual):
        attend_heads(
            chunk_masks(pos_ref[pl.ds(chunk, 1), :]),
            width,
            query,
            key_before,
            key,
            value_before,
            value,
            residual,
            (hidden_ref, chunk_rows(chunk)),
        )

    whole = chunk_rows(0)
    attend_one(
        split,
        (query_first_ref, whole),
        (key_first_ref, whole),
        (key_first_ref, chunk_rows(1)),
        (value_first_ref, whole),
        (value_first_ref, chunk_rows(1)),
        (residual_first_ref, whole),
    )
    key_buf[:CHUNK, :] = key_first_ref[CHUNK:, :]
    value_buf[:CHUNK, :] = value_first_ref[CHUNK:, :]
    is_low = half_index() == 0
    own_weight, other_weight = own_weight_ref[...], other_weight_ref[...]
    weight_ref[:half_width, :] = jnp.where(is_low, own_weight, other_weight)
    weight_ref[half_width:, :] = jnp.where(is_low, other_weight, own_weight)

    def step(chunk, token):
        for which in range(4):
            copy(which, chunk).wait()
        rows, before = chunk_rows(chunk - split), chunk_rows(chunk - split - 1)
        attend_one(
            chunk,
            (query_buf, rows),
            (key_buf, before),
            (key_buf, rows),
            (value_buf, before),
            (value_buf, rows),
            (residual_buf, rows),
        )
        return token

    lax.fori_loop(split + 1, chunks, step, 0)
    shared = dot(hidden_ref[split * CHUNK :, :], weight_ref[...])
    b_ref[...] = shared[:, :STATES].astype(BF16)
    c_ref[split * CHUNK :, :] = shared[:, STATES:].astype(BF16)
    for chunk in range(split):
        for which in range(4):
            copy_early(which, chunk).wait()


def attend_late(split, positions, query, key, value, residual, firsts, weights):
    row_count, width = query.shape
    chunks = row_count // CHUNK
    late = row_count - split * CHUNK
    return pl.pallas_call(
        functools.partial(late_kernel, split),
        in_specs=[VMEM] + [HBM] * 4 + [VMEM] * 6,
        out_specs=[VMEM] * 8,
        out_shape=[
            shaped((row_count, width), BF16),
            shaped((row_count, STATES), BF16),
            shaped((width, 2 * STATES), BF16),
            shaped((late, STATES), BF16),
        ]
        + [shaped((split * CHUNK, width), BF16)] * 4,
        scratch_shapes=[pltpu.VMEM((late, width), BF16)] * 4 + [pltpu.SemaphoreType.DMA((4, chunks))],
        compiler_params=params(),
        cost_estimate=cost(6 * 10**9, 10**7),
        name="attention_late",
    )(
        *near_by(positions),
        *far_off(query, key, value, residual),
        *near_by(*firsts, *weights),
    )


def early_kernel(
    split,
    pos_ref,
    edge_ref,
    key_ref,
    query_ref,
    value_ref,
    residual_ref,
    weight_ref,
    hidden_in_ref,
    c_in_ref,
    hidden_ref,
    c_ref,
    b_ref,
):
    width = query_ref.shape[1]
    early = split * CHUNK

    def attend_one(chunk, key_before, value_before):
        rows = chunk_rows(chunk)
        attend_heads(
            chunk_masks(pos_ref[pl.ds(chunk, 1), :]),
            width,
            (query_ref, rows),
            key_before,
            (key_ref, rows),
            value_before,
            (value_ref, rows),
            (residual_ref, rows),
            (hidden_ref, rows),
        )

    def step(chunk, token):
        rows = chunk_rows(chunk - 1)
        attend_one(chunk, (key_ref, rows), (value_ref, rows))
        return token

    lax.fori_loop(1, split, step, 0)
    attend_one(0, (edge_ref, slice(0, WINDOW)), (edge_ref, slice(WINDOW, 2 * WINDOW)))
    shared = dot(hidden_ref[:early, :], weight_ref[...])
    b_ref[...] = shared[:, :STATES].astype(BF16)
    c_ref[:early, :] = shared[:, STATES:].astype(BF16)


def attend_early(split, positions, edges, parts, weight, hidden, c_mat):
    return pl.pallas_call(
        functools.partial(early_kernel, split),
        in_specs=[VMEM] * 9,
        out_specs=[VMEM] * 3,
        out_shape=[
            shaped(hidden.shape, BF16),
            shaped(c_mat.shape, BF16),
            shaped((split * CHUNK, STATES), BF16),
        ],
        input_output_aliases={7: 0, 8: 1},
        compiler_params=params(),
        cost_estimate=cost(2 * 10**9, 2 * 10**6),
        name="attention_early",
    )(*near_by(positions, edges, *parts, weight, hidden, c_mat))


def scale_kernel(
    rate_ref,
    hidden_ref,
    c_ref,
    scaled_ref,
    rows_ref,
    fall_ref,
    carry_ref,
    c_far_ref,
    rise,
    fall,
    carry,
    logs,
    sems,
):
    heads, row_count = rate_ref.shape
    width = hidden_ref.shape[1]
    chunks = row_count // CHUNK
    copy = pltpu.make_async_copy(c_ref, c_far_ref, sems.at[0])
    copy.start()
    spread = spread_matrix(heads, width)
    lower = lower_ones()
    row_idx = lax.broadcasted_iota(jnp.int32, (8, heads), 0)
    for chunk in range(chunks):
        rows = slice(chunk * CHUNK, (chunk + 1) * CHUNK)
        total = chunk_sums(lower, rate_ref[:, rows])
        middle = total[CHUNK // 2 - 1 : CHUNK // 2]
        last = total[CHUNK - 1 :]
        rise[rows, :] = jnp.exp(total - middle).astype(BF16)
        logs[chunk * 8 : (chunk + 1) * 8, :] = jnp.where(
            row_idx == 0,
            middle - last,
            jnp.where(row_idx == 1, -last, jnp.where(row_idx == 2, -middle, 0.0)),
        )
    high, low = split_rows(jnp.exp(logs[...]))
    for lanes in lane_tiles(width):
        wide = dot(rise[...], spread[:, lanes])
        scaled_ref[:, lanes] = (wide * hidden_ref[:, lanes].astype(F32)).astype(BF16)
        rows_ref[:, lanes] = dot(high, spread[:, lanes]) + dot(low, spread[:, lanes])
    fade_wide(rate_ref, fall, carry, fall_ref, carry_ref)
    copy.wait()


def scale_hidden(rate_turned, hidden, c_mat):
    row_count, width = hidden.shape
    heads = rate_turned.shape[0]
    chunks = row_count // CHUNK
    return pl.pallas_call(
        scale_kernel,
        in_specs=[VMEM] * 3,
        out_specs=[VMEM] * 4 + [HBM],
        out_shape=[
            shaped((row_count, width), BF16),
            shaped((chunks * 8, width), F32),
            shaped((row_count, width), BF16),
            shaped((row_count, width), BF16),
            far_shaped(c_mat.shape, BF16),
        ],
        scratch_shapes=[pltpu.VMEM((row_count, heads), BF16)] * 3
        + [pltpu.VMEM((chunks * 8, heads), F32), pltpu.SemaphoreType.DMA((1,))],
        compiler_params=params(),
        cost_estimate=cost(10**9, 4 * 10**6),
        name="scale_hidden",
    )(*near_by(rate_turned, hidden, c_mat))


def state_kernel(
    early_own_ref,
    early_other_ref,
    late_own_ref,
    late_other_ref,
    scaled_ref,
    rows_ref,
    state_ref,
    turned_far_ref,
    turned,
    sems,
):
    row_count, width = scaled_ref.shape
    chunks = row_count // CHUNK
    early = early_own_ref.shape[0]
    for chunk in range(chunks):
        at = chunk * CHUNK
        if at < early:
            span = slice(at, at + CHUNK)
            own, other = early_own_ref[span, :], early_other_ref[span, :]
        else:
            span = slice(at - early, at - early + CHUNK)
            own, other = late_own_ref[span, :], late_other_ref[span, :]
        turned[:, at : at + CHUNK] = (own.astype(F32) + other.astype(F32)).T.astype(BF16)
    turned_copy = pltpu.make_async_copy(turned, turned_far_ref, sems.at[0])
    turned_copy.start()
    tile = min(width, 256)

    def step(at, carry):
        lanes = pl.ds(pl.multiple_of(at * tile, tile), tile)
        total = fade = None
        for chunk in range(chunks):
            span = slice(chunk * CHUNK, (chunk + 1) * CHUNK)
            factor = rows_ref[chunk * 8 : (chunk + 1) * 8, lanes]
            added = dot(turned[:, span], scaled_ref[span, lanes]) * factor[0:1]
            total = added if total is None else total * factor[1:2] + added
            fade = factor[1:2] if fade is None else fade * factor[1:2]
        state_ref[:STATES, lanes] = total.astype(BF16)
        state_ref[STATES:, lanes] = fade_rows(fade)
        return carry

    lax.fori_loop(0, width // tile, step, 0)
    turned_copy.wait()


def fade_rows(fade):
    high, low = split_rows(fade)
    row = lax.broadcasted_iota(jnp.int32, (EXTRA, fade.shape[1]), 0)
    return jnp.where(row == 0, high.astype(F32), jnp.where(row == 1, low.astype(F32), 0.0)).astype(BF16)


def fade_of(message):
    return message[STATES : STATES + 1].astype(F32) + message[STATES + 1 : STATES + 2].astype(F32)


def block_state(early_own, early_other, late_own, late_other, scaled, factor_rows):
    row_count, width = scaled.shape
    return pl.pallas_call(
        state_kernel,
        in_specs=[VMEM] * 6,
        out_specs=[VMEM, HBM],
        out_shape=[shaped((STATES + EXTRA, width), BF16), far_shaped((STATES, row_count), BF16)],
        scratch_shapes=[pltpu.VMEM((STATES, row_count), BF16), pltpu.SemaphoreType.DMA((1,))],
        compiler_params=params(),
        cost_estimate=cost(3 * 10**8, 4 * 10**6),
        name="block_state",
    )(*near_by(early_own, early_other, late_own, late_other, scaled, factor_rows))


def join_kernel(level, own_ref, other_ref, joined_ref):
    half_width = joined_ref.shape[1]
    own, other = own_ref[...], other_ref[...]
    if own.shape[1] != half_width:
        is_low = half_index() == 0
        own = jnp.where(is_low, own[:, :half_width], own[:, half_width:])
        other = jnp.where(is_low, other[:, :half_width], other[:, half_width:])
    upper = shard_bit(level) == 1
    own_fade, other_fade = fade_of(own), fade_of(other)
    lower, higher = jnp.where(upper, other, own), jnp.where(upper, own, other)
    fade = jnp.where(upper, own_fade, other_fade)
    joined_ref[:STATES, :] = (lower[:STATES].astype(F32) * fade + higher[:STATES].astype(F32)).astype(BF16)
    if joined_ref.shape[0] > STATES:
        joined_ref[STATES:, :] = fade_rows(own_fade * other_fade)


def join(level, own, other, half_width, last):
    return pl.pallas_call(
        functools.partial(join_kernel, level),
        in_specs=[VMEM, VMEM],
        out_specs=VMEM,
        out_shape=shaped((STATES if last else STATES + EXTRA, half_width), BF16),
        compiler_params=params(),
        cost_estimate=cost(10**6, 10**5),
        name="join_runs",
    )(*near_by(own, other))


def runs_kernel(
    local_levels,
    turned_far_ref,
    codes_ref,
    hidden_ref,
    scaled_ref,
    rows_ref,
    wide_ref,
    runs_ref,
    hidden_far_ref,
    turned,
    sems,
):
    row_count, width = scaled_ref.shape
    chunks = row_count // CHUNK
    turned_copy = pltpu.make_async_copy(turned_far_ref, turned, sems.at[chunks])
    turned_copy.start()
    copies = []
    for chunk in range(chunks):
        rows = pl.ds(chunk * CHUNK, CHUNK)
        copies.append(pltpu.make_async_copy(hidden_ref.at[rows], hidden_far_ref.at[rows], sems.at[chunk]))
        copies[-1].start()
    codes = codes_ref[...].astype(F32).T.astype(BF16)
    levels = codes.shape[1]
    pair = 2 * CHUNK
    level_of = lax.broadcasted_iota(jnp.int32, (levels, pair), 0)
    lane = lax.broadcasted_iota(jnp.int32, (levels, pair), 1)
    for at in range(0, wide_ref.shape[1], pair):
        start = (level_of * CHUNK) - at
        pick = ((lane >= start) & (lane < start + CHUNK)).astype(F32).astype(BF16)
        wide_ref[:, at : at + pair] = dot(codes, pick).astype(BF16)
    turned_copy.wait()
    tile = min(width, 256)

    def step(at, token):
        lanes = pl.ds(pl.multiple_of(at * tile, tile), tile)
        held = {}
        for chunk in range(chunks):
            factor = rows_ref[chunk * 8 : (chunk + 1) * 8, lanes]
            for level in range(local_levels):
                start = (chunk * local_levels + level) * STATES
                if level in held:
                    run = (held[level] * factor[2:3]).astype(BF16)
                else:
                    run = jnp.zeros((STATES, tile), BF16)
                runs_ref[start : start + STATES, lanes] = run
            if chunk == chunks - 1:
                break
            span = slice(chunk * CHUNK, (chunk + 1) * CHUNK)
            joined = dot(turned[:, span], scaled_ref[span, lanes]) * factor[0:1]
            held = {level: state * factor[1:2] for level, state in held.items()}
            level = 0
            while level in held:
                joined = joined + held.pop(level)
                level += 1
            held[level] = joined
        return token

    lax.fori_loop(0, width // tile, step, 0)
    for copy in copies:
        copy.wait()


def codes_and_runs(turned_far, codes_turned, hidden, scaled, factor_rows):
    row_count, width = scaled.shape
    levels = codes_turned.shape[0]
    levels += levels % 2
    chunks = row_count // CHUNK
    local_levels = chunks.bit_length() - 1
    return pl.pallas_call(
        functools.partial(runs_kernel, local_levels),
        in_specs=[HBM] + [VMEM] * 4,
        out_specs=[VMEM, VMEM, HBM],
        out_shape=[
            shaped((row_count, levels * CHUNK), BF16),
            shaped((chunks * local_levels * STATES, width), BF16),
            far_shaped(hidden.shape, BF16),
        ],
        scratch_shapes=[pltpu.VMEM((STATES, row_count), BF16), pltpu.SemaphoreType.DMA((chunks + 1,))],
        compiler_params=params(),
        cost_estimate=cost(10**9, 10**7),
        name="codes_and_runs",
    )(*far_off(turned_far), *near_by(codes_turned, hidden, scaled, factor_rows))


def weights_kernel(
    local_levels,
    cross_levels,
    scale_ref,
    turned_far_ref,
    c_far_ref,
    c_other_ref,
    codes_ref,
    left_ref,
    early_reads_ref,
    last_reads_ref,
    turned,
    c_buf,
    sems,
):
    row_count = c_other_ref.shape[0]
    copies = [
        pltpu.make_async_copy(turned_far_ref, turned, sems.at[0]),
        pltpu.make_async_copy(c_far_ref, c_buf, sems.at[1]),
    ]
    for copy in copies:
        copy.start()
    for copy in copies:
        copy.wait()

    query_row = lax.broadcasted_iota(jnp.int32, (CHUNK, CHUNK), 0)
    key_lane = lax.broadcasted_iota(jnp.int32, (CHUNK, CHUNK), 1)
    differ = jnp.bitwise_xor(query_row, key_lane)
    inner_levels = CHUNK.bit_length() - 1

    def step(chunk, token):
        rows = chunk_rows(chunk)

        def lam_of(level):
            return codes_ref[rows, level * CHUNK : (level + 1) * CHUNK].astype(F32) * scale_ref[0:1, level : level + 1]

        c_wide = (c_buf[rows, :].astype(F32) + c_other_ref[rows, :].astype(F32)).astype(BF16).astype(F32)
        gram = dot(c_wide.astype(BF16), turned[:, rows])
        weight = lam_of(0)
        for level in range(1, inner_levels + 1):
            weight = jnp.where(differ >= 1 << (level - 1), lam_of(level), weight)
        left_ref[rows, :CHUNK] = jnp.where(key_lane <= query_row, gram * weight, 0.0).astype(BF16)
        for level in range(local_levels + cross_levels):
            read = (c_wide * lam_of(inner_levels + 1 + level)).astype(BF16)
            if level < local_levels:
                left_ref[rows, (level + 1) * CHUNK : (level + 2) * CHUNK] = read
            elif level < local_levels + cross_levels - 1:
                at = (level - local_levels) * STATES
                early_reads_ref[rows, at : at + STATES] = read
            else:
                last_reads_ref[rows, :] = read
        return token

    lax.fori_loop(0, row_count // CHUNK, step, 0)


def level_products(scale, turned_far, c_far, c_other, codes_wide, cross_levels):
    row_count = c_other.shape[0]
    local_levels = (row_count // CHUNK).bit_length() - 1
    return pl.pallas_call(
        functools.partial(weights_kernel, local_levels, cross_levels),
        in_specs=[VMEM] + [HBM] * 2 + [VMEM] * 2,
        out_specs=[VMEM] * 3,
        out_shape=[
            shaped((row_count, (1 + local_levels) * STATES), BF16),
            shaped((row_count, (cross_levels - 1) * STATES), BF16),
            shaped((row_count, STATES), BF16),
        ],
        scratch_shapes=[
            pltpu.VMEM((STATES, row_count), BF16),
            pltpu.VMEM((row_count, STATES), BF16),
            pltpu.SemaphoreType.DMA((2,)),
        ],
        compiler_params=params(),
        cost_estimate=cost(10**9, 10**7),
        name="level_products",
    )(*near_by(scale), *far_off(turned_far, c_far), *near_by(c_other, codes_wide))


def carried_state(message, before, upper):
    return (message[:STATES].astype(F32) * (before * upper.astype(F32))).astype(BF16)


def local_kernel(
    local_levels,
    cross_levels,
    hidden_far_ref,
    left_ref,
    early_reads_ref,
    scaled_ref,
    fall_ref,
    carry_ref,
    runs_ref,
    near_ref,
    *refs,
):
    received = refs[: cross_levels - 2]
    swapped = refs[cross_levels - 2 : 2 * (cross_levels - 2)]
    local_ref, hidden_ref, before_ref, carried, crossed, sems = refs[2 * (cross_levels - 2) :]
    row_count, width = scaled_ref.shape
    chunks = row_count // CHUNK
    copies = [
        pltpu.make_async_copy(
            hidden_far_ref.at[chunk_rows(chunk)], hidden_ref.at[chunk_rows(chunk)], sems.at[chunk]
        )
        for chunk in range(chunks)
    ]
    for copy in copies:
        copy.start()

    is_low = half_index() == 0
    before = jnp.ones((1, width), F32)
    for level in range(cross_levels - 1):
        upper = shard_bit(level)
        if level == 0:
            message = near_ref[...]
        else:
            own, other = received[level - 1][...], swapped[level - 1][...]
            message = jnp.concatenate(
                [jnp.where(is_low, own, other), jnp.where(is_low, other, own)], axis=1
            )
        carried[level * STATES : (level + 1) * STATES, :] = carried_state(message, before, upper)
        before = jnp.where(upper == 1, before * fade_of(message), before)
    before_ref[...] = jnp.broadcast_to(before, before_ref.shape)
    tiles = lane_tiles(width)
    for lanes in tiles:
        crossed[:, lanes] = dot(early_reads_ref[...], carried[:, lanes]) * carry_ref[:, lanes].astype(F32)

    def step(chunk, token):
        rows = chunk_rows(chunk)
        left = left_ref[rows, :]
        run_rows = local_levels * STATES
        runs = pl.ds(pl.multiple_of(chunk * run_rows, run_rows), run_rows)
        for lanes in tiles:
            summed = dot(left, jnp.concatenate([scaled_ref[rows, lanes], runs_ref[runs, lanes]], axis=0))
            local_ref[rows, lanes] = (
                summed * fall_ref[rows, lanes].astype(F32) + crossed[rows, lanes]
            ).astype(BF16)
        return token

    lax.fori_loop(0, chunks, step, 0)
    for copy in copies:
        copy.wait()


def local_terms(hidden_far, left, early_reads, scaled, fall, carry, runs, near, received, swapped):
    row_count, width = scaled.shape
    local_levels = (row_count // CHUNK).bit_length() - 1
    cross_levels = 2 + len(received)
    return pl.pallas_call(
        functools.partial(local_kernel, local_levels, cross_levels),
        in_specs=[HBM] + [VMEM] * (7 + 2 * len(received)),
        out_specs=[VMEM] * 3,
        out_shape=[shaped((row_count, width), BF16)] * 2 + [shaped((8, width), F32)],
        scratch_shapes=[
            pltpu.VMEM(((cross_levels - 1) * STATES, width), BF16),
            pltpu.VMEM((row_count, width), F32),
            pltpu.SemaphoreType.DMA((row_count // CHUNK,)),
        ],
        compiler_params=params(),
        cost_estimate=cost(3 * 10**9, 10**7),
        name="local_terms",
    )(
        *far_off(hidden_far),
        *near_by(left, early_reads, scaled, fall, carry, runs, near, *received, *swapped),
    )


def finish_kernel(
    swap, cross_levels, message_ref, before_ref, hidden_ref, reads_ref, local_ref, carry_ref, gain_ref, *refs
):
    row_count, width = local_ref.shape
    half_width = width // 2
    own_start = half_index() * half_width
    start = half_width - own_start if swap else own_start
    upper = shard_bit(cross_levels - 1)
    tile = min(half_width, 256)
    row = lax.broadcasted_iota(jnp.int32, (tile, tile), 0) // HEAD_VALUES
    lane = lax.broadcasted_iota(jnp.int32, (tile, tile), 1) // HEAD_VALUES
    mean_mat = jnp.where(row == lane, 1.0 / HEAD_VALUES, 0.0).astype(BF16)
    copies = []
    if swap:
        held_ref, out_ref, result, sems = refs
    else:
        (result,) = refs

    def copy_out(source, here, lanes, at):
        for piece in range(OUT_PIECES):
            rows = pl.ds(piece * (row_count // OUT_PIECES), row_count // OUT_PIECES)
            copies.append(
                pltpu.make_async_copy(source.at[rows, here], out_ref.at[rows, lanes], sems.at[at, piece])
            )
            copies[-1].start()

    if swap:
        lanes = pl.ds(pl.multiple_of(own_start, half_width), half_width)
        copy_out(held_ref, pl.ds(0, half_width), lanes, 0)
    for at in range(half_width // tile):
        lanes = pl.ds(pl.multiple_of(start + at * tile, tile), tile)
        here = slice(at * tile, (at + 1) * tile)
        carried = carried_state(message_ref[:, here], before_ref[0:1, lanes], upper)
        cross = dot(reads_ref[...], carried).astype(BF16)
        mixed = local_ref[:, lanes] + cross * carry_ref[:, lanes]
        mean = dot(mixed * mixed, mean_mat)
        normed = mixed * lax.rsqrt(mean + 1e-05).astype(BF16) * gain_ref[:, lanes].astype(BF16)
        result[:, here] = hidden_ref[:, lanes] + normed
        if swap:
            copy_out(result, here, lanes, 1 + at)
    for copy in copies:
        copy.wait()


def finish(cross_levels, message, before, hidden, reads, local, carry, gain, held):
    row_count, width = local.shape
    half_width = width // 2
    swap = held is not None
    half_shape = (row_count, half_width)
    return pl.pallas_call(
        functools.partial(finish_kernel, swap, cross_levels),
        in_specs=[VMEM] * (8 if swap else 7),
        out_specs=HBM if swap else VMEM,
        out_shape=far_shaped((row_count, width), BF16) if swap else shaped(half_shape, BF16),
        scratch_shapes=[
            pltpu.VMEM(half_shape, BF16),
            pltpu.SemaphoreType.DMA((1 + max(1, half_width // 256), OUT_PIECES)),
        ]
        if swap
        else [],
        compiler_params=params(),
        cost_estimate=cost(2 * 10**9, 8 * 10**6),
        name="carried_and_norm",
    )(*near_by(message, before, hidden, reads, local, carry, gain, *([held] if swap else [])))


def from_behind(x, axis, by):
    length = lax.axis_size(axis)
    return lax.ppermute(x, axis, [(i, i + by) for i in range(length - by)])


def partner(x, axis, distance):
    return lax.ppermute(x, axis, [(i, i ^ 1 << distance) for i in range(lax.axis_size(axis))])


def mirrored(x):
    length = lax.axis_size("seq")
    return lax.ppermute(x, "seq", [(i, length - 1 - i) for i in range(length)])


def summed_over_heads(share):
    rounds = lax.axis_size("head").bit_length() - 1
    if rounds == 0:
        return share, jnp.zeros_like(share)
    total = share
    for distance in range(rounds - 1):
        total = (total.astype(F32) + partner(total, "head", distance).astype(F32)).astype(BF16)
    return total, partner(total, "head", rounds - 1)


def body(
    residual_in,
    query_rows,
    key_rows,
    value_rows,
    bc_weight,
    decay_rate,
    level_codes,
    level_scale,
    positions,
    ssm_gain,
):
    row_count, width = residual_in.shape
    half_width = width // 2
    shard_axes = ("seq", "fsdp")
    cross_levels = lax.axis_size(shard_axes).bit_length() - 1

    weights = (bc_weight, partner(bc_weight, "fsdp", 0))
    split = max(1, row_count // CHUNK // 4)
    edge, *firsts = edge_rows(split, key_rows, value_rows, query_rows, residual_in)
    edges = from_behind(edge, shard_axes, 1)
    pos_rows = positions.reshape(row_count // CHUNK, CHUNK)
    rate_turned = decay_rate.T
    hidden, c_mat, weight, b_late, *parts = attend_late(
        split, pos_rows, query_rows, key_rows, value_rows, residual_in, firsts, weights
    )
    late_own, late_other = summed_over_heads(b_late)
    hidden, c_mat, b_early = attend_early(split, pos_rows, edges, parts, weight, hidden, c_mat)
    early_own, early_other = summed_over_heads(b_early)
    scaled, factor_rows, fall, carry, c_far = scale_hidden(rate_turned, hidden, c_mat)
    c_mat, scaled = lax.optimization_barrier((c_mat, scaled))
    c_sent, c_other = summed_over_heads(c_mat)
    if lax.axis_size("head") > 2:
        c_far = c_sent
    state, turned_far = block_state(
        early_own, early_other, late_own, late_other, scaled, factor_rows
    )
    near = partner(state, "fsdp", 0)
    joined = join(0, state, near, half_width, cross_levels == 2)
    received, swapped = [], []
    for level in range(1, cross_levels):
        other = mirrored(joined) if level == cross_levels - 1 else partner(joined, "seq", level - 1)
        if level == 1:
            codes_wide, runs, hidden_far = codes_and_runs(
                turned_far, level_codes.T, hidden, scaled, factor_rows
            )
            other, codes_wide = lax.optimization_barrier((other, codes_wide))
        received.append(other)
        if level < cross_levels - 1:
            joined = join(level, joined, other, half_width, level == cross_levels - 2)
            swapped.append(partner(other, "fsdp", 0))
    left, early_reads, last_reads = level_products(
        level_scale[None, :], turned_far, c_far, c_other, codes_wide, cross_levels
    )
    local, hidden, before = local_terms(
        hidden_far, left, early_reads, scaled, fall, carry, runs, near, received[:-1], swapped
    )
    last, local = lax.optimization_barrier((received[-1], local))
    last_swapped = partner(last, "fsdp", 0)
    gain = ssm_gain[None, :]
    half = finish(cross_levels, last, before, hidden, last_reads, local, carry, gain, None)
    return finish(cross_levels, last_swapped, before, hidden, last_reads, local, carry, gain, half)


def solution(mesh):
    in_specs = (
        P(("groups", "seq", "fsdp"), "head"),
        P(("groups", "seq", "fsdp"), "head"),
        P(("groups", "seq", "fsdp"), "head"),
        P(("groups", "seq", "fsdp"), "head"),
        P(("head", "fsdp"), None),
        P(("groups", "seq", "fsdp"), "head"),
        P(("groups", "seq", "fsdp"), None),
        P(),
        P(("groups", "seq", "fsdp")),
        P("head"),
    )
    out_specs = P(("groups", "seq", "fsdp"), "head")
    return jax.shard_map(body, mesh=mesh, in_specs=in_specs, out_specs=out_specs, check_vma=False)
```

```python
import functools
import math

import jax
import jax.numpy as jnp
from jax import lax
from jax.experimental import pallas as pl
from jax.experimental.pallas import tpu as pltpu
from jax.sharding import PartitionSpec as P

HEAD_DIM = 128
HEAD_VALUES = 64
STATES = 128
WINDOW = 128
CHUNK = 128
EXTRA = 16
OUT_PIECES = 4
VMEM_LIMIT = 24 * 1024 * 1024
HIDDEN = -1e30

F32 = jnp.float32
BF16 = jnp.bfloat16
VMEM = pl.BlockSpec(memory_space=pltpu.VMEM)
SMEM = pl.BlockSpec(memory_space=pltpu.SMEM)
HBM = pl.BlockSpec(memory_space=pltpu.HBM)


def params():
    return pltpu.CompilerParams(vmem_limit_bytes=VMEM_LIMIT)


def cost(flops, moved, transcendentals=0):
    return pl.CostEstimate(flops=flops, bytes_accessed=moved, transcendentals=transcendentals)


def shaped(shape, dtype):
    return pltpu.VMEM(shape, dtype)


def far_shaped(shape, dtype):
    return pltpu.HBM(shape, dtype)


def near_by(*arrays):
    return [pltpu.with_memory_space_constraint(x, pltpu.VMEM) for x in arrays]


def far_off(*arrays):
    return [pltpu.with_memory_space_constraint(x, pltpu.HBM) for x in arrays]


def dot(left, right):
    return jnp.dot(left, right, preferred_element_type=F32)


def dot_turned(left, right):
    return lax.dot_general(left, right, (((1,), (1,)), ((), ())), preferred_element_type=F32)


def chunk_rows(index, count=1):
    return pl.ds(pl.multiple_of(index * CHUNK, CHUNK), count * CHUNK)


def spread_matrix(heads, width):
    lane = lax.broadcasted_iota(jnp.int32, (heads, width), 1)
    start = lax.broadcasted_iota(jnp.int32, (heads, width), 0) * HEAD_VALUES
    return ((lane >= start) & (lane < start + HEAD_VALUES)).astype(F32).astype(BF16)


def lane_tiles(width):
    tile = min(width, 256)
    return [slice(at, at + tile) for at in range(0, width, tile)]


def split_rows(rows):
    high = rows.astype(BF16)
    return high, (rows - high.astype(F32)).astype(BF16)


def half_index():
    return lax.axis_index("fsdp")


def shard_bit(level):
    shard = lax.axis_index("seq") * lax.axis_size("fsdp") + lax.axis_index("fsdp")
    return jnp.bitwise_and(jnp.right_shift(shard, level), 1)


def edge_kernel(key_ref, value_ref, edge_ref, sems):
    row_count = key_ref.shape[0]
    part = WINDOW // 4
    copies = [
        pltpu.make_async_copy(
            ref.at[pl.ds(row_count - WINDOW + piece * part, part)],
            edge_ref.at[pl.ds(at * WINDOW + piece * part, part)],
            sems.at[at, piece],
        )
        for at, ref in enumerate((key_ref, value_ref))
        for piece in range(4)
    ]
    for copy in copies:
        copy.start()
    for copy in copies:
        copy.wait()


def edge_rows(key_rows, value_rows):
    width = key_rows.shape[1]
    return pl.pallas_call(
        edge_kernel,
        in_specs=[HBM] * 2,
        out_specs=VMEM,
        out_shape=shaped((2 * WINDOW, width), BF16),
        scratch_shapes=[pltpu.SemaphoreType.DMA((2, 4))],
        compiler_params=params(),
        cost_estimate=cost(0, 2**20),
        name="edge_rows",
    )(*far_off(key_rows, value_rows))


def lower_ones():
    row = lax.broadcasted_iota(jnp.int32, (CHUNK, CHUNK), 0)
    lane = lax.broadcasted_iota(jnp.int32, (CHUNK, CHUNK), 1)
    lower = (lane <= row).astype(F32).astype(BF16)
    return jnp.concatenate([lower] * 3, axis=1)


def chunk_sums(lower, rate):
    first = rate.astype(BF16)
    second, third = split_rows(rate - first.astype(F32))
    return dot_turned(lower, jnp.concatenate([first, second, third], axis=1))


def fade_wide(rate_ref, fall, carry, fall_ref, carry_ref):
    heads, row_count = rate_ref.shape
    width = fall_ref.shape[1]
    lower = lower_ones()
    spread = spread_matrix(heads, width)
    prefix = jnp.zeros((1, heads), F32)
    for at in range(0, row_count, CHUNK):
        rows = slice(at, at + CHUNK)
        total = chunk_sums(lower, rate_ref[:, rows])
        fall[rows, :] = jnp.exp(total[CHUNK // 2 - 1 : CHUNK // 2] - total).astype(BF16)
        carry[rows, :] = jnp.exp(-(total + prefix)).astype(BF16)
        prefix = prefix + total[CHUNK - 1 :]
    for lanes in lane_tiles(width):
        fall_ref[:, lanes] = dot(fall[...], spread[:, lanes]).astype(BF16)
        carry_ref[:, lanes] = dot(carry[...], spread[:, lanes]).astype(BF16)


def chunk_masks(doc_pos):
    key_row = lax.broadcasted_iota(jnp.int32, (WINDOW, WINDOW), 0)
    query_lane = lax.broadcasted_iota(jnp.int32, (WINDOW, WINDOW), 1)
    away = query_lane - key_row
    away = jnp.where(away < 0, away + WINDOW, away)
    bias = jnp.where(away <= doc_pos, 0.0, HIDDEN).astype(F32).T
    return bias


def attend_chunk(bias, query, key_before, key, value_before, value, residual):
    query_row = lax.broadcasted_iota(jnp.int32, (WINDOW, WINDOW), 0)
    key_lane = lax.broadcasted_iota(jnp.int32, (WINDOW, WINDOW), 1)
    current = key_lane <= query_row
    current_share = current.astype(F32).astype(BF16)
    before_share = (1.0 - current.astype(F32)).astype(BF16)
    ones = jnp.ones((2 * WINDOW, HEAD_DIM), BF16)
    factor = math.log2(math.e) / math.sqrt(HEAD_DIM)
    scores = dot_turned(query, jnp.concatenate([key_before, key], axis=0))
    merged = jnp.where(current, scores[:, WINDOW:], scores[:, :WINDOW]) + bias
    top = jnp.max(merged, axis=1, keepdims=True)
    weights = jnp.exp2((merged - top) * factor).astype(BF16)
    weights = jnp.concatenate([weights * before_share, weights * current_share], axis=1)
    values = jnp.concatenate([value_before, value], axis=0)
    summed = dot(weights, jnp.concatenate([values, ones], axis=1))
    attended = summed[:, :HEAD_DIM] / summed[:, HEAD_DIM:]
    return (residual.astype(F32) + attended).astype(BF16)


def attend_heads(bias, width, query, key_before, key, value_before, value, residual, hidden):
    def lanes_of(at, ref, rows):
        return ref[rows, at : at + HEAD_DIM]

    for at in range(0, width, HEAD_DIM):
        hidden[0][hidden[1], at : at + HEAD_DIM] = attend_chunk(
            bias,
            lanes_of(at, *query),
            lanes_of(at, *key_before),
            lanes_of(at, *key),
            lanes_of(at, *value_before),
            lanes_of(at, *value),
            lanes_of(at, *residual),
        )


def late_kernel(
    split,
    pos_ref,
    query_ref,
    key_ref,
    value_ref,
    residual_ref,
    own_weight_ref,
    other_weight_ref,
    hidden_ref,
    c_ref,
    weight_ref,
    b_ref,
    key_early_ref,
    query_early_ref,
    value_early_ref,
    residual_early_ref,
    key_buf,
    value_buf,
    query_buf,
    residual_buf,
    sems,
):
    row_count, width = query_ref.shape
    chunks = row_count // CHUNK
    half_width = width // 2
    arrays = (
        (key_ref, key_buf, key_early_ref),
        (value_ref, value_buf, value_early_ref),
        (query_ref, query_buf, query_early_ref),
        (residual_ref, residual_buf, residual_early_ref),
    )

    def copy(which, chunk):
        source, buffer, _ = arrays[which]
        return pltpu.make_async_copy(
            source.at[chunk_rows(chunk)], buffer.at[chunk_rows(chunk - split)], sems.at[which, chunk - split]
        )

    def copy_early(which, chunk):
        source, _, early = arrays[which]
        rows = chunk_rows(chunk)
        return pltpu.make_async_copy(source.at[rows], early.at[rows], sems.at[which, chunk + chunks - split])

    for which in range(2):
        copy_early(which, split - 1).start()
    for chunk in range(split, chunks):
        for which in range(4):
            copy(which, chunk).start()
    for which in range(2, 4):
        copy_early(which, split - 1).start()
    for chunk in range(split - 1):
        for which in range(4):
            copy_early(which, chunk).start()
    is_low = half_index() == 0
    own_weight, other_weight = own_weight_ref[...], other_weight_ref[...]
    weight_ref[:half_width, :] = jnp.where(is_low, own_weight, other_weight)
    weight_ref[half_width:, :] = jnp.where(is_low, other_weight, own_weight)

    def attend_one(chunk, key_before, value_before):
        for which in range(4):
            copy(which, chunk).wait()
        rows = chunk_rows(chunk - split)
        attend_heads(
            chunk_masks(pos_ref[pl.ds(chunk, 1), :]),
            width,
            (query_buf, rows),
            key_before,
            (key_buf, rows),
            value_before,
            (value_buf, rows),
            (residual_buf, rows),
            (hidden_ref, chunk_rows(chunk)),
        )

    for which in range(2):
        copy_early(which, split - 1).wait()
    last = chunk_rows(split - 1)
    attend_one(split, (key_early_ref, last), (value_early_ref, last))

    def step(chunk, token):
        before = chunk_rows(chunk - split - 1)
        attend_one(chunk, (key_buf, before), (value_buf, before))
        return token

    lax.fori_loop(split + 1, chunks, step, 0)
    shared = dot(hidden_ref[split * CHUNK :, :], weight_ref[...])
    b_ref[...] = shared[:, :STATES].astype(BF16)
    c_ref[split * CHUNK :, :] = shared[:, STATES:].astype(BF16)
    for which in range(2, 4):
        copy_early(which, split - 1).wait()
    for chunk in range(split - 1):
        for which in range(4):
            copy_early(which, chunk).wait()


def attend_late(split, positions, query, key, value, residual, weights):
    row_count, width = query.shape
    chunks = row_count // CHUNK
    late = row_count - split * CHUNK
    return pl.pallas_call(
        functools.partial(late_kernel, split),
        in_specs=[VMEM] + [HBM] * 4 + [VMEM] * 2,
        out_specs=[VMEM] * 8,
        out_shape=[
            shaped((row_count, width), BF16),
            shaped((row_count, STATES), BF16),
            shaped((width, 2 * STATES), BF16),
            shaped((late, STATES), BF16),
        ]
        + [shaped((split * CHUNK, width), BF16)] * 4,
        scratch_shapes=[pltpu.VMEM((late, width), BF16)] * 4 + [pltpu.SemaphoreType.DMA((4, chunks))],
        compiler_params=params(),
        cost_estimate=cost(6 * 10**9, 10**7),
        name="attention_late",
    )(
        *near_by(positions),
        *far_off(query, key, value, residual),
        *near_by(*weights),
    )


def early_kernel(
    split,
    pos_ref,
    edge_ref,
    key_ref,
    query_ref,
    value_ref,
    residual_ref,
    weight_ref,
    hidden_in_ref,
    c_in_ref,
    hidden_ref,
    c_ref,
    b_ref,
):
    width = query_ref.shape[1]
    early = split * CHUNK

    def attend_one(chunk, key_before, value_before):
        rows = chunk_rows(chunk)
        attend_heads(
            chunk_masks(pos_ref[pl.ds(chunk, 1), :]),
            width,
            (query_ref, rows),
            key_before,
            (key_ref, rows),
            value_before,
            (value_ref, rows),
            (residual_ref, rows),
            (hidden_ref, rows),
        )

    def step(chunk, token):
        rows = chunk_rows(chunk - 1)
        attend_one(chunk, (key_ref, rows), (value_ref, rows))
        return token

    lax.fori_loop(1, split, step, 0)
    attend_one(0, (edge_ref, slice(0, WINDOW)), (edge_ref, slice(WINDOW, 2 * WINDOW)))
    shared = dot(hidden_ref[:early, :], weight_ref[...])
    b_ref[...] = shared[:, :STATES].astype(BF16)
    c_ref[:early, :] = shared[:, STATES:].astype(BF16)


def attend_early(split, positions, edges, parts, weight, hidden, c_mat):
    return pl.pallas_call(
        functools.partial(early_kernel, split),
        in_specs=[VMEM] * 9,
        out_specs=[VMEM] * 3,
        out_shape=[
            shaped(hidden.shape, BF16),
            shaped(c_mat.shape, BF16),
            shaped((split * CHUNK, STATES), BF16),
        ],
        input_output_aliases={7: 0, 8: 1},
        compiler_params=params(),
        cost_estimate=cost(2 * 10**9, 2 * 10**6),
        name="attention_early",
    )(*near_by(positions, edges, *parts, weight, hidden, c_mat))


def scale_kernel(
    rate_ref,
    hidden_ref,
    c_ref,
    scaled_ref,
    rows_ref,
    fall_ref,
    carry_ref,
    c_far_ref,
    rise,
    fall,
    carry,
    logs,
    sems,
):
    heads, row_count = rate_ref.shape
    width = hidden_ref.shape[1]
    chunks = row_count // CHUNK
    copy = pltpu.make_async_copy(c_ref, c_far_ref, sems.at[0])
    copy.start()
    spread = spread_matrix(heads, width)
    lower = lower_ones()
    row_idx = lax.broadcasted_iota(jnp.int32, (8, heads), 0)
    for chunk in range(chunks):
        rows = slice(chunk * CHUNK, (chunk + 1) * CHUNK)
        total = chunk_sums(lower, rate_ref[:, rows])
        middle = total[CHUNK // 2 - 1 : CHUNK // 2]
        last = total[CHUNK - 1 :]
        rise[rows, :] = jnp.exp(total - middle).astype(BF16)
        logs[chunk * 8 : (chunk + 1) * 8, :] = jnp.where(
            row_idx == 0,
            middle - last,
            jnp.where(row_idx == 1, -last, jnp.where(row_idx == 2, -middle, 0.0)),
        )
    high, low = split_rows(jnp.exp(logs[...]))
    for lanes in lane_tiles(width):
        wide = dot(rise[...], spread[:, lanes])
        scaled_ref[:, lanes] = (wide * hidden_ref[:, lanes].astype(F32)).astype(BF16)
        rows_ref[:, lanes] = dot(high, spread[:, lanes]) + dot(low, spread[:, lanes])
    fade_wide(rate_ref, fall, carry, fall_ref, carry_ref)
    copy.wait()


def scale_hidden(rate_turned, hidden, c_mat):
    row_count, width = hidden.shape
    heads = rate_turned.shape[0]
    chunks = row_count // CHUNK
    return pl.pallas_call(
        scale_kernel,
        in_specs=[VMEM] * 3,
        out_specs=[VMEM] * 4 + [HBM],
        out_shape=[
            shaped((row_count, width), BF16),
            shaped((chunks * 8, width), F32),
            shaped((row_count, width), BF16),
            shaped((row_count, width), BF16),
            far_shaped(c_mat.shape, BF16),
        ],
        scratch_shapes=[pltpu.VMEM((row_count, heads), BF16)] * 3
        + [pltpu.VMEM((chunks * 8, heads), F32), pltpu.SemaphoreType.DMA((1,))],
        compiler_params=params(),
        cost_estimate=cost(10**9, 4 * 10**6),
        name="scale_hidden",
    )(*near_by(rate_turned, hidden, c_mat))


def state_kernel(
    early_own_ref,
    early_other_ref,
    late_own_ref,
    late_other_ref,
    scaled_ref,
    rows_ref,
    state_ref,
    turned_far_ref,
    turned,
    sems,
):
    row_count, width = scaled_ref.shape
    chunks = row_count // CHUNK
    early = early_own_ref.shape[0]
    for chunk in range(chunks):
        at = chunk * CHUNK
        if at < early:
            span = slice(at, at + CHUNK)
            own, other = early_own_ref[span, :], early_other_ref[span, :]
        else:
            span = slice(at - early, at - early + CHUNK)
            own, other = late_own_ref[span, :], late_other_ref[span, :]
        turned[:, at : at + CHUNK] = (own.astype(F32) + other.astype(F32)).T.astype(BF16)
    turned_copy = pltpu.make_async_copy(turned, turned_far_ref, sems.at[0])
    turned_copy.start()
    tile = min(width, 256)

    def step(at, carry):
        lanes = pl.ds(pl.multiple_of(at * tile, tile), tile)
        total = fade = None
        for chunk in range(chunks):
            span = slice(chunk * CHUNK, (chunk + 1) * CHUNK)
            factor = rows_ref[chunk * 8 : (chunk + 1) * 8, lanes]
            added = dot(turned[:, span], scaled_ref[span, lanes]) * factor[0:1]
            total = added if total is None else total * factor[1:2] + added
            fade = factor[1:2] if fade is None else fade * factor[1:2]
        state_ref[:STATES, lanes] = total.astype(BF16)
        state_ref[STATES:, lanes] = fade_rows(fade)
        return carry

    lax.fori_loop(0, width // tile, step, 0)
    turned_copy.wait()


def fade_rows(fade):
    high, low = split_rows(fade)
    row = lax.broadcasted_iota(jnp.int32, (EXTRA, fade.shape[1]), 0)
    return jnp.where(row == 0, high.astype(F32), jnp.where(row == 1, low.astype(F32), 0.0)).astype(BF16)


def fade_of(message):
    return message[STATES : STATES + 1].astype(F32) + message[STATES + 1 : STATES + 2].astype(F32)


def block_state(early_own, early_other, late_own, late_other, scaled, factor_rows):
    row_count, width = scaled.shape
    return pl.pallas_call(
        state_kernel,
        in_specs=[VMEM] * 6,
        out_specs=[VMEM, HBM],
        out_shape=[shaped((STATES + EXTRA, width), BF16), far_shaped((STATES, row_count), BF16)],
        scratch_shapes=[pltpu.VMEM((STATES, row_count), BF16), pltpu.SemaphoreType.DMA((1,))],
        compiler_params=params(),
        cost_estimate=cost(3 * 10**8, 4 * 10**6),
        name="block_state",
    )(*near_by(early_own, early_other, late_own, late_other, scaled, factor_rows))


def join_kernel(level, own_ref, other_ref, joined_ref):
    half_width = joined_ref.shape[1]
    own, other = own_ref[...], other_ref[...]
    if own.shape[1] != half_width:
        is_low = half_index() == 0
        own = jnp.where(is_low, own[:, :half_width], own[:, half_width:])
        other = jnp.where(is_low, other[:, :half_width], other[:, half_width:])
    upper = shard_bit(level) == 1
    own_fade, other_fade = fade_of(own), fade_of(other)
    lower, higher = jnp.where(upper, other, own), jnp.where(upper, own, other)
    fade = jnp.where(upper, own_fade, other_fade)
    joined_ref[:STATES, :] = (lower[:STATES].astype(F32) * fade + higher[:STATES].astype(F32)).astype(BF16)
    if joined_ref.shape[0] > STATES:
        joined_ref[STATES:, :] = fade_rows(own_fade * other_fade)


def join(level, own, other, half_width, last):
    return pl.pallas_call(
        functools.partial(join_kernel, level),
        in_specs=[VMEM, VMEM],
        out_specs=VMEM,
        out_shape=shaped((STATES if last else STATES + EXTRA, half_width), BF16),
        compiler_params=params(),
        cost_estimate=cost(10**6, 10**5),
        name="join_runs",
    )(*near_by(own, other))


def run_place(chunk, level=0):
    return sum(bin(at).count("1") for at in range(chunk)) + bin(chunk & ((1 << level) - 1)).count("1")


def runs_kernel(
    local_levels,
    turned_far_ref,
    c_far_ref,
    codes_ref,
    hidden_ref,
    scaled_ref,
    rows_ref,
    wide_ref,
    runs_ref,
    turned,
    c_ref,
    hidden_far_ref,
    sems,
):
    row_count, width = scaled_ref.shape
    chunks = row_count // CHUNK
    turned_copy = pltpu.make_async_copy(turned_far_ref, turned, sems.at[chunks])
    turned_copy.start()
    copies = [pltpu.make_async_copy(c_far_ref, c_ref, sems.at[chunks + 1])]
    copies[0].start()
    for chunk in range(chunks):
        rows = pl.ds(chunk * CHUNK, CHUNK)
        copies.append(pltpu.make_async_copy(hidden_ref.at[rows], hidden_far_ref.at[rows], sems.at[chunk]))
        copies[-1].start()
    codes = codes_ref[...].astype(F32).T.astype(BF16)
    levels = codes.shape[1]
    pair = 2 * CHUNK
    level_of = lax.broadcasted_iota(jnp.int32, (levels, pair), 0)
    lane = lax.broadcasted_iota(jnp.int32, (levels, pair), 1)
    for at in range(0, wide_ref.shape[1], pair):
        start = (level_of * CHUNK) - at
        pick = ((lane >= start) & (lane < start + CHUNK)).astype(F32).astype(BF16)
        wide_ref[:, at : at + pair] = dot(codes, pick).astype(BF16)
    turned_copy.wait()
    tile = min(width, 256)

    def step(at, token):
        lanes = pl.ds(pl.multiple_of(at * tile, tile), tile)
        held = {}
        for chunk in range(chunks):
            factor = rows_ref[chunk * 8 : (chunk + 1) * 8, lanes]
            for level in sorted(held):
                start = run_place(chunk, level) * STATES
                runs_ref[start : start + STATES, lanes] = (held[level] * factor[2:3]).astype(BF16)
            if chunk == chunks - 1:
                break
            span = slice(chunk * CHUNK, (chunk + 1) * CHUNK)
            joined = dot(turned[:, span], scaled_ref[span, lanes]) * factor[0:1]
            held = {level: state * factor[1:2] for level, state in held.items()}
            level = 0
            while level in held:
                joined = joined + held.pop(level)
                level += 1
            held[level] = joined
        return token

    lax.fori_loop(0, width // tile, step, 0)
    for copy in copies:
        copy.wait()


def codes_and_runs(turned_far, c_far, codes_turned, hidden, scaled, factor_rows):
    row_count, width = scaled.shape
    levels = codes_turned.shape[0]
    levels += levels % 2
    chunks = row_count // CHUNK
    local_levels = chunks.bit_length() - 1
    return pl.pallas_call(
        functools.partial(runs_kernel, local_levels),
        in_specs=[HBM] * 2 + [VMEM] * 4,
        out_specs=[VMEM] * 4 + [HBM],
        out_shape=[
            shaped((row_count, levels * CHUNK), BF16),
            shaped((max(1, run_place(chunks)) * STATES, width), BF16),
            shaped(turned_far.shape, BF16),
            shaped(c_far.shape, BF16),
            far_shaped(hidden.shape, BF16),
        ],
        scratch_shapes=[pltpu.SemaphoreType.DMA((chunks + 2,))],
        compiler_params=params(),
        cost_estimate=cost(10**9, 10**7),
        name="codes_and_runs",
    )(*far_off(turned_far, c_far), *near_by(codes_turned, hidden, scaled, factor_rows))


def weights_kernel(
    local_levels,
    cross_levels,
    scale_ref,
    turned,
    c_buf,
    c_other_ref,
    codes_ref,
    left_ref,
    early_reads_ref,
    last_reads_ref,
):
    row_count = c_other_ref.shape[0]

    query_row = lax.broadcasted_iota(jnp.int32, (CHUNK, CHUNK), 0)
    key_lane = lax.broadcasted_iota(jnp.int32, (CHUNK, CHUNK), 1)
    differ = jnp.bitwise_xor(query_row, key_lane)
    inner_levels = CHUNK.bit_length() - 1

    def step(chunk, token):
        rows = chunk_rows(chunk)

        def lam_of(level):
            return codes_ref[rows, level * CHUNK : (level + 1) * CHUNK].astype(F32) * scale_ref[0:1, level : level + 1]

        c_wide = (c_buf[rows, :].astype(F32) + c_other_ref[rows, :].astype(F32)).astype(BF16).astype(F32)
        gram = dot(c_wide.astype(BF16), turned[:, rows])
        weight = lam_of(0)
        for level in range(1, inner_levels + 1):
            weight = jnp.where(differ >= 1 << (level - 1), lam_of(level), weight)
        left_ref[rows, :CHUNK] = jnp.where(key_lane <= query_row, gram * weight, 0.0).astype(BF16)
        for level in range(local_levels + cross_levels):
            read = (c_wide * lam_of(inner_levels + 1 + level)).astype(BF16)
            if level < local_levels:
                left_ref[rows, (level + 1) * CHUNK : (level + 2) * CHUNK] = read
            elif level < local_levels + cross_levels - 1:
                at = (level - local_levels) * STATES
                early_reads_ref[rows, at : at + STATES] = read
            else:
                last_reads_ref[rows, :] = read
        return token

    lax.fori_loop(0, row_count // CHUNK, step, 0)


def level_products(scale, b_turned, c_own, c_other, codes_wide, cross_levels):
    row_count = c_other.shape[0]
    local_levels = (row_count // CHUNK).bit_length() - 1
    return pl.pallas_call(
        functools.partial(weights_kernel, local_levels, cross_levels),
        in_specs=[VMEM] * 5,
        out_specs=[VMEM] * 3,
        out_shape=[
            shaped((row_count, (1 + local_levels) * STATES), BF16),
            shaped((row_count, (cross_levels - 1) * STATES), BF16),
            shaped((row_count, STATES), BF16),
        ],
        compiler_params=params(),
        cost_estimate=cost(10**9, 10**7),
        name="level_products",
    )(*near_by(scale, b_turned, c_own, c_other, codes_wide))


def carried_state(message, before, upper):
    return (message[:STATES].astype(F32) * (before * upper.astype(F32))).astype(BF16)


def local_kernel(
    local_levels,
    cross_levels,
    hidden_far_ref,
    left_ref,
    early_reads_ref,
    scaled_ref,
    fall_ref,
    carry_ref,
    runs_ref,
    near_ref,
    *refs,
):
    received = refs[: cross_levels - 2]
    swapped = refs[cross_levels - 2 : 2 * (cross_levels - 2)]
    local_ref, hidden_ref, before_ref, carried, crossed, sems = refs[2 * (cross_levels - 2) :]
    row_count, width = scaled_ref.shape
    chunks = row_count // CHUNK
    copies = [
        pltpu.make_async_copy(
            hidden_far_ref.at[chunk_rows(chunk)], hidden_ref.at[chunk_rows(chunk)], sems.at[chunk]
        )
        for chunk in range(chunks)
    ]
    for copy in copies:
        copy.start()

    is_low = half_index() == 0
    before = jnp.ones((1, width), F32)
    for level in range(cross_levels - 1):
        upper = shard_bit(level)
        if level == 0:
            message = near_ref[...]
        else:
            own, other = received[level - 1][...], swapped[level - 1][...]
            message = jnp.concatenate(
                [jnp.where(is_low, own, other), jnp.where(is_low, other, own)], axis=1
            )
        carried[level * STATES : (level + 1) * STATES, :] = carried_state(message, before, upper)
        before = jnp.where(upper == 1, before * fade_of(message), before)
    before_ref[...] = jnp.broadcast_to(before, before_ref.shape)
    tiles = lane_tiles(width)
    for lanes in tiles:
        crossed[:, lanes] = dot(early_reads_ref[...], carried[:, lanes]) * carry_ref[:, lanes].astype(F32)

    for chunk in range(chunks):
        rows = slice(chunk * CHUNK, (chunk + 1) * CHUNK)
        levels = [level for level in range(local_levels) if chunk >> level & 1]
        left = [left_ref[rows, :CHUNK]]
        left += [left_ref[rows, (level + 1) * CHUNK : (level + 2) * CHUNK] for level in levels]
        left = jnp.concatenate(left, axis=1)
        runs = slice(run_place(chunk) * STATES, run_place(chunk + 1) * STATES)
        for lanes in tiles:
            right = scaled_ref[rows, lanes]
            if levels:
                right = jnp.concatenate([right, runs_ref[runs, lanes]], axis=0)
            local_ref[rows, lanes] = (
                dot(left, right) * fall_ref[rows, lanes].astype(F32) + crossed[rows, lanes]
            ).astype(BF16)
    for copy in copies:
        copy.wait()


def local_terms(hidden_far, left, early_reads, scaled, fall, carry, runs, near, received, swapped):
    row_count, width = scaled.shape
    local_levels = (row_count // CHUNK).bit_length() - 1
    cross_levels = 2 + len(received)
    return pl.pallas_call(
        functools.partial(local_kernel, local_levels, cross_levels),
        in_specs=[HBM] + [VMEM] * (7 + 2 * len(received)),
        out_specs=[VMEM] * 3,
        out_shape=[shaped((row_count, width), BF16)] * 2 + [shaped((8, width), F32)],
        scratch_shapes=[
            pltpu.VMEM(((cross_levels - 1) * STATES, width), BF16),
            pltpu.VMEM((row_count, width), F32),
            pltpu.SemaphoreType.DMA((row_count // CHUNK,)),
        ],
        compiler_params=params(),
        cost_estimate=cost(3 * 10**9, 10**7),
        name="local_terms",
    )(
        *far_off(hidden_far),
        *near_by(left, early_reads, scaled, fall, carry, runs, near, *received, *swapped),
    )


def finish_kernel(
    swap, cross_levels, message_ref, before_ref, hidden_ref, reads_ref, local_ref, carry_ref, gain_ref, *refs
):
    row_count, width = local_ref.shape
    half_width = width // 2
    own_start = half_index() * half_width
    start = half_width - own_start if swap else own_start
    upper = shard_bit(cross_levels - 1)
    tile = min(half_width, 256)
    row = lax.broadcasted_iota(jnp.int32, (tile, tile), 0) // HEAD_VALUES
    lane = lax.broadcasted_iota(jnp.int32, (tile, tile), 1) // HEAD_VALUES
    mean_mat = jnp.where(row == lane, 1.0 / HEAD_VALUES, 0.0).astype(BF16)
    copies = []
    if swap:
        held_ref, out_ref, result, sems = refs
    else:
        (result,) = refs

    def copy_out(source, here, lanes, at):
        for piece in range(OUT_PIECES):
            rows = pl.ds(piece * (row_count // OUT_PIECES), row_count // OUT_PIECES)
            copies.append(
                pltpu.make_async_copy(source.at[rows, here], out_ref.at[rows, lanes], sems.at[at, piece])
            )
            copies[-1].start()

    if swap:
        lanes = pl.ds(pl.multiple_of(own_start, half_width), half_width)
        copy_out(held_ref, pl.ds(0, half_width), lanes, 0)
    for at in range(half_width // tile):
        lanes = pl.ds(pl.multiple_of(start + at * tile, tile), tile)
        here = slice(at * tile, (at + 1) * tile)
        carried = carried_state(message_ref[:, here], before_ref[0:1, lanes], upper)
        cross = dot(reads_ref[...], carried).astype(BF16)
        mixed = local_ref[:, lanes] + cross * carry_ref[:, lanes]
        mean = dot(mixed * mixed, mean_mat)
        normed = mixed * lax.rsqrt(mean + 1e-05).astype(BF16) * gain_ref[:, lanes].astype(BF16)
        result[:, here] = hidden_ref[:, lanes] + normed
        if swap:
            copy_out(result, here, lanes, 1 + at)
    for copy in copies:
        copy.wait()


def finish(cross_levels, message, before, hidden, reads, local, carry, gain, held):
    row_count, width = local.shape
    half_width = width // 2
    swap = held is not None
    half_shape = (row_count, half_width)
    return pl.pallas_call(
        functools.partial(finish_kernel, swap, cross_levels),
        in_specs=[VMEM] * (8 if swap else 7),
        out_specs=HBM if swap else VMEM,
        out_shape=far_shaped((row_count, width), BF16) if swap else shaped(half_shape, BF16),
        scratch_shapes=[
            pltpu.VMEM(half_shape, BF16),
            pltpu.SemaphoreType.DMA((1 + max(1, half_width // 256), OUT_PIECES)),
        ]
        if swap
        else [],
        compiler_params=params(),
        cost_estimate=cost(2 * 10**9, 8 * 10**6),
        name="carried_and_norm",
    )(*near_by(message, before, hidden, reads, local, carry, gain, *([held] if swap else [])))


def from_behind(x, axis, by):
    length = lax.axis_size(axis)
    return lax.ppermute(x, axis, [(i, i + by) for i in range(length - by)])


def partner(x, axis, distance):
    return lax.ppermute(x, axis, [(i, i ^ 1 << distance) for i in range(lax.axis_size(axis))])


def mirrored(x):
    length = lax.axis_size("seq")
    return lax.ppermute(x, "seq", [(i, length - 1 - i) for i in range(length)])


def summed_over_heads(share):
    rounds = lax.axis_size("head").bit_length() - 1
    if rounds == 0:
        return share, jnp.zeros_like(share)
    total = share
    for distance in range(rounds - 1):
        total = (total.astype(F32) + partner(total, "head", distance).astype(F32)).astype(BF16)
    return total, partner(total, "head", rounds - 1)


def body(
    residual_in,
    query_rows,
    key_rows,
    value_rows,
    bc_weight,
    decay_rate,
    level_codes,
    level_scale,
    positions,
    ssm_gain,
):
    row_count, width = residual_in.shape
    half_width = width // 2
    shard_axes = ("seq", "fsdp")
    cross_levels = lax.axis_size(shard_axes).bit_length() - 1

    weights = (bc_weight, partner(bc_weight, "fsdp", 0))
    split = max(1, row_count // CHUNK // 4)
    edges = from_behind(edge_rows(key_rows, value_rows), shard_axes, 1)
    pos_rows = positions.reshape(row_count // CHUNK, CHUNK)
    rate_turned = decay_rate.T
    hidden, c_mat, weight, b_late, *parts = attend_late(
        split, pos_rows, query_rows, key_rows, value_rows, residual_in, weights
    )
    late_own, late_other = summed_over_heads(b_late)
    hidden, c_mat, b_early = attend_early(split, pos_rows, edges, parts, weight, hidden, c_mat)
    early_own, early_other = summed_over_heads(b_early)
    scaled, factor_rows, fall, carry, c_far = scale_hidden(rate_turned, hidden, c_mat)
    c_mat, scaled = lax.optimization_barrier((c_mat, scaled))
    c_sent, c_other = summed_over_heads(c_mat)
    if lax.axis_size("head") > 2:
        c_far = c_sent
    state, turned_far = block_state(
        early_own, early_other, late_own, late_other, scaled, factor_rows
    )
    near = partner(state, "fsdp", 0)
    joined = join(0, state, near, half_width, cross_levels == 2)
    received, swapped = [], []
    for level in range(1, cross_levels):
        other = mirrored(joined) if level == cross_levels - 1 else partner(joined, "seq", level - 1)
        if level == 1:
            codes_wide, runs, b_turned, c_own, hidden_far = codes_and_runs(
                turned_far, c_far, level_codes.T, hidden, scaled, factor_rows
            )
            other, codes_wide = lax.optimization_barrier((other, codes_wide))
        received.append(other)
        if level < cross_levels - 1:
            joined = join(level, joined, other, half_width, level == cross_levels - 2)
            swapped.append(partner(other, "fsdp", 0))
    left, early_reads, last_reads = level_products(
        level_scale[None, :], b_turned, c_own, c_other, codes_wide, cross_levels
    )
    local, hidden, before = local_terms(
        hidden_far, left, early_reads, scaled, fall, carry, runs, near, received[:-1], swapped
    )
    last, local = lax.optimization_barrier((received[-1], local))
    last_swapped = partner(last, "fsdp", 0)
    gain = ssm_gain[None, :]
    half = finish(cross_levels, last, before, hidden, last_reads, local, carry, gain, None)
    return finish(cross_levels, last_swapped, before, hidden, last_reads, local, carry, gain, half)


def solution(mesh):
    in_specs = (
        P(("groups", "seq", "fsdp"), "head"),
        P(("groups", "seq", "fsdp"), "head"),
        P(("groups", "seq", "fsdp"), "head"),
        P(("groups", "seq", "fsdp"), "head"),
        P(("head", "fsdp"), None),
        P(("groups", "seq", "fsdp"), "head"),
        P(("groups", "seq", "fsdp"), None),
        P(),
        P(("groups", "seq", "fsdp")),
        P("head"),
    )
    out_specs = P(("groups", "seq", "fsdp"), "head")
    return jax.shard_map(body, mesh=mesh, in_specs=in_specs, out_specs=out_specs, check_vma=False)
```

```python
import functools
import math

import jax
import jax.numpy as jnp
from jax import lax
from jax.experimental import pallas as pl
from jax.experimental.pallas import tpu as pltpu
from jax.sharding import PartitionSpec as P

HEAD_DIM = 128
HEAD_VALUES = 64
STATES = 128
WINDOW = 128
CHUNK = 128
EXTRA = 16
OUT_PIECES = 4
VMEM_LIMIT = 24 * 1024 * 1024
HIDDEN = -1e30

F32 = jnp.float32
BF16 = jnp.bfloat16
VMEM = pl.BlockSpec(memory_space=pltpu.VMEM)
SMEM = pl.BlockSpec(memory_space=pltpu.SMEM)
HBM = pl.BlockSpec(memory_space=pltpu.HBM)


def params():
    return pltpu.CompilerParams(vmem_limit_bytes=VMEM_LIMIT)


def cost(flops, moved, transcendentals=0):
    return pl.CostEstimate(flops=flops, bytes_accessed=moved, transcendentals=transcendentals)


def shaped(shape, dtype):
    return pltpu.VMEM(shape, dtype)


def far_shaped(shape, dtype):
    return pltpu.HBM(shape, dtype)


def near_by(*arrays):
    return [pltpu.with_memory_space_constraint(x, pltpu.VMEM) for x in arrays]


def far_off(*arrays):
    return [pltpu.with_memory_space_constraint(x, pltpu.HBM) for x in arrays]


def dot(left, right):
    return jnp.dot(left, right, preferred_element_type=F32)


def dot_turned(left, right):
    return lax.dot_general(left, right, (((1,), (1,)), ((), ())), preferred_element_type=F32)


def chunk_rows(index, count=1):
    return pl.ds(pl.multiple_of(index * CHUNK, CHUNK), count * CHUNK)


def spread_matrix(heads, width):
    lane = lax.broadcasted_iota(jnp.int32, (heads, width), 1)
    start = lax.broadcasted_iota(jnp.int32, (heads, width), 0) * HEAD_VALUES
    return ((lane >= start) & (lane < start + HEAD_VALUES)).astype(F32).astype(BF16)


def lane_tiles(width):
    tile = min(width, 256)
    return [slice(at, at + tile) for at in range(0, width, tile)]


def split_rows(rows):
    high = rows.astype(BF16)
    return high, (rows - high.astype(F32)).astype(BF16)


def half_index():
    return lax.axis_index("fsdp")


def shard_bit(level):
    shard = lax.axis_index("seq") * lax.axis_size("fsdp") + lax.axis_index("fsdp")
    return jnp.bitwise_and(jnp.right_shift(shard, level), 1)


def edge_kernel(key_ref, value_ref, edge_ref, sems):
    row_count = key_ref.shape[0]
    part = WINDOW // 4
    copies = [
        pltpu.make_async_copy(
            ref.at[pl.ds(row_count - WINDOW + piece * part, part)],
            edge_ref.at[pl.ds(at * WINDOW + piece * part, part)],
            sems.at[at, piece],
        )
        for at, ref in enumerate((key_ref, value_ref))
        for piece in range(4)
    ]
    for copy in copies:
        copy.start()
    for copy in copies:
        copy.wait()


def edge_rows(key_rows, value_rows):
    width = key_rows.shape[1]
    return pl.pallas_call(
        edge_kernel,
        in_specs=[HBM] * 2,
        out_specs=VMEM,
        out_shape=shaped((2 * WINDOW, width), BF16),
        scratch_shapes=[pltpu.SemaphoreType.DMA((2, 4))],
        compiler_params=params(),
        cost_estimate=cost(0, 2**20),
        name="edge_rows",
    )(*far_off(key_rows, value_rows))


def lower_ones():
    row = lax.broadcasted_iota(jnp.int32, (CHUNK, CHUNK), 0)
    lane = lax.broadcasted_iota(jnp.int32, (CHUNK, CHUNK), 1)
    lower = (lane <= row).astype(F32).astype(BF16)
    return jnp.concatenate([lower] * 3, axis=1)


def chunk_sums(lower, rate):
    first = rate.astype(BF16)
    second, third = split_rows(rate - first.astype(F32))
    return dot_turned(lower, jnp.concatenate([first, second, third], axis=1))


def fade_wide(rate_ref, fall, carry, fall_ref, carry_ref):
    heads, row_count = rate_ref.shape
    width = fall_ref.shape[1]
    lower = lower_ones()
    spread = spread_matrix(heads, width)
    prefix = jnp.zeros((1, heads), F32)
    for at in range(0, row_count, CHUNK):
        rows = slice(at, at + CHUNK)
        total = chunk_sums(lower, rate_ref[:, rows])
        fall[rows, :] = jnp.exp(total[CHUNK // 2 - 1 : CHUNK // 2] - total).astype(BF16)
        carry[rows, :] = jnp.exp(-(total + prefix)).astype(BF16)
        prefix = prefix + total[CHUNK - 1 :]
    for lanes in lane_tiles(width):
        fall_ref[:, lanes] = dot(fall[...], spread[:, lanes]).astype(BF16)
        carry_ref[:, lanes] = dot(carry[...], spread[:, lanes]).astype(BF16)


def chunk_masks(doc_pos):
    key_row = lax.broadcasted_iota(jnp.int32, (WINDOW, WINDOW), 0)
    query_lane = lax.broadcasted_iota(jnp.int32, (WINDOW, WINDOW), 1)
    away = query_lane - key_row
    away = jnp.where(away < 0, away + WINDOW, away)
    bias = jnp.where(away <= doc_pos, 0.0, HIDDEN).astype(F32).T
    return bias


def attend_chunk(bias, query, key_before, key, value_before, value, residual):
    query_row = lax.broadcasted_iota(jnp.int32, (WINDOW, WINDOW), 0)
    key_lane = lax.broadcasted_iota(jnp.int32, (WINDOW, WINDOW), 1)
    current = key_lane <= query_row
    current_share = current.astype(F32).astype(BF16)
    before_share = (1.0 - current.astype(F32)).astype(BF16)
    ones = jnp.ones((2 * WINDOW, HEAD_DIM), BF16)
    factor = math.log2(math.e) / math.sqrt(HEAD_DIM)
    scores = dot_turned(query, jnp.concatenate([key_before, key], axis=0))
    merged = jnp.where(current, scores[:, WINDOW:], scores[:, :WINDOW]) + bias
    top = jnp.max(merged, axis=1, keepdims=True)
    weights = jnp.exp2((merged - top) * factor).astype(BF16)
    weights = jnp.concatenate([weights * before_share, weights * current_share], axis=1)
    values = jnp.concatenate([value_before, value], axis=0)
    summed = dot(weights, jnp.concatenate([values, ones], axis=1))
    attended = summed[:, :HEAD_DIM] / summed[:, HEAD_DIM:]
    return (residual.astype(F32) + attended).astype(BF16)


def attend_heads(bias, width, query, key_before, key, value_before, value, residual, hidden):
    def lanes_of(at, ref, rows):
        return ref[rows, at : at + HEAD_DIM]

    for at in range(0, width, HEAD_DIM):
        hidden[0][hidden[1], at : at + HEAD_DIM] = attend_chunk(
            bias,
            lanes_of(at, *query),
            lanes_of(at, *key_before),
            lanes_of(at, *key),
            lanes_of(at, *value_before),
            lanes_of(at, *value),
            lanes_of(at, *residual),
        )


def late_kernel(
    split,
    pos_ref,
    query_ref,
    key_ref,
    value_ref,
    residual_ref,
    own_weight_ref,
    other_weight_ref,
    hidden_ref,
    c_ref,
    weight_ref,
    b_ref,
    key_early_ref,
    query_early_ref,
    value_early_ref,
    residual_early_ref,
    key_buf,
    value_buf,
    query_buf,
    residual_buf,
    sems,
):
    row_count, width = query_ref.shape
    chunks = row_count // CHUNK
    half_width = width // 2
    arrays = (
        (key_ref, key_buf, key_early_ref),
        (value_ref, value_buf, value_early_ref),
        (query_ref, query_buf, query_early_ref),
        (residual_ref, residual_buf, residual_early_ref),
    )

    def copy(which, chunk):
        source, buffer, _ = arrays[which]
        return pltpu.make_async_copy(
            source.at[chunk_rows(chunk)], buffer.at[chunk_rows(chunk - split)], sems.at[which, chunk - split]
        )

    def copy_early(which, chunk):
        source, _, early = arrays[which]
        rows = chunk_rows(chunk)
        return pltpu.make_async_copy(source.at[rows], early.at[rows], sems.at[which, chunk + chunks - split])

    for which in range(2):
        copy_early(which, split - 1).start()
    for chunk in range(split, chunks):
        for which in range(4):
            copy(which, chunk).start()
    for which in range(2, 4):
        copy_early(which, split - 1).start()
    for chunk in range(split - 1):
        for which in range(4):
            copy_early(which, chunk).start()
    is_low = half_index() == 0
    own_weight, other_weight = own_weight_ref[...], other_weight_ref[...]
    weight_ref[:half_width, :] = jnp.where(is_low, own_weight, other_weight)
    weight_ref[half_width:, :] = jnp.where(is_low, other_weight, own_weight)

    def attend_one(chunk, key_before, value_before):
        for which in range(4):
            copy(which, chunk).wait()
        rows = chunk_rows(chunk - split)
        attend_heads(
            chunk_masks(pos_ref[pl.ds(chunk, 1), :]),
            width,
            (query_buf, rows),
            key_before,
            (key_buf, rows),
            value_before,
            (value_buf, rows),
            (residual_buf, rows),
            (hidden_ref, chunk_rows(chunk)),
        )

    for which in range(2):
        copy_early(which, split - 1).wait()
    last = chunk_rows(split - 1)
    attend_one(split, (key_early_ref, last), (value_early_ref, last))

    def step(chunk, token):
        before = chunk_rows(chunk - split - 1)
        attend_one(chunk, (key_buf, before), (value_buf, before))
        return token

    lax.fori_loop(split + 1, chunks, step, 0)
    shared = dot(hidden_ref[split * CHUNK :, :], weight_ref[...])
    b_ref[...] = shared[:, :STATES].astype(BF16)
    c_ref[split * CHUNK :, :] = shared[:, STATES:].astype(BF16)
    for which in range(2, 4):
        copy_early(which, split - 1).wait()
    for chunk in range(split - 1):
        for which in range(4):
            copy_early(which, chunk).wait()


def attend_late(split, positions, query, key, value, residual, weights):
    row_count, width = query.shape
    chunks = row_count // CHUNK
    late = row_count - split * CHUNK
    return pl.pallas_call(
        functools.partial(late_kernel, split),
        in_specs=[VMEM] + [HBM] * 4 + [VMEM] * 2,
        out_specs=[VMEM] * 8,
        out_shape=[
            shaped((row_count, width), BF16),
            shaped((row_count, STATES), BF16),
            shaped((width, 2 * STATES), BF16),
            shaped((late, STATES), BF16),
        ]
        + [shaped((split * CHUNK, width), BF16)] * 4,
        scratch_shapes=[pltpu.VMEM((late, width), BF16)] * 4 + [pltpu.SemaphoreType.DMA((4, chunks))],
        compiler_params=params(),
        cost_estimate=cost(6 * 10**9, 10**7),
        name="attention_late",
    )(
        *near_by(positions),
        *far_off(query, key, value, residual),
        *near_by(*weights),
    )


def early_kernel(
    split,
    pos_ref,
    edge_ref,
    key_ref,
    query_ref,
    value_ref,
    residual_ref,
    weight_ref,
    hidden_in_ref,
    c_in_ref,
    hidden_ref,
    c_ref,
    b_ref,
):
    width = query_ref.shape[1]
    early = split * CHUNK

    def attend_one(chunk, key_before, value_before):
        rows = chunk_rows(chunk)
        attend_heads(
            chunk_masks(pos_ref[pl.ds(chunk, 1), :]),
            width,
            (query_ref, rows),
            key_before,
            (key_ref, rows),
            value_before,
            (value_ref, rows),
            (residual_ref, rows),
            (hidden_ref, rows),
        )

    def step(chunk, token):
        rows = chunk_rows(chunk - 1)
        attend_one(chunk, (key_ref, rows), (value_ref, rows))
        return token

    lax.fori_loop(1, split, step, 0)
    attend_one(0, (edge_ref, slice(0, WINDOW)), (edge_ref, slice(WINDOW, 2 * WINDOW)))
    shared = dot(hidden_ref[:early, :], weight_ref[...])
    b_ref[...] = shared[:, :STATES].astype(BF16)
    c_ref[:early, :] = shared[:, STATES:].astype(BF16)


def attend_early(split, positions, edges, parts, weight, hidden, c_mat):
    return pl.pallas_call(
        functools.partial(early_kernel, split),
        in_specs=[VMEM] * 9,
        out_specs=[VMEM] * 3,
        out_shape=[
            shaped(hidden.shape, BF16),
            shaped(c_mat.shape, BF16),
            shaped((split * CHUNK, STATES), BF16),
        ],
        input_output_aliases={7: 0, 8: 1},
        compiler_params=params(),
        cost_estimate=cost(2 * 10**9, 2 * 10**6),
        name="attention_early",
    )(*near_by(positions, edges, *parts, weight, hidden, c_mat))


def scale_kernel(
    rate_ref,
    hidden_ref,
    c_ref,
    scaled_ref,
    rows_ref,
    fall_ref,
    carry_ref,
    c_far_ref,
    rise,
    fall,
    carry,
    logs,
    sems,
):
    heads, row_count = rate_ref.shape
    width = hidden_ref.shape[1]
    chunks = row_count // CHUNK
    copy = pltpu.make_async_copy(c_ref, c_far_ref, sems.at[0])
    copy.start()
    spread = spread_matrix(heads, width)
    lower = lower_ones()
    row_idx = lax.broadcasted_iota(jnp.int32, (8, heads), 0)
    for chunk in range(chunks):
        rows = slice(chunk * CHUNK, (chunk + 1) * CHUNK)
        total = chunk_sums(lower, rate_ref[:, rows])
        middle = total[CHUNK // 2 - 1 : CHUNK // 2]
        last = total[CHUNK - 1 :]
        rise[rows, :] = jnp.exp(total - middle).astype(BF16)
        logs[chunk * 8 : (chunk + 1) * 8, :] = jnp.where(
            row_idx == 0,
            middle - last,
            jnp.where(row_idx == 1, -last, jnp.where(row_idx == 2, -middle, 0.0)),
        )
    high, low = split_rows(jnp.exp(logs[...]))
    for lanes in lane_tiles(width):
        wide = dot(rise[...], spread[:, lanes])
        scaled_ref[:, lanes] = (wide * hidden_ref[:, lanes].astype(F32)).astype(BF16)
        rows_ref[:, lanes] = dot(high, spread[:, lanes]) + dot(low, spread[:, lanes])
    fade_wide(rate_ref, fall, carry, fall_ref, carry_ref)
    copy.wait()


def scale_hidden(rate_turned, hidden, c_mat):
    row_count, width = hidden.shape
    heads = rate_turned.shape[0]
    chunks = row_count // CHUNK
    return pl.pallas_call(
        scale_kernel,
        in_specs=[VMEM] * 3,
        out_specs=[VMEM] * 4 + [HBM],
        out_shape=[
            shaped((row_count, width), BF16),
            shaped((chunks * 8, width), F32),
            shaped((row_count, width), BF16),
            shaped((row_count, width), BF16),
            far_shaped(c_mat.shape, BF16),
        ],
        scratch_shapes=[pltpu.VMEM((row_count, heads), BF16)] * 3
        + [pltpu.VMEM((chunks * 8, heads), F32), pltpu.SemaphoreType.DMA((1,))],
        compiler_params=params(),
        cost_estimate=cost(10**9, 4 * 10**6),
        name="scale_hidden",
    )(*near_by(rate_turned, hidden, c_mat))


def state_kernel(
    early_own_ref,
    early_other_ref,
    late_own_ref,
    late_other_ref,
    scaled_ref,
    rows_ref,
    state_ref,
    turned_far_ref,
    turned,
    sems,
):
    row_count, width = scaled_ref.shape
    chunks = row_count // CHUNK
    early = early_own_ref.shape[0]
    for chunk in range(chunks):
        at = chunk * CHUNK
        if at < early:
            span = slice(at, at + CHUNK)
            own, other = early_own_ref[span, :], early_other_ref[span, :]
        else:
            span = slice(at - early, at - early + CHUNK)
            own, other = late_own_ref[span, :], late_other_ref[span, :]
        turned[:, at : at + CHUNK] = (own.astype(F32) + other.astype(F32)).T.astype(BF16)
    turned_copy = pltpu.make_async_copy(turned, turned_far_ref, sems.at[0])
    turned_copy.start()
    tile = min(width, 256)

    def step(at, carry):
        lanes = pl.ds(pl.multiple_of(at * tile, tile), tile)
        total = fade = None
        for chunk in range(chunks):
            span = slice(chunk * CHUNK, (chunk + 1) * CHUNK)
            factor = rows_ref[chunk * 8 : (chunk + 1) * 8, lanes]
            added = dot(turned[:, span], scaled_ref[span, lanes]) * factor[0:1]
            total = added if total is None else total * factor[1:2] + added
            fade = factor[1:2] if fade is None else fade * factor[1:2]
        state_ref[:STATES, lanes] = total.astype(BF16)
        state_ref[STATES:, lanes] = fade_rows(fade)
        return carry

    lax.fori_loop(0, width // tile, step, 0)
    turned_copy.wait()


def fade_rows(fade):
    high, low = split_rows(fade)
    row = lax.broadcasted_iota(jnp.int32, (EXTRA, fade.shape[1]), 0)
    return jnp.where(row == 0, high.astype(F32), jnp.where(row == 1, low.astype(F32), 0.0)).astype(BF16)


def fade_of(message):
    return message[STATES : STATES + 1].astype(F32) + message[STATES + 1 : STATES + 2].astype(F32)


def block_state(early_own, early_other, late_own, late_other, scaled, factor_rows):
    row_count, width = scaled.shape
    return pl.pallas_call(
        state_kernel,
        in_specs=[VMEM] * 6,
        out_specs=[VMEM, HBM],
        out_shape=[shaped((STATES + EXTRA, width), BF16), far_shaped((STATES, row_count), BF16)],
        scratch_shapes=[pltpu.VMEM((STATES, row_count), BF16), pltpu.SemaphoreType.DMA((1,))],
        compiler_params=params(),
        cost_estimate=cost(3 * 10**8, 4 * 10**6),
        name="block_state",
    )(*near_by(early_own, early_other, late_own, late_other, scaled, factor_rows))


def join_kernel(level, own_ref, other_ref, joined_ref):
    half_width = joined_ref.shape[1]
    own, other = own_ref[...], other_ref[...]
    if own.shape[1] != half_width:
        is_low = half_index() == 0
        own = jnp.where(is_low, own[:, :half_width], own[:, half_width:])
        other = jnp.where(is_low, other[:, :half_width], other[:, half_width:])
    upper = shard_bit(level) == 1
    own_fade, other_fade = fade_of(own), fade_of(other)
    lower, higher = jnp.where(upper, other, own), jnp.where(upper, own, other)
    fade = jnp.where(upper, own_fade, other_fade)
    joined_ref[:STATES, :] = (lower[:STATES].astype(F32) * fade + higher[:STATES].astype(F32)).astype(BF16)
    if joined_ref.shape[0] > STATES:
        joined_ref[STATES:, :] = fade_rows(own_fade * other_fade)


def join(level, own, other, half_width, last):
    return pl.pallas_call(
        functools.partial(join_kernel, level),
        in_specs=[VMEM, VMEM],
        out_specs=VMEM,
        out_shape=shaped((STATES if last else STATES + EXTRA, half_width), BF16),
        compiler_params=params(),
        cost_estimate=cost(10**6, 10**5),
        name="join_runs",
    )(*near_by(own, other))


def run_place(chunk, level=0):
    return sum(bin(at).count("1") for at in range(chunk)) + bin(chunk & ((1 << level) - 1)).count("1")


def runs_kernel(
    local_levels,
    turned_far_ref,
    c_far_ref,
    codes_ref,
    hidden_ref,
    scaled_ref,
    rows_ref,
    wide_ref,
    runs_ref,
    turned,
    c_ref,
    hidden_far_ref,
    sems,
):
    row_count, width = scaled_ref.shape
    chunks = row_count // CHUNK
    turned_copy = pltpu.make_async_copy(turned_far_ref, turned, sems.at[chunks])
    turned_copy.start()
    copies = [pltpu.make_async_copy(c_far_ref, c_ref, sems.at[chunks + 1])]
    copies[0].start()
    for chunk in range(chunks):
        rows = pl.ds(chunk * CHUNK, CHUNK)
        copies.append(pltpu.make_async_copy(hidden_ref.at[rows], hidden_far_ref.at[rows], sems.at[chunk]))
        copies[-1].start()
    codes = codes_ref[...].astype(F32).T.astype(BF16)
    levels = codes.shape[1]
    pair = 2 * CHUNK
    level_of = lax.broadcasted_iota(jnp.int32, (levels, pair), 0)
    lane = lax.broadcasted_iota(jnp.int32, (levels, pair), 1)
    for at in range(0, wide_ref.shape[1], pair):
        start = (level_of * CHUNK) - at
        pick = ((lane >= start) & (lane < start + CHUNK)).astype(F32).astype(BF16)
        wide_ref[:, at : at + pair] = dot(codes, pick).astype(BF16)
    turned_copy.wait()
    tile = min(width, 256)

    def step(at, token):
        lanes = pl.ds(pl.multiple_of(at * tile, tile), tile)
        held = {}
        for chunk in range(chunks):
            factor = rows_ref[chunk * 8 : (chunk + 1) * 8, lanes]
            for level in sorted(held):
                start = run_place(chunk, level) * STATES
                runs_ref[start : start + STATES, lanes] = (held[level] * factor[2:3]).astype(BF16)
            if chunk == chunks - 1:
                break
            span = slice(chunk * CHUNK, (chunk + 1) * CHUNK)
            joined = dot(turned[:, span], scaled_ref[span, lanes]) * factor[0:1]
            held = {level: state * factor[1:2] for level, state in held.items()}
            level = 0
            while level in held:
                joined = joined + held.pop(level)
                level += 1
            held[level] = joined
        return token

    lax.fori_loop(0, width // tile, step, 0)
    for copy in copies:
        copy.wait()


def codes_and_runs(turned_far, c_far, codes_turned, hidden, scaled, factor_rows):
    row_count, width = scaled.shape
    levels = codes_turned.shape[0]
    levels += levels % 2
    chunks = row_count // CHUNK
    local_levels = chunks.bit_length() - 1
    return pl.pallas_call(
        functools.partial(runs_kernel, local_levels),
        in_specs=[HBM] * 2 + [VMEM] * 4,
        out_specs=[VMEM] * 4 + [HBM],
        out_shape=[
            shaped((row_count, levels * CHUNK), BF16),
            shaped((max(1, run_place(chunks)) * STATES, width), BF16),
            shaped(turned_far.shape, BF16),
            shaped(c_far.shape, BF16),
            far_shaped(hidden.shape, BF16),
        ],
        scratch_shapes=[pltpu.SemaphoreType.DMA((chunks + 2,))],
        compiler_params=params(),
        cost_estimate=cost(10**9, 10**7),
        name="codes_and_runs",
    )(*far_off(turned_far, c_far), *near_by(codes_turned, hidden, scaled, factor_rows))


def weights_kernel(
    local_levels,
    cross_levels,
    scale_ref,
    turned,
    c_buf,
    c_other_ref,
    codes_ref,
    left_ref,
    early_reads_ref,
    last_reads_ref,
):
    row_count = c_other_ref.shape[0]

    query_row = lax.broadcasted_iota(jnp.int32, (CHUNK, CHUNK), 0)
    key_lane = lax.broadcasted_iota(jnp.int32, (CHUNK, CHUNK), 1)
    differ = jnp.bitwise_xor(query_row, key_lane)
    inner_levels = CHUNK.bit_length() - 1

    def step(chunk, token):
        rows = chunk_rows(chunk)

        def lam_of(level):
            return codes_ref[rows, level * CHUNK : (level + 1) * CHUNK].astype(F32) * scale_ref[0:1, level : level + 1]

        c_wide = (c_buf[rows, :].astype(F32) + c_other_ref[rows, :].astype(F32)).astype(BF16).astype(F32)
        gram = dot(c_wide.astype(BF16), turned[:, rows])
        weight = lam_of(0)
        for level in range(1, inner_levels + 1):
            weight = jnp.where(differ >= 1 << (level - 1), lam_of(level), weight)
        left_ref[rows, :CHUNK] = jnp.where(key_lane <= query_row, gram * weight, 0.0).astype(BF16)
        for level in range(local_levels + cross_levels):
            read = (c_wide * lam_of(inner_levels + 1 + level)).astype(BF16)
            if level < local_levels:
                left_ref[rows, (level + 1) * CHUNK : (level + 2) * CHUNK] = read
            elif level < local_levels + cross_levels - 1:
                at = (level - local_levels) * STATES
                early_reads_ref[rows, at : at + STATES] = read
            else:
                last_reads_ref[rows, :] = read
        return token

    lax.fori_loop(0, row_count // CHUNK, step, 0)


def level_products(scale, b_turned, c_own, c_other, codes_wide, cross_levels):
    row_count = c_other.shape[0]
    local_levels = (row_count // CHUNK).bit_length() - 1
    return pl.pallas_call(
        functools.partial(weights_kernel, local_levels, cross_levels),
        in_specs=[VMEM] * 5,
        out_specs=[VMEM] * 3,
        out_shape=[
            shaped((row_count, (1 + local_levels) * STATES), BF16),
            shaped((row_count, (cross_levels - 1) * STATES), BF16),
            shaped((row_count, STATES), BF16),
        ],
        compiler_params=params(),
        cost_estimate=cost(10**9, 10**7),
        name="level_products",
    )(*near_by(scale, b_turned, c_own, c_other, codes_wide))


def carried_state(message, before, upper):
    return (message[:STATES].astype(F32) * (before * upper.astype(F32))).astype(BF16)


def local_kernel(
    local_levels,
    cross_levels,
    hidden_far_ref,
    left_ref,
    early_reads_ref,
    scaled_ref,
    fall_ref,
    carry_ref,
    runs_ref,
    near_ref,
    *refs,
):
    received = refs[: cross_levels - 2]
    swapped = refs[cross_levels - 2 : 2 * (cross_levels - 2)]
    local_ref, hidden_ref, before_ref, carried, crossed, sems = refs[2 * (cross_levels - 2) :]
    row_count, width = scaled_ref.shape
    chunks = row_count // CHUNK
    copies = [
        pltpu.make_async_copy(
            hidden_far_ref.at[chunk_rows(chunk)], hidden_ref.at[chunk_rows(chunk)], sems.at[chunk]
        )
        for chunk in range(chunks)
    ]
    for copy in copies:
        copy.start()

    is_low = half_index() == 0
    before = jnp.ones((1, width), F32)
    for level in range(cross_levels - 1):
        upper = shard_bit(level)
        if level == 0:
            message = near_ref[...]
        else:
            own, other = received[level - 1][...], swapped[level - 1][...]
            message = jnp.concatenate(
                [jnp.where(is_low, own, other), jnp.where(is_low, other, own)], axis=1
            )
        carried[level * STATES : (level + 1) * STATES, :] = carried_state(message, before, upper)
        before = jnp.where(upper == 1, before * fade_of(message), before)
    before_ref[...] = jnp.broadcast_to(before, before_ref.shape)
    tiles = lane_tiles(width)
    for lanes in tiles:
        crossed[:, lanes] = dot(early_reads_ref[...], carried[:, lanes]).astype(BF16) * carry_ref[:, lanes]

    for chunk in range(chunks):
        rows = slice(chunk * CHUNK, (chunk + 1) * CHUNK)
        levels = [level for level in range(local_levels) if chunk >> level & 1]
        left = [left_ref[rows, :CHUNK]]
        left += [left_ref[rows, (level + 1) * CHUNK : (level + 2) * CHUNK] for level in levels]
        left = jnp.concatenate(left, axis=1)
        runs = slice(run_place(chunk) * STATES, run_place(chunk + 1) * STATES)
        for lanes in tiles:
            right = scaled_ref[rows, lanes]
            if levels:
                right = jnp.concatenate([right, runs_ref[runs, lanes]], axis=0)
            local_ref[rows, lanes] = (
                dot(left, right) * fall_ref[rows, lanes].astype(F32) + crossed[rows, lanes].astype(F32)
            ).astype(BF16)
    for copy in copies:
        copy.wait()


def local_terms(hidden_far, left, early_reads, scaled, fall, carry, runs, near, received, swapped):
    row_count, width = scaled.shape
    local_levels = (row_count // CHUNK).bit_length() - 1
    cross_levels = 2 + len(received)
    return pl.pallas_call(
        functools.partial(local_kernel, local_levels, cross_levels),
        in_specs=[HBM] + [VMEM] * (7 + 2 * len(received)),
        out_specs=[VMEM] * 3,
        out_shape=[shaped((row_count, width), BF16)] * 2 + [shaped((8, width), F32)],
        scratch_shapes=[
            pltpu.VMEM(((cross_levels - 1) * STATES, width), BF16),
            pltpu.VMEM((row_count, width), BF16),
            pltpu.SemaphoreType.DMA((row_count // CHUNK,)),
        ],
        compiler_params=params(),
        cost_estimate=cost(3 * 10**9, 10**7),
        name="local_terms",
    )(
        *far_off(hidden_far),
        *near_by(left, early_reads, scaled, fall, carry, runs, near, *received, *swapped),
    )


def finish_kernel(
    swap, cross_levels, message_ref, before_ref, hidden_ref, reads_ref, local_ref, carry_ref, gain_ref, *refs
):
    row_count, width = local_ref.shape
    half_width = width // 2
    own_start = half_index() * half_width
    start = half_width - own_start if swap else own_start
    upper = shard_bit(cross_levels - 1)
    tile = min(half_width, 256)
    row = lax.broadcasted_iota(jnp.int32, (tile, tile), 0) // HEAD_VALUES
    lane = lax.broadcasted_iota(jnp.int32, (tile, tile), 1) // HEAD_VALUES
    mean_mat = jnp.where(row == lane, 1.0 / HEAD_VALUES, 0.0).astype(BF16)
    copies = []
    if swap:
        held_ref, out_ref, result, sems = refs
    else:
        (result,) = refs

    def copy_out(source, here, lanes, at):
        for piece in range(OUT_PIECES):
            rows = pl.ds(piece * (row_count // OUT_PIECES), row_count // OUT_PIECES)
            copies.append(
                pltpu.make_async_copy(source.at[rows, here], out_ref.at[rows, lanes], sems.at[at, piece])
            )
            copies[-1].start()

    if swap:
        lanes = pl.ds(pl.multiple_of(own_start, half_width), half_width)
        copy_out(held_ref, pl.ds(0, half_width), lanes, 0)
    for at in range(half_width // tile):
        lanes = pl.ds(pl.multiple_of(start + at * tile, tile), tile)
        here = slice(at * tile, (at + 1) * tile)
        carried = carried_state(message_ref[:, here], before_ref[0:1, lanes], upper)
        blocks = 2 if swap else 1
        for block in range(blocks):
            rows = slice(block * (row_count // blocks), (block + 1) * (row_count // blocks))
            cross = dot(reads_ref[rows, :], carried).astype(BF16)
            mixed = local_ref[rows, lanes] + cross * carry_ref[rows, lanes]
            mean = dot(mixed * mixed, mean_mat)
            normed = mixed * lax.rsqrt(mean + 1e-05).astype(BF16) * gain_ref[:, lanes].astype(BF16)
            result[rows, here] = hidden_ref[rows, lanes] + normed
            if swap:
                span = pl.ds(block * (row_count // blocks), row_count // blocks)
                copies.append(
                    pltpu.make_async_copy(
                        result.at[span, here], out_ref.at[span, lanes], sems.at[1 + at, block]
                    )
                )
                copies[-1].start()
    for copy in copies:
        copy.wait()


def finish(cross_levels, message, before, hidden, reads, local, carry, gain, held):
    row_count, width = local.shape
    half_width = width // 2
    swap = held is not None
    half_shape = (row_count, half_width)
    return pl.pallas_call(
        functools.partial(finish_kernel, swap, cross_levels),
        in_specs=[VMEM] * (8 if swap else 7),
        out_specs=HBM if swap else VMEM,
        out_shape=far_shaped((row_count, width), BF16) if swap else shaped(half_shape, BF16),
        scratch_shapes=[
            pltpu.VMEM(half_shape, BF16),
            pltpu.SemaphoreType.DMA((1 + max(1, half_width // 256), OUT_PIECES)),
        ]
        if swap
        else [],
        compiler_params=params(),
        cost_estimate=cost(2 * 10**9, 8 * 10**6),
        name="carried_and_norm",
    )(*near_by(message, before, hidden, reads, local, carry, gain, *([held] if swap else [])))


def from_behind(x, axis, by):
    length = lax.axis_size(axis)
    return lax.ppermute(x, axis, [(i, i + by) for i in range(length - by)])


def partner(x, axis, distance):
    return lax.ppermute(x, axis, [(i, i ^ 1 << distance) for i in range(lax.axis_size(axis))])


def mirrored(x):
    length = lax.axis_size("seq")
    return lax.ppermute(x, "seq", [(i, length - 1 - i) for i in range(length)])


def summed_over_heads(share):
    rounds = lax.axis_size("head").bit_length() - 1
    if rounds == 0:
        return share, jnp.zeros_like(share)
    total = share
    for distance in range(rounds - 1):
        total = (total.astype(F32) + partner(total, "head", distance).astype(F32)).astype(BF16)
    return total, partner(total, "head", rounds - 1)


def body(
    residual_in,
    query_rows,
    key_rows,
    value_rows,
    bc_weight,
    decay_rate,
    level_codes,
    level_scale,
    positions,
    ssm_gain,
):
    row_count, width = residual_in.shape
    half_width = width // 2
    shard_axes = ("seq", "fsdp")
    cross_levels = lax.axis_size(shard_axes).bit_length() - 1

    weights = (bc_weight, partner(bc_weight, "fsdp", 0))
    split = max(1, row_count // CHUNK // 4)
    edges = from_behind(edge_rows(key_rows, value_rows), shard_axes, 1)
    pos_rows = positions.reshape(row_count // CHUNK, CHUNK)
    rate_turned = decay_rate.T
    hidden, c_mat, weight, b_late, *parts = attend_late(
        split, pos_rows, query_rows, key_rows, value_rows, residual_in, weights
    )
    late_own, late_other = summed_over_heads(b_late)
    hidden, c_mat, b_early = attend_early(split, pos_rows, edges, parts, weight, hidden, c_mat)
    early_own, early_other = summed_over_heads(b_early)
    scaled, factor_rows, fall, carry, c_far = scale_hidden(rate_turned, hidden, c_mat)
    c_mat, scaled = lax.optimization_barrier((c_mat, scaled))
    c_sent, c_other = summed_over_heads(c_mat)
    if lax.axis_size("head") > 2:
        c_far = c_sent
    state, turned_far = block_state(
        early_own, early_other, late_own, late_other, scaled, factor_rows
    )
    near = partner(state, "fsdp", 0)
    joined = join(0, state, near, half_width, cross_levels == 2)
    received, swapped = [], []
    for level in range(1, cross_levels):
        other = mirrored(joined) if level == cross_levels - 1 else partner(joined, "seq", level - 1)
        if level == 1:
            codes_wide, runs, b_turned, c_own, hidden_far = codes_and_runs(
                turned_far, c_far, level_codes.T, hidden, scaled, factor_rows
            )
            other, codes_wide = lax.optimization_barrier((other, codes_wide))
        received.append(other)
        if level < cross_levels - 1:
            joined = join(level, joined, other, half_width, level == cross_levels - 2)
            swapped.append(partner(other, "fsdp", 0))
    left, early_reads, last_reads = level_products(
        level_scale[None, :], b_turned, c_own, c_other, codes_wide, cross_levels
    )
    local, hidden, before = local_terms(
        hidden_far, left, early_reads, scaled, fall, carry, runs, near, received[:-1], swapped
    )
    last, local = lax.optimization_barrier((received[-1], local))
    last_swapped = partner(last, "fsdp", 0)
    gain = ssm_gain[None, :]
    half = finish(cross_levels, last, before, hidden, last_reads, local, carry, gain, None)
    return finish(cross_levels, last_swapped, before, hidden, last_reads, local, carry, gain, half)


def solution(mesh):
    in_specs = (
        P(("groups", "seq", "fsdp"), "head"),
        P(("groups", "seq", "fsdp"), "head"),
        P(("groups", "seq", "fsdp"), "head"),
        P(("groups", "seq", "fsdp"), "head"),
        P(("head", "fsdp"), None),
        P(("groups", "seq", "fsdp"), "head"),
        P(("groups", "seq", "fsdp"), None),
        P(),
        P(("groups", "seq", "fsdp")),
        P("head"),
    )
    out_specs = P(("groups", "seq", "fsdp"), "head")
    return jax.shard_map(body, mesh=mesh, in_specs=in_specs, out_specs=out_specs, check_vma=False)
```
